256 devices in a mesh: wide: 32 (over x_lo, z, core), narrow: 8 (over y, x_hi).
Axes of the slice: x: 4 (x_hi: 2, x_lo: 2; x = x_hi * 2 + x_lo), y: 4, z: 8, core: 2. Of those that a mesh axis runs over, the one named last changes fastest.
Arguments:
- divergence: float32 [256, 512, 1024], P('wide', None, 'narrow'), may hold values from -6 to 6
- marker_force: float32 [256, 4096], P('wide', 'narrow'), may hold values from -15 to 15
- marker_height: float32 [256, 4096], P('wide', 'narrow'), may hold values from 0 to 8
- marker_cell: int32 [256, 4096], P('wide', 'narrow'), may hold values from 0 to 127
Outputs:
- pressure: float32 [256, 512, 1024], P('wide', None, 'narrow')
The draws below stay inside these ranges and needn't reach their ends.
All inputs are finite; a program needn't handle non-finite values.
Results may differ from the reference program's by a relative error of at most 0.0025.
Values sent between devices are 32-bit elements; how exact they have to be, the bound alone decides.
No kernel may reach another device: no remote copies, remote signals or barrier semaphores. Data moves between devices by JAX's collectives and lax.ppermute only.
A program may use at most 64 MiB of HBM per device.

```python
import math
import jax
import jax.numpy as jnp
from jax import lax

NX = 1024
NY = 512
NZ = 256
MARKS_ROW = 8
XL = 128
MROWS = 256
MCOLS = 4096
N_WIDE = 32
N_NARROW = 8


def place_ends(entries, rng, least, top_value):
    spot = [jax.random.randint(jax.random.fold_in(rng, axis), (), 0, length) for axis, length in enumerate(entries.shape)]
    main_axis = entries.shape.index(max(entries.shape))
    neighbour = spot[:main_axis] + [(spot[main_axis] + 1) % entries.shape[main_axis]] + spot[main_axis + 1:]
    return entries.at[tuple(spot)].set(least).at[tuple(neighbour)].set(top_value)


def block_levels(stream_key, dims, cuts, low, high):
    loudness = 1.0
    for dim, shards_of in cuts:
        draws = jax.random.uniform(jax.random.fold_in(jax.random.fold_in(stream_key, 6), dim), (shards_of,), jnp.float32, low / len(cuts), high / len(cuts))
        loudness = loudness * jnp.repeat(jnp.exp(draws), dims[dim] // shards_of).reshape((-1,) + (1,) * (len(dims) - 1 - dim))
    return loudness


def scatter_about(key, extent, spread, limit, cuts=(), held_as=jnp.bfloat16):
    array = jax.random.normal(key, extent, jnp.float32) * spread
    if len(cuts) > 0:
        array = block_levels(key, extent, cuts, -0.22, 0.18) * array
    return jnp.clip(array, min=-limit, max=limit).astype(held_as)


def setup_inputs(seed: int = 0) -> dict:
    key_of = jax.random.split(jax.random.key(seed), 5)
    return {
        "divergence": scatter_about(key_of[0], (NZ, NY, NX), 1.0, 6.0, ((0, 32), (2, 8)), jnp.float32),
        "marker_force": scatter_about(key_of[1], (MROWS, MCOLS), 3.0, 15.0, ((0, 32), (1, 8)), jnp.float32),
        "marker_height": jnp.clip(8.0 * jax.random.uniform(key_of[2], (MROWS, MCOLS), jnp.float32) ** block_levels(key_of[2], (MROWS, MCOLS), ((0, 32), (1, 8)), -0.2, 0.2), 0.0, 8.0),
        "marker_cell": place_ends(jax.random.randint(key_of[3], (MROWS, MCOLS), 0, XL), jax.random.fold_in(key_of[3], 1), 0, XL - 1).astype(jnp.int32),
    }


def cosine_table(length_n):
    index_k = jnp.arange(length_n, dtype=jnp.int32)[:, None]
    index_n = jnp.arange(length_n, dtype=jnp.int32)[None, :]
    turns = index_k * (2 * index_n + 1) % (4 * length_n)
    radians = turns.astype(jnp.float32) * (math.pi / (2 * length_n))
    scaling = jnp.where(index_k == 0, math.sqrt(1.0 / length_n), math.sqrt(2.0 / length_n))
    return (scaling * jnp.cos(radians)).astype(jnp.float32)

def eigen_values(mode_ids, length_n):
    return 2.0 - 2.0 * jnp.cos(mode_ids.astype(jnp.float32) * (math.pi / length_n))

def thomas_solve(right_side, diag_terms):
    zero_rows = jnp.zeros(diag_terms.shape, jnp.float32)

    def forward(state_pair, row_term):
        upper_coef, partial_value = state_pair
        pivots = diag_terms + upper_coef
        upper_next = -1.0 / pivots
        partial_next = (row_term + partial_value) / pivots
        return ((upper_next, partial_next), (upper_next, partial_next))
    unused, stored = lax.scan(forward, (zero_rows, zero_rows), right_side)

    def backward(later_value, stored_pair):
        solved = stored_pair[1] - stored_pair[0] * later_value
        return (solved, solved)
    unused_last, values = lax.scan(backward, zero_rows, stored, reverse=True)
    return values

def reference(divergence, marker_force, marker_height, marker_cell):
    slab_planes = NZ // N_WIDE
    width_x = NX // N_NARROW
    highest = lax.Precision.HIGHEST
    forces = marker_force.reshape(N_WIDE, MARKS_ROW, N_NARROW, NY)
    heights = marker_height.reshape(N_WIDE, MARKS_ROW, N_NARROW, NY)
    cells = marker_cell.reshape(N_WIDE, MARKS_ROW, N_NARROW, NY)
    centers = jnp.arange(-1, slab_planes + 1, dtype=jnp.float32) + 0.5

    def slab_spread(pieces):
        force_s, height_s, cell_s = pieces
        weights = jnp.maximum(0.0, 1.0 - jnp.abs(centers[:, None, None, None] - height_s[None]))
        weighted = weights * force_s[None]
        onehot = (cell_s[:, :, :, None] == jnp.arange(width_x, dtype=jnp.int32)[None, None, None, :]).astype(jnp.float32)
        planes = jnp.einsum('jmny,mnyx->jynx', weighted, onehot, precision=highest)
        return planes.reshape(slab_planes + 2, NY, NX)
    extended = lax.map(slab_spread, (forces, heights, cells))
    interior = extended[:, 1:-1]
    interior = interior.at[1:, 0].add(extended[:-1, -1])
    interior = interior.at[:-1, -1].add(extended[1:, 0])
    source = divergence + interior.reshape(NZ, NY, NX)
    table_y = cosine_table(NY)
    table_x = cosine_table(NX)
    along_y = jnp.einsum('ky,zyx->zkx', table_y, source, precision=highest)
    modes = jnp.einsum('zkx,jx->zkj', along_y, table_x, precision=highest)
    diag_terms = 2.0 + eigen_values(jnp.arange(NY, dtype=jnp.int32), NY)[:, None] + eigen_values(jnp.arange(NX, dtype=jnp.int32), NX)[None, :]
    coeffs = thomas_solve(modes, diag_terms)
    back_x = jnp.einsum('zkj,jx->zkx', coeffs, table_x, precision=highest)
    return jnp.einsum('ky,zkx->zyx', table_y, back_x, precision=highest)
```

```python
import functools

import jax
import jax.numpy as jnp
import ml_dtypes
import numpy as np
from jax import lax
from jax.experimental import pallas as pl
from jax.experimental.pallas import tpu as pltpu
from jax.sharding import PartitionSpec as P

BOTH = ("wide", "narrow")
NZ, NY, NX = 256, 512, 1024
NW, NN = 32, 8
SLAB = NZ // NW
XL = NX // NN
INNER = SLAB - 1
DEST = NW * NN
HALF = NY // 2
ROWS = 5
GROUP = 32
MARKS = 8
F32, BF16 = jnp.float32, jnp.bfloat16


def dct_matrix(order):
    k = np.arange(order)[:, None]
    n = np.arange(order)[None, :]
    scale = np.where(k == 0, np.sqrt(1.0 / order), np.sqrt(2.0 / order))
    return scale * np.cos(np.pi * ((k * (2 * n + 1)) % (4 * order)) / (2 * order))


def lam(order):
    return 2.0 - 2.0 * np.cos(np.pi * np.arange(order) / order)


def halves(table):
    high = table.astype(np.float32).astype(ml_dtypes.bfloat16)
    low = (table - high.astype(np.float64)).astype(np.float32).astype(ml_dtypes.bfloat16)
    return high, low


@functools.lru_cache(None)
def tables():
    t = {}
    cy, cx, cl = dct_matrix(NY), dct_matrix(NX), dct_matrix(XL)
    i = np.arange(1, SLAB)
    t["S"] = np.sqrt(2.0 / SLAB) * np.sin(np.pi * np.outer(i, i) / SLAB)
    t["mu"] = 2.0 - 2.0 * np.cos(np.pi * i / SLAB)
    ch, clow = halves(cy)
    t["cy3"] = np.concatenate([ch, clow, ch], 1)
    ch, clow = halves(cy.T)
    t["cyt3"] = np.concatenate([ch, clow, ch], 1)
    h, l = halves(cl.T)
    t["clt3"] = np.concatenate([h, h, l], 0)
    h, l = halves(cl)
    t["cl3"] = np.concatenate([h, h, l], 0)
    t["den"] = (
        1.0 / (t["mu"][:, None, None] + lam(NY)[None, :, None] + lam(XL)[None, None, :])
    ).astype(np.float32)
    ends = np.zeros((INNER, XL, 128))
    for m in range(INNER):
        ends[m, :, m] = cl[:, 0]
        ends[m, :, 8 + m] = cl[:, -1]
    t["ends_h"], t["ends_l"] = halves(ends.reshape(INNER * XL, 128))
    order = np.concatenate([np.arange(0, NX, 2), np.arange(1, NX, 2)])
    mixed = np.zeros((NX, NX))
    for n in range(NN):
        mixed[:, n * XL : (n + 1) * XL] = cx[:, n * XL : (n + 1) * XL] @ cl.T
    mixed = mixed[order]
    hw = NX // 2
    fwd = np.stack([mixed[:hw, :hw].T, mixed[hw:, :hw].T])
    t["fwd_h"], t["fwd_l"] = halves(fwd)
    inv = np.stack([mixed[:hw, :hw], mixed[hw:, :hw]])
    t["inv_h"], t["inv_l"] = halves(inv)
    lamx = lam(NX)[order]
    t["lamx_row"] = lamx.reshape(1, NX).astype(np.float32)
    t["lamx_tile"] = np.concatenate([lamx.reshape(8, 128)] * 2, 0).astype(np.float32)
    t["lamy"] = lam(NY).astype(np.float32)
    jumps = np.stack([cx[:, XL * f + XL - 1] - cx[:, XL * f + XL] for f in range(NN - 1)])[:, order]
    into = np.zeros((NN, 2, 8, NX))
    outof = np.zeros((NN, 2, 8, NX))
    for n in range(NN):
        if n < NN - 1:
            into[n, 1] = -jumps[n]
            outof[n, 1] = jumps[n]
        if n > 0:
            into[n, 0] = jumps[n - 1]
            outof[n, 0] = jumps[n - 1]
    t["into_h"], t["into_l"] = halves(into.reshape(128, NX))
    t["outof_h"], t["outof_l"] = halves(outof.reshape(128, NX).T)
    push = np.zeros((128, XL))
    for kk in range(2):
        for m in range(8):
            push[kk * 64 + m] = cl[:, 0]
            push[kk * 64 + 8 + m] = -cl[:, -1]
    h, l = halves(push)
    t["push3"] = np.concatenate([h, h, l], 0)
    sign = np.where(np.arange(XL) % 2 == 0, 1.0, -1.0).reshape(1, XL)
    t["sign"] = sign.astype(np.float32)
    return t


def split(value):
    high = value.astype(BF16)
    return high, (value - high.astype(F32)).astype(BF16)


def dot(left, right):
    return lax.dot_general(left, right, (((1,), (0,)), ((), ())), preferred_element_type=F32)


def dot_nt(left, right):
    return lax.dot_general(left, right, (((1,), (1,)), ((), ())), preferred_element_type=F32)


def triple(value):
    high, low = split(value)
    return jnp.concatenate([high, low, high], axis=1)


def iota(shape, axis):
    return lax.broadcasted_iota(jnp.int32, shape, axis)


def forward_kernel(S, div, marks, cy3, clt3, den, ends_h, ends_l, pay, keep, zh, zl, freq, faces):
    spot = iota((GROUP, 256), 1) % GROUP == iota((GROUP, 256), 0)
    cell_ids = iota((XL, 256), 0).astype(F32)
    centers = iota((SLAB, 256), 0).astype(F32) + 0.5

    def onehot(cells):
        return jnp.where(cells == cell_ids, 1.0, 0.0).astype(BF16)

    def spread_rows(weights):
        high = weights.astype(BF16).astype(F32)
        low = weights - high
        parts = []
        for value in (high, low):
            for j in range(weights.shape[0]):
                parts.append(jnp.where(spot, value[j : j + 1], 0.0).astype(BF16))
        return jnp.concatenate(parts, axis=0)

    def markers(g, carry):
        force, height, cells = marks[g, 0:1, :], marks[g, 1:2, :], marks[g, 2:3, :]
        up_w, up_c, dn_w, dn_c = (marks[g, r : r + 1, :] for r in range(3, 7))
        weights = force * jnp.maximum(0.0, 1.0 - jnp.abs(centers - height))
        own = dot_nt(spread_rows(weights), onehot(cells))
        own = own[: SLAB * GROUP] + own[SLAB * GROUP :]
        up = dot_nt(spread_rows(up_w), onehot(up_c))
        dn = dot_nt(spread_rows(dn_w), onehot(dn_c))
        rows = pl.ds(pl.multiple_of(g * GROUP, GROUP), GROUP)
        planes = []
        for z in range(SLAB):
            value = div[z, rows, :] + own[z * GROUP : (z + 1) * GROUP]
            if z == 0:
                value = value + up[:GROUP] + up[GROUP:]
            if z == SLAB - 1:
                value = value + dn[:GROUP] + dn[GROUP:]
            planes.append(value)
        source = jnp.concatenate(planes, axis=0)
        high, low = split(dot(triple(source), clt3[...]))
        for z in range(SLAB):
            zh[z, rows, :] = high[z * GROUP : (z + 1) * GROUP]
            zl[z, rows, :] = low[z * GROUP : (z + 1) * GROUP]
        return carry

    lax.fori_loop(0, NY // GROUP, markers, 0)

    def along_y(p, carry):
        high = jnp.concatenate([zh[2 * p], zh[2 * p + 1]], axis=1)
        low = jnp.concatenate([zl[2 * p], zl[2 * p + 1]], axis=1)
        right = jnp.concatenate([high, high, low], axis=0)
        for half in range(2):
            rows = slice(half * HALF, (half + 1) * HALF)
            value = dot(cy3[rows, :], right)
            freq[2 * p, rows, :] = value[:, :XL]
            freq[2 * p + 1, rows, :] = value[:, XL:]
        return carry

    lax.fori_loop(0, SLAB // 2, along_y, 0)

    step = 32

    def slab(c, carry):
        rows = pl.ds(pl.multiple_of(c * step, step), step)
        f = [freq[z, rows, :] for z in range(SLAB)]
        even = [f[i] + f[SLAB - i] for i in range(1, 4)] + [f[4]]
        odd = [f[i] - f[SLAB - i] for i in range(1, 4)]
        p_odd = p_even = None
        solved = []
        for m in range(INNER):
            if m % 2 == 0:
                hat = sum(float(S[m, i]) * even[i] for i in range(4))
            else:
                hat = sum(float(S[m, i]) * odd[i] for i in range(3))
            keep[m, rows, :] = hat
            value = hat * den[m, rows, :]
            solved.append(value)
            part = float(S[m, 0]) * value
            if m % 2 == 0:
                p_odd = part if p_odd is None else p_odd + part
            else:
                p_even = part if p_even is None else p_even + part
        zh_rows = f[0] + p_odd + p_even
        freq[0, rows, :] = zh_rows
        freq[1, rows, :] = p_odd - p_even
        high, low = split(jnp.concatenate(solved, axis=1))
        faces[rows, :] = dot(high, ends_h[...]) + dot(low, ends_h[...]) + dot(high, ends_l[...])
        return carry

    lax.fori_loop(0, NY // step, slab, 0)
    for kk in range(2):
        rows = slice(kk * HALF, (kk + 1) * HALF)
        pay[pl.ds(kk, DEST, stride=ROWS), :] = freq[0, rows, :]
        pay[pl.ds(2 + kk, DEST, stride=ROWS), :] = freq[1, rows, :]
    pay[pl.ds(4, DEST, stride=ROWS), :] = faces[:HALF, :] + pltpu.roll(faces[HALF:, :], 64, 1)


def middle_kernel(
    S, mu, dest, lamy, recv, fwd_h, fwd_l, inv_h, inv_l, into_h, into_l, outof_h, outof_l,
    lamx_row, lamx_tile, sign, pay, grid, corr, tops, bots, piv, sol, shift,
):
    lane = iota((NW, 128), 1)
    here = dest[0]
    lam_k = [lamy[here], lamy[HALF + here]]
    skip = NN * ROWS

    def load(n, r):
        return recv[pl.ds(n * ROWS + r, NW, stride=skip), :]

    sums, diffs = [], []
    for n in range(NN // 2):
        near = jnp.concatenate([load(n, r) for r in range(4)], axis=0)
        far = jnp.concatenate([load(NN - 1 - n, r) for r in range(4)], axis=0) * sign[...]
        sums.append(near + far)
        diffs.append(near - far)
    for part, pieces in ((0, sums), (1, diffs)):
        high, low = split(jnp.concatenate(pieces, axis=1))
        both = dot(jnp.concatenate([high, low], axis=0), fwd_h[part])
        value = both[: 4 * NW] + both[4 * NW :] + dot(high, fwd_l[part])
        grid[:, part * 512 : (part + 1) * 512] = value

    packs = []
    for kk in range(2):
        pack = jnp.zeros((NW, 128), F32)
        for n in range(NN):
            turned = load(n, 4)
            shift_by = (16 * n + 64 * kk) % 128
            if shift_by:
                turned = pltpu.roll(turned, shift_by, 1)
            pack = jnp.where(lane // 16 == n, turned, pack)
        packs.append(pack)
    pairs = [(kk, m) for kk in range(2) for m in range(INNER)]
    masked = jnp.concatenate([jnp.where(lane % 8 == m, packs[kk], 0.0) for kk, m in pairs], axis=0)
    mask_h, mask_l = split(masked)
    mask_both = jnp.concatenate([mask_h, mask_l], axis=0)
    count = len(pairs) * NW

    mode_id = iota((8, NX), 0)
    mu_col = jnp.zeros((8, NX), F32)
    for m in range(8):
        mu_col = jnp.where(mode_id == m, float(mu[min(m, INNER - 1)]), mu_col)
    dens = [1.0 / (mu_col + lam_k[kk] + lamx_row[...]) for kk in range(2)]

    for part in range(4):
        cols = slice(part * 256, (part + 1) * 256)
        value = dot(mask_both, into_h[:, cols])
        value = value[:count] + value[count:] + dot(mask_h, into_l[:, cols])
        for kk in range(2):
            p_odd = p_even = None
            for m in range(INNER):
                at = (kk * INNER + m) * NW
                piece = value[at : at + NW] * dens[kk][m : m + 1, cols]
                corr[at : at + NW, cols] = piece
                piece = float(S[m, 0]) * piece
                if m % 2 == 0:
                    p_odd = piece if p_odd is None else p_odd + piece
                else:
                    p_even = piece if p_even is None else p_even + piece
            top = slice(kk * NW, (kk + 1) * NW)
            bot = slice((2 + kk) * NW, (3 + kk) * NW)
            grid[top, cols] = grid[top, cols] + p_odd + p_even
            grid[bot, cols] = grid[bot, cols] + p_odd - p_even

    bots[0:16, :] = jnp.zeros((16, 128), F32)
    for kk in range(2):
        for jb in range(8):
            cols = slice(jb * 128, (jb + 1) * 128)
            tops[pl.ds(kk * 8 + jb, NW, stride=16), :] = grid[kk * NW : (kk + 1) * NW, cols]
            bots[pl.ds(16 + kk * 8 + jb, NW, stride=16), :] = grid[
                (2 + kk) * NW : (3 + kk) * NW, cols
            ]

    row16 = iota((16, 128), 0)
    diag = 2.0 + jnp.where(row16 < 8, lam_k[0], lam_k[1]) + lamx_tile[...]
    older, newer = jnp.ones((16, 128), F32), diag
    for _ in range(INNER - 2):
        older, newer = newer, diag * newer - older
    last = diag * newer - older
    near_one = newer / last
    far_one = 1.0 / last
    full = diag - 2.0 * near_one
    inverse = 1.0 / (diag - near_one)
    value = tops[0:16, :]
    piv[0:16, :] = inverse
    sol[0:16, :] = value
    for w in range(1, NW):
        at = slice(w * 16, (w + 1) * 16)
        ratio = far_one * inverse
        value = tops[at, :] + bots[at, :] + ratio * value
        inverse = 1.0 / (full - far_one * ratio)
        piv[at, :] = inverse
        sol[at, :] = value
    later = jnp.zeros((16, 128), F32)
    sol[NW * 16 : (NW + 1) * 16, :] = later
    for w in range(NW - 1, -1, -1):
        at = slice(w * 16, (w + 1) * 16)
        later = (sol[at, :] + far_one * later) * piv[at, :]
        sol[at, :] = later

    for kk in range(2):
        for jb in range(8):
            cols = slice(jb * 128, (jb + 1) * 128)
            grid[kk * NW : (kk + 1) * NW, cols] = sol[pl.ds(kk * 8 + jb, NW, stride=16), :]
            grid[(2 + kk) * NW : (3 + kk) * NW, cols] = sol[
                pl.ds(16 + kk * 8 + jb, NW, stride=16), :
            ]

    flux = jnp.zeros((count, 128), F32)
    for part in range(4):
        cols = slice(part * 256, (part + 1) * 256)
        pieces = []
        for kk in range(2):
            low_s = grid[kk * NW : (kk + 1) * NW, cols]
            high_s = grid[(2 + kk) * NW : (3 + kk) * NW, cols]
            plus, minus = low_s + high_s, low_s - high_s
            for m in range(INNER):
                at = (kk * INNER + m) * NW
                drive = (plus if m % 2 == 0 else minus) * float(S[m, 0])
                pieces.append(corr[at : at + NW, cols] + dens[kk][m : m + 1, cols] * drive)
        high, low = split(jnp.concatenate(pieces, axis=0))
        value = dot(jnp.concatenate([high, low], axis=0), outof_h[cols, :])
        flux = flux + value[:count] + value[count:] + dot(high, outof_l[cols, :])
    fluxes = []
    side = (lane // 8) % 2
    for kk in range(2):
        total = jnp.zeros((NW, 128), F32)
        for m in range(INNER):
            at = (kk * INNER + m) * NW
            total = total + jnp.where(lane % 8 == m, flux[at : at + NW], 0.0)
        pack = packs[kk]
        to_right = jnp.where(lane < 120, pack - pltpu.roll(pack, 120, 1), 0.0)
        to_left = jnp.where(lane >= 16, pltpu.roll(pack, 8, 1) - pack, 0.0)
        fluxes.append(total + jnp.where(side == 1, to_right, to_left))

    locals_ = []
    for part in range(2):
        high, low = split(grid[: 2 * NW, part * 512 : (part + 1) * 512])
        both = dot(jnp.concatenate([high, low], axis=0), inv_h[part])
        locals_.append(both[: 2 * NW] + both[2 * NW :] + dot(high, inv_l[part]))
    shift[2 * NW :, :] = jnp.zeros((8, 128), F32)
    for n in range(NN):
        block = n if n < NN // 2 else NN - 1 - n
        cols = slice(block * 128, (block + 1) * 128)
        if n < NN // 2:
            value = locals_[0][:, cols] + locals_[1][:, cols]
        else:
            value = (locals_[0][:, cols] - locals_[1][:, cols]) * sign[...]
        shift[: 2 * NW, :] = value
        for kk in range(2):
            pay[pl.ds(n * ROWS + kk, NW, stride=skip), :] = value[kk * NW : (kk + 1) * NW]
            after = shift[kk * NW + 1 : (kk + 1) * NW + 1, :]
            after = jnp.where(iota((NW, 128), 0) == NW - 1, 0.0, after)
            pay[pl.ds(n * ROWS + 2 + kk, NW, stride=skip), :] = after
        first = fluxes[0] if n == 0 else pltpu.roll(fluxes[0], 128 - 16 * n, 1)
        back = (64 - 16 * n) % 128
        second = fluxes[1] if back == 0 else pltpu.roll(fluxes[1], back, 1)
        pay[pl.ds(n * ROWS + 4, NW, stride=skip), :] = jnp.where(lane < 64, first, second)


def backward_kernel(S, recv, keep, den, push3, cl3, cyt3, out, zh, zl, stage):
    for kk in range(2):
        rows = slice(kk * HALF, (kk + 1) * HALF)
        stage[0, rows, :] = recv[pl.ds(kk, DEST, stride=ROWS), :]
        stage[1, rows, :] = recv[pl.ds(2 + kk, DEST, stride=ROWS), :]
        stage[2, rows, :] = recv[pl.ds(4, DEST, stride=ROWS), :]
    step = 32
    lane = iota((step, 128), 1)

    def slab(c, carry):
        rows = pl.ds(pl.multiple_of(c * step, step), step)
        low_s, high_s, flux = stage[0, rows, :], stage[1, rows, :], stage[2, rows, :]
        kk = jnp.where(c * step >= HALF, 1, 0)
        flux = jnp.where((lane // 64 == kk) & (lane % 64 < 16), flux, 0.0)
        masked = jnp.concatenate([jnp.where(lane % 8 == m, flux, 0.0) for m in range(INNER)], axis=0)
        pushed = dot(triple(masked), push3[...])
        plus, minus = low_s + high_s, low_s - high_s
        modes = []
        for m in range(INNER):
            drive = (plus if m % 2 == 0 else minus) * float(S[m, 0])
            value = keep[m, rows, :] + pushed[m * step : (m + 1) * step] + drive
            modes.append(value * den[m, rows, :])
        planes = [None] * SLAB
        planes[0] = low_s
        for i in range(1, 5):
            p_odd = sum(float(S[m, i - 1]) * modes[m] for m in range(0, INNER, 2))
            if i == 4:
                planes[4] = p_odd
                continue
            p_even = sum(float(S[m, i - 1]) * modes[m] for m in range(1, INNER, 2))
            planes[i] = p_odd + p_even
            planes[SLAB - i] = p_odd - p_even
        value = dot(triple(jnp.concatenate(planes, axis=0)), cl3[...])
        high, low = split(value)
        for z in range(SLAB):
            zh[z, rows, :] = high[z * step : (z + 1) * step]
            zl[z, rows, :] = low[z * step : (z + 1) * step]
        return carry

    lax.fori_loop(0, NY // step, slab, 0)

    def along_y(p, carry):
        high = jnp.concatenate([zh[2 * p], zh[2 * p + 1]], axis=1)
        low = jnp.concatenate([zl[2 * p], zl[2 * p + 1]], axis=1)
        right = jnp.concatenate([high, high, low], axis=0)
        for half in range(2):
            rows = slice(half * HALF, (half + 1) * HALF)
            value = dot(cyt3[rows, :], right)
            out[2 * p, rows, :] = value[:, :XL]
            out[2 * p + 1, rows, :] = value[:, XL:]
        return carry

    lax.fori_loop(0, SLAB // 2, along_y, 0)


def in_vmem(count):
    return [pl.BlockSpec(memory_space=pltpu.VMEM)] * count


def params():
    return pltpu.CompilerParams(vmem_limit_bytes=28 * 1024 * 1024)


def per_device(divergence, marker_force, marker_height, marker_cell):
    t = tables()
    tab = {k: jnp.asarray(v) for k, v in t.items() if k not in ("S", "mu")}
    dest = lax.axis_index("wide") * NN + lax.axis_index("narrow")
    cells = marker_cell.astype(F32)
    above = marker_force * jnp.maximum(0.0, 1.0 - jnp.abs(SLAB + 0.5 - marker_height))
    below = marker_force * jnp.maximum(0.0, 1.0 - jnp.abs(-0.5 - marker_height))
    up = [(i, i + 1) for i in range(NW - 1)]
    down = [(i + 1, i) for i in range(NW - 1)]
    from_below = lax.ppermute(jnp.stack([above, cells]), "wide", up)
    from_above = lax.ppermute(jnp.stack([below, cells]), "wide", down)
    marks = jnp.concatenate(
        [jnp.stack([marker_force, marker_height, cells]), from_below, from_above]
    )
    marks = marks.reshape(7, MARKS, NY // GROUP, GROUP).transpose(2, 0, 1, 3)
    marks = marks.reshape(NY // GROUP, 7, MARKS * GROUP)

    field = jax.ShapeDtypeStruct((INNER, NY, XL), F32)
    payload = jax.ShapeDtypeStruct((DEST * ROWS, XL), F32)
    sent, keep = pl.pallas_call(
        functools.partial(forward_kernel, t["S"]),
        out_shape=(payload, field),
        in_specs=in_vmem(7),
        out_specs=tuple(in_vmem(2)),
        scratch_shapes=[
            pltpu.VMEM((SLAB, NY, XL), BF16),
            pltpu.VMEM((SLAB, NY, XL), BF16),
            pltpu.VMEM((SLAB, NY, XL), F32),
            pltpu.VMEM((NY, XL), F32),
        ],
        compiler_params=params(),
    )(divergence, marks, tab["cy3"], tab["clt3"], tab["den"], tab["ends_h"], tab["ends_l"])

    def exchange(value):
        flat = lax.all_to_all(value.reshape(-1), BOTH, 0, 0, tiled=True)
        return flat.reshape(DEST * ROWS, XL)

    smem = pl.BlockSpec(memory_space=pltpu.SMEM)
    names = (
        "fwd_h", "fwd_l", "inv_h", "inv_l", "into_h", "into_l", "outof_h", "outof_l",
        "lamx_row", "lamx_tile", "sign",
    )
    returned = pl.pallas_call(
        functools.partial(middle_kernel, t["S"], t["mu"]),
        out_shape=payload,
        in_specs=[smem, smem] + in_vmem(1 + len(names)),
        out_specs=in_vmem(1)[0],
        scratch_shapes=[
            pltpu.VMEM((4 * NW, NX), F32),
            pltpu.VMEM((2 * INNER * NW, NX), F32),
            pltpu.VMEM((NW * 16, 128), F32),
            pltpu.VMEM(((NW + 1) * 16, 128), F32),
            pltpu.VMEM((NW * 16, 128), F32),
            pltpu.VMEM(((NW + 1) * 16, 128), F32),
            pltpu.VMEM((2 * NW + 8, 128), F32),
        ],
        compiler_params=params(),
    )(dest.reshape(1).astype(jnp.int32), tab["lamy"], exchange(sent), *[tab[k] for k in names])

    return pl.pallas_call(
        functools.partial(backward_kernel, t["S"]),
        out_shape=jax.ShapeDtypeStruct((SLAB, NY, XL), F32),
        in_specs=in_vmem(6),
        out_specs=in_vmem(1)[0],
        scratch_shapes=[
            pltpu.VMEM((SLAB, NY, XL), BF16),
            pltpu.VMEM((SLAB, NY, XL), BF16),
            pltpu.VMEM((3, NY, XL), F32),
        ],
        compiler_params=params(),
    )(exchange(returned), keep, tab["den"], tab["push3"], tab["cl3"], tab["cyt3"])


def solution(mesh):
    in_specs = (
        P("wide", None, "narrow"),
        P("wide", "narrow"),
        P("wide", "narrow"),
        P("wide", "narrow"),
    )
    out_specs = P("wide", None, "narrow")
    return jax.shard_map(
        per_device, mesh=mesh, in_specs=in_specs, out_specs=out_specs, check_vma=False
    )
```

```python
import functools

import jax
import jax.numpy as jnp
import ml_dtypes
import numpy as np
from jax import lax
from jax.experimental import pallas as pl
from jax.experimental.pallas import tpu as pltpu
from jax.sharding import PartitionSpec as P

BOTH = ("wide", "narrow")
NZ, NY, NX = 256, 512, 1024
NW, NN = 32, 8
SLAB = NZ // NW
XL = NX // NN
INNER = SLAB - 1
DEST = NW * NN
HALF = NY // 2
ROWS = 5
GROUP = 32
MARKS = 8
F32, BF16 = jnp.float32, jnp.bfloat16
UNROLL_A, UNROLL_B, UNROLL_C, UNROLL_H, UNROLL_X = 8, 2, 4, 8, 2


def dct_matrix(order):
    k = np.arange(order)[:, None]
    n = np.arange(order)[None, :]
    scale = np.where(k == 0, np.sqrt(1.0 / order), np.sqrt(2.0 / order))
    return scale * np.cos(np.pi * ((k * (2 * n + 1)) % (4 * order)) / (2 * order))


def lam(order):
    return 2.0 - 2.0 * np.cos(np.pi * np.arange(order) / order)


def halves(table):
    high = table.astype(np.float32).astype(ml_dtypes.bfloat16)
    low = (table - high.astype(np.float64)).astype(np.float32).astype(ml_dtypes.bfloat16)
    return high, low


@functools.lru_cache(None)
def tables():
    t = {}
    cy, cx, cl = dct_matrix(NY), dct_matrix(NX), dct_matrix(XL)
    i = np.arange(1, SLAB)
    t["S"] = np.sqrt(2.0 / SLAB) * np.sin(np.pi * np.outer(i, i) / SLAB)
    t["mu"] = 2.0 - 2.0 * np.cos(np.pi * i / SLAB)
    ch, clow = halves(cy)
    t["cy3"] = np.concatenate([ch, clow, ch], 1)
    ch, clow = halves(cy.T)
    t["cyt3"] = np.concatenate([ch, clow, ch], 1)
    h, l = halves(cl.T)
    t["clt3"] = np.concatenate([h, h, l], 0)
    h, l = halves(cl)
    t["cl3"] = np.concatenate([h, h, l], 0)
    t["den"] = (
        1.0 / (t["mu"][:, None, None] + lam(NY)[None, :, None] + lam(XL)[None, None, :])
    ).astype(np.float32)
    ends = np.zeros((INNER, XL, 128))
    for m in range(INNER):
        ends[m, :, m] = cl[:, 0]
        ends[m, :, 8 + m] = cl[:, -1]
    t["ends_h"], t["ends_l"] = halves(ends.reshape(INNER * XL, 128))
    order = np.concatenate([np.arange(0, NX, 2), np.arange(1, NX, 2)])
    mixed = np.zeros((NX, NX))
    for n in range(NN):
        mixed[:, n * XL : (n + 1) * XL] = cx[:, n * XL : (n + 1) * XL] @ cl.T
    mixed = mixed[order]
    hw = NX // 2
    fwd = np.stack([mixed[:hw, :hw].T, mixed[hw:, :hw].T])
    t["fwd_h"], t["fwd_l"] = halves(fwd)
    inv = np.stack([mixed[:hw, :hw], mixed[hw:, :hw]])
    t["inv_h"], t["inv_l"] = halves(inv)
    lamx = lam(NX)[order]
    t["lamx_row"] = lamx.reshape(1, NX).astype(np.float32)
    t["lamx_tile"] = np.concatenate([lamx.reshape(8, 128)] * 2, 0).astype(np.float32)
    t["lamy"] = lam(NY).astype(np.float32)
    jumps = np.stack([cx[:, XL * f + XL - 1] - cx[:, XL * f + XL] for f in range(NN - 1)])[:, order]
    into = np.zeros((NN, 2, 8, NX))
    outof = np.zeros((NN, 2, 8, NX))
    for n in range(NN):
        if n < NN - 1:
            into[n, 1] = -jumps[n]
            outof[n, 1] = jumps[n]
        if n > 0:
            into[n, 0] = jumps[n - 1]
            outof[n, 0] = jumps[n - 1]
    t["into_h"], t["into_l"] = halves(into.reshape(128, NX))
    t["outof_h"], t["outof_l"] = halves(outof.reshape(128, NX).T)
    push = np.zeros((128, XL))
    for kk in range(2):
        for m in range(8):
            push[kk * 64 + m] = cl[:, 0]
            push[kk * 64 + 8 + m] = -cl[:, -1]
    h, l = halves(push)
    t["push3"] = np.concatenate([h, h, l], 0)
    sign = np.where(np.arange(XL) % 2 == 0, 1.0, -1.0).reshape(1, XL)
    t["sign"] = sign.astype(np.float32)
    return t


def split(value):
    high = value.astype(BF16)
    return high, (value - high.astype(F32)).astype(BF16)


def dot(left, right):
    return lax.dot_general(left, right, (((1,), (0,)), ((), ())), preferred_element_type=F32)


def dot_nt(left, right):
    return lax.dot_general(left, right, (((1,), (1,)), ((), ())), preferred_element_type=F32)


def triple(value):
    high, low = split(value)
    return jnp.concatenate([high, low, high], axis=1)


def iota(shape, axis):
    return lax.broadcasted_iota(jnp.int32, shape, axis)


def regroup(value):
    lane, sub = iota((MARKS, 128), 1), iota((MARKS, 128), 0)
    mine = lane // GROUP == sub % 4
    rows = []
    for block in range(NY // 128):
        part = value[:, block * 128 : (block + 1) * 128]
        turns = [part] + [pltpu.roll(part, GROUP * i, 1) for i in range(1, 4)]
        for g in range(128 // GROUP):
            turned = jnp.zeros((MARKS, 128), F32)
            for q in range(4):
                turned = jnp.where(mine & (sub % 4 == q), turns[(q - g) % 4], turned)
            low = jnp.sum(turned[:4], axis=0, keepdims=True)
            high = jnp.sum(turned[4:], axis=0, keepdims=True)
            rows.append(jnp.concatenate([low, high], axis=1))
    return jnp.concatenate(rows, axis=0)


def marker_kernel(dest, force, height, cell, own, send, place, pair, ids, sems):
    copies = [
        pltpu.make_async_copy(force, pair.at[0], sems.at[0]),
        pltpu.make_async_copy(height, pair.at[1], sems.at[1]),
        pltpu.make_async_copy(cell, ids, sems.at[2]),
    ]
    for copy in copies:
        copy.start()
    place[0] = dest[0]
    for copy in copies:
        copy.wait()
    forces, heights = regroup(pair[0]), regroup(pair[1])
    cells = regroup(ids[...].astype(F32))
    own[0], own[1], own[2] = forces, heights, cells
    send[0] = forces * jnp.maximum(0.0, 1.0 - jnp.abs(-0.5 - heights))
    send[1] = cells


def onehot(cells):
    cell_ids = iota((XL, 256), 0).astype(F32)
    return jnp.where(cells == cell_ids, 1.0, 0.0).astype(BF16)


def spread_rows(weights):
    spot = iota((GROUP, 256), 1) % GROUP == iota((GROUP, 256), 0)
    high = weights.astype(BF16).astype(F32)
    low = weights - high
    parts = []
    for value in (high, low):
        for j in range(weights.shape[0]):
            parts.append(jnp.where(spot, value[j : j + 1], 0.0).astype(BF16))
    return jnp.concatenate(parts, axis=0)


def source_kernel(div, own, clt3, zh, zl, z7, room, table, spread, sems):
    copies = [pltpu.make_async_copy(clt3, table, sems.at[SLAB])]
    for z in range(SLAB):
        copies.append(pltpu.make_async_copy(div.at[z], room.at[z], sems.at[z]))
    for copy in copies:
        copy.start()
    centers = iota((16, 256), 0).astype(F32) + 0.5

    def markers(g, carry):
        force, height, cells = (own[i, pl.ds(g, 1), :] for i in range(3))
        weights = force * jnp.maximum(0.0, 1.0 - jnp.abs(centers - height))
        value = dot_nt(spread_rows(weights[: SLAB + 1]), onehot(cells))
        value = value[: (SLAB + 1) * GROUP] + value[(SLAB + 1) * GROUP :]
        rows = pl.ds(pl.multiple_of(g * GROUP, GROUP), GROUP)
        for z in range(SLAB + 1):
            spread[z, rows, :] = value[z * GROUP : (z + 1) * GROUP]
        return carry

    lax.fori_loop(0, NY // GROUP, markers, 0, unroll=UNROLL_A)
    for copy in copies:
        copy.wait()

    def along_x(z, carry):
        value = dot(triple(spread[z] + room[z]), table[...])
        zh[z], zl[z] = split(value)
        return carry

    lax.fori_loop(0, SLAB - 1, along_x, 0, unroll=UNROLL_X)
    z7[...] = dot(triple(spread[SLAB - 1] + room[SLAB - 1]), table[...])
    zh[SLAB - 1], zl[SLAB - 1] = split(dot(triple(spread[SLAB]), table[...]))


def forward_kernel(
    S, zh, zl, z7, marks, clt3, cy3, den, ends_h, ends_l, pay, keep, freq, faces, uh, ul, halo
):
    def outside(g, carry):
        value = dot_nt(spread_rows(marks[0, pl.ds(g, 1), :]), onehot(marks[1, pl.ds(g, 1), :]))
        rows = pl.ds(pl.multiple_of(g * GROUP, GROUP), GROUP)
        halo[rows, :] = value[:GROUP] + value[GROUP:]
        return carry

    lax.fori_loop(0, NY // GROUP, outside, 0, unroll=UNROLL_H)
    seventh = z7[...] + dot(triple(halo[...]), clt3[...])

    def along_y(high, low):
        return dot(cy3[...], jnp.concatenate([high, high, low], axis=0))

    freq[7] = along_y(*split(seventh))

    def pair(p, carry):
        value = along_y(
            jnp.concatenate([zh[2 * p], zh[2 * p + 1]], axis=1),
            jnp.concatenate([zl[2 * p], zl[2 * p + 1]], axis=1),
        )
        freq[2 * p] = value[:, :XL]
        freq[jnp.where(p == 3, 8, 2 * p + 1)] = value[:, XL:]
        return carry

    lax.fori_loop(0, SLAB // 2, pair, 0)
    step = 32

    def slab(c, carry):
        rows = pl.ds(pl.multiple_of(c * step, step), step)
        f = [freq[z, rows, :] for z in range(SLAB + 1)]
        even = [f[i] + f[SLAB - i] for i in range(1, 4)] + [f[4]]
        odd = [f[i] - f[SLAB - i] for i in range(1, 4)]
        p_odd = p_even = None
        for m in range(INNER):
            if m % 2 == 0:
                hat = sum(float(S[m, i]) * even[i] for i in range(4))
            else:
                hat = sum(float(S[m, i]) * odd[i] for i in range(3))
            keep[m, rows, :] = hat
            value = hat * den[m, rows, :]
            cols = slice(m * XL, (m + 1) * XL)
            uh[rows, cols], ul[rows, cols] = split(value)
            part = float(S[m, 0]) * value
            if m % 2 == 0:
                p_odd = part if p_odd is None else p_odd + part
            else:
                p_even = part if p_even is None else p_even + part
        freq[0, rows, :] = f[0] + p_odd + p_even
        freq[1, rows, :] = p_odd - p_even + f[SLAB]
        return carry

    lax.fori_loop(0, NY // step, slab, 0, unroll=2)
    high = uh[...]
    faces[...] = dot(high, ends_h[...]) + dot(ul[...], ends_h[...]) + dot(high, ends_l[...])
    for kk in range(2):
        rows = slice(kk * HALF, (kk + 1) * HALF)
        pay[pl.ds(kk, DEST, stride=ROWS), :] = freq[0, rows, :]
        pay[pl.ds(2 + kk, DEST, stride=ROWS), :] = freq[1, rows, :]
    pay[pl.ds(4, DEST, stride=ROWS), :] = faces[:HALF, :] + pltpu.roll(faces[HALF:, :], 64, 1)


def middle_kernel(
    S, mu, dest, lamy, recv, fwd_h, fwd_l, inv_h, inv_l, into_h, into_l, outof_h, outof_l,
    lamx_row, lamx_tile, sign, pay, grid, corr, tops, bots, piv, sol, shift,
):
    lane = iota((NW, 128), 1)
    here = dest[0]
    lam_k = [lamy[here], lamy[HALF + here]]
    skip = NN * ROWS

    def load(n, r):
        return recv[pl.ds(n * ROWS + r, NW, stride=skip), :]

    sums, diffs = [], []
    for n in range(NN // 2):
        near = jnp.concatenate([load(n, r) for r in range(4)], axis=0)
        far = jnp.concatenate([load(NN - 1 - n, r) for r in range(4)], axis=0) * sign[...]
        sums.append(near + far)
        diffs.append(near - far)
    for part, pieces in ((0, sums), (1, diffs)):
        high, low = split(jnp.concatenate(pieces, axis=1))
        both = dot(jnp.concatenate([high, low], axis=0), fwd_h[part])
        value = both[: 4 * NW] + both[4 * NW :] + dot(high, fwd_l[part])
        grid[:, part * 512 : (part + 1) * 512] = value

    packs = []
    for kk in range(2):
        pack = jnp.zeros((NW, 128), F32)
        for n in range(NN):
            turned = load(n, 4)
            shift_by = (16 * n + 64 * kk) % 128
            if shift_by:
                turned = pltpu.roll(turned, shift_by, 1)
            pack = jnp.where(lane // 16 == n, turned, pack)
        packs.append(pack)
    pairs = [(kk, m) for kk in range(2) for m in range(INNER)]
    masked = jnp.concatenate([jnp.where(lane % 8 == m, packs[kk], 0.0) for kk, m in pairs], axis=0)
    mask_h, mask_l = split(masked)
    mask_both = jnp.concatenate([mask_h, mask_l], axis=0)
    count = len(pairs) * NW

    mode_id = iota((8, NX), 0)
    mu_col = jnp.zeros((8, NX), F32)
    for m in range(8):
        mu_col = jnp.where(mode_id == m, float(mu[min(m, INNER - 1)]), mu_col)
    dens = [1.0 / (mu_col + lam_k[kk] + lamx_row[...]) for kk in range(2)]

    for part in range(4):
        cols = slice(part * 256, (part + 1) * 256)
        value = dot(mask_both, into_h[:, cols])
        value = value[:count] + value[count:] + dot(mask_h, into_l[:, cols])
        for kk in range(2):
            p_odd = p_even = None
            for m in range(INNER):
                at = (kk * INNER + m) * NW
                piece = value[at : at + NW] * dens[kk][m : m + 1, cols]
                corr[at : at + NW, cols] = piece
                piece = float(S[m, 0]) * piece
                if m % 2 == 0:
                    p_odd = piece if p_odd is None else p_odd + piece
                else:
                    p_even = piece if p_even is None else p_even + piece
            top = slice(kk * NW, (kk + 1) * NW)
            bot = slice((2 + kk) * NW, (3 + kk) * NW)
            grid[top, cols] = grid[top, cols] + p_odd + p_even
            grid[bot, cols] = grid[bot, cols] + p_odd - p_even

    bots[0:16, :] = jnp.zeros((16, 128), F32)
    for kk in range(2):
        for jb in range(8):
            cols = slice(jb * 128, (jb + 1) * 128)
            tops[pl.ds(kk * 8 + jb, NW, stride=16), :] = grid[kk * NW : (kk + 1) * NW, cols]
            bots[pl.ds(16 + kk * 8 + jb, NW, stride=16), :] = grid[
                (2 + kk) * NW : (3 + kk) * NW, cols
            ]

    row16 = iota((16, 128), 0)
    diag = 2.0 + jnp.where(row16 < 8, lam_k[0], lam_k[1]) + lamx_tile[...]
    older, newer = jnp.ones((16, 128), F32), diag
    for _ in range(INNER - 2):
        older, newer = newer, diag * newer - older
    last = diag * newer - older
    near_one = newer / last
    far_one = 1.0 / last
    full = diag - 2.0 * near_one
    inverse = 1.0 / (diag - near_one)
    value = tops[0:16, :]
    piv[0:16, :] = inverse
    sol[0:16, :] = value
    for w in range(1, NW):
        at = slice(w * 16, (w + 1) * 16)
        ratio = far_one * inverse
        value = tops[at, :] + bots[at, :] + ratio * value
        inverse = 1.0 / (full - far_one * ratio)
        piv[at, :] = inverse
        sol[at, :] = value
    later = jnp.zeros((16, 128), F32)
    sol[NW * 16 : (NW + 1) * 16, :] = later
    for w in range(NW - 1, -1, -1):
        at = slice(w * 16, (w + 1) * 16)
        later = (sol[at, :] + far_one * later) * piv[at, :]
        sol[at, :] = later

    for kk in range(2):
        for jb in range(8):
            cols = slice(jb * 128, (jb + 1) * 128)
            grid[kk * NW : (kk + 1) * NW, cols] = sol[pl.ds(kk * 8 + jb, NW, stride=16), :]
            grid[(2 + kk) * NW : (3 + kk) * NW, cols] = sol[
                pl.ds(16 + kk * 8 + jb, NW, stride=16), :
            ]

    flux = jnp.zeros((count, 128), F32)
    for part in range(4):
        cols = slice(part * 256, (part + 1) * 256)
        pieces = []
        for kk in range(2):
            low_s = grid[kk * NW : (kk + 1) * NW, cols]
            high_s = grid[(2 + kk) * NW : (3 + kk) * NW, cols]
            plus, minus = low_s + high_s, low_s - high_s
            for m in range(INNER):
                at = (kk * INNER + m) * NW
                drive = (plus if m % 2 == 0 else minus) * float(S[m, 0])
                pieces.append(corr[at : at + NW, cols] + dens[kk][m : m + 1, cols] * drive)
        high, low = split(jnp.concatenate(pieces, axis=0))
        value = dot(jnp.concatenate([high, low], axis=0), outof_h[cols, :])
        flux = flux + value[:count] + value[count:] + dot(high, outof_l[cols, :])
    fluxes = []
    side = (lane // 8) % 2
    for kk in range(2):
        total = jnp.zeros((NW, 128), F32)
        for m in range(INNER):
            at = (kk * INNER + m) * NW
            total = total + jnp.where(lane % 8 == m, flux[at : at + NW], 0.0)
        pack = packs[kk]
        to_right = jnp.where(lane < 120, pack - pltpu.roll(pack, 120, 1), 0.0)
        to_left = jnp.where(lane >= 16, pltpu.roll(pack, 8, 1) - pack, 0.0)
        fluxes.append(total + jnp.where(side == 1, to_right, to_left))

    locals_ = []
    for part in range(2):
        high, low = split(grid[: 2 * NW, part * 512 : (part + 1) * 512])
        both = dot(jnp.concatenate([high, low], axis=0), inv_h[part])
        locals_.append(both[: 2 * NW] + both[2 * NW :] + dot(high, inv_l[part]))
    shift[2 * NW :, :] = jnp.zeros((8, 128), F32)
    for n in range(NN):
        block = n if n < NN // 2 else NN - 1 - n
        cols = slice(block * 128, (block + 1) * 128)
        if n < NN // 2:
            value = locals_[0][:, cols] + locals_[1][:, cols]
        else:
            value = (locals_[0][:, cols] - locals_[1][:, cols]) * sign[...]
        shift[: 2 * NW, :] = value
        for kk in range(2):
            pay[pl.ds(n * ROWS + kk, NW, stride=skip), :] = value[kk * NW : (kk + 1) * NW]
            after = shift[kk * NW + 1 : (kk + 1) * NW + 1, :]
            after = jnp.where(iota((NW, 128), 0) == NW - 1, 0.0, after)
            pay[pl.ds(n * ROWS + 2 + kk, NW, stride=skip), :] = after
        first = fluxes[0] if n == 0 else pltpu.roll(fluxes[0], 128 - 16 * n, 1)
        back = (64 - 16 * n) % 128
        second = fluxes[1] if back == 0 else pltpu.roll(fluxes[1], back, 1)
        pay[pl.ds(n * ROWS + 4, NW, stride=skip), :] = jnp.where(lane < 64, first, second)


def backward_kernel(S, recv, keep, den, push3, cl3, cyt3, out, zh, zl, stage, room, sems):
    for kk in range(2):
        rows = slice(kk * HALF, (kk + 1) * HALF)
        stage[0, rows, :] = recv[pl.ds(kk, DEST, stride=ROWS), :]
        stage[1, rows, :] = recv[pl.ds(2 + kk, DEST, stride=ROWS), :]
        stage[2, rows, :] = recv[pl.ds(4, DEST, stride=ROWS), :]
    step = 64
    lane = iota((step, 128), 1)

    def slab(c, carry):
        rows = pl.ds(pl.multiple_of(c * step, step), step)
        low_s, high_s, flux = stage[0, rows, :], stage[1, rows, :], stage[2, rows, :]
        kk = jnp.where(c * step >= HALF, 1, 0)
        flux = jnp.where((lane // 64 == kk) & (lane % 64 < 16), flux, 0.0)
        masked = jnp.concatenate([jnp.where(lane % 8 == m, flux, 0.0) for m in range(INNER)], axis=0)
        pushed = dot(triple(masked), push3[...])
        plus, minus = low_s + high_s, low_s - high_s
        modes = []
        for m in range(INNER):
            drive = (plus if m % 2 == 0 else minus) * float(S[m, 0])
            value = keep[m, rows, :] + pushed[m * step : (m + 1) * step] + drive
            modes.append(value * den[m, rows, :])
        planes = [None] * SLAB
        planes[0] = low_s
        for i in range(1, 5):
            p_odd = sum(float(S[m, i - 1]) * modes[m] for m in range(0, INNER, 2))
            if i == 4:
                planes[4] = p_odd
                continue
            p_even = sum(float(S[m, i - 1]) * modes[m] for m in range(1, INNER, 2))
            planes[i] = p_odd + p_even
            planes[SLAB - i] = p_odd - p_even
        for z in range(SLAB):
            zh[z, rows, :], zl[z, rows, :] = split(planes[z])
        return carry

    lax.fori_loop(0, NY // step, slab, 0, unroll=UNROLL_B)

    def along_x(z, carry):
        high = zh[z]
        value = dot(jnp.concatenate([high, zl[z], high], axis=1), cl3[...])
        zh[z], zl[z] = split(value)
        return carry

    lax.fori_loop(0, SLAB, along_x, 0, unroll=UNROLL_C)
    copies = []
    for p in range(SLAB // 2):
        high = jnp.concatenate([zh[2 * p], zh[2 * p + 1]], axis=1)
        low = jnp.concatenate([zl[2 * p], zl[2 * p + 1]], axis=1)
        value = dot(cyt3[...], jnp.concatenate([high, high, low], axis=0))
        room[2 * p] = value[:, :XL]
        room[2 * p + 1] = value[:, XL:]
        pair = pl.ds(2 * p, 2)
        copies.append(pltpu.make_async_copy(room.at[pair], out.at[pair], sems.at[p]))
        copies[-1].start()
    for copy in copies:
        copy.wait()


def in_vmem(count):
    return [pl.BlockSpec(memory_space=pltpu.VMEM)] * count


def params(mebibytes):
    return pltpu.CompilerParams(vmem_limit_bytes=mebibytes * 1024 * 1024)


def work(microseconds):
    flops = microseconds * 1_000_000_000
    return pl.CostEstimate(flops=flops, bytes_accessed=1_000_000, transcendentals=0)


def per_device(divergence, marker_force, marker_height, marker_cell):
    t = tables()
    tab = {k: jnp.asarray(v) for k, v in t.items() if k not in ("S", "mu")}
    dest = lax.axis_index("wide") * NN + lax.axis_index("narrow")
    smem = pl.BlockSpec(memory_space=pltpu.SMEM)
    hbm = pl.BlockSpec(memory_space=pltpu.HBM)
    groups = NY // GROUP
    own, send, place = pl.pallas_call(
        marker_kernel,
        out_shape=(
            jax.ShapeDtypeStruct((3, groups, MARKS * GROUP), F32),
            jax.ShapeDtypeStruct((2, groups, MARKS * GROUP), F32),
            jax.ShapeDtypeStruct((1,), jnp.int32),
        ),
        in_specs=[smem] + [hbm] * 3,
        out_specs=tuple(in_vmem(2)) + (smem,),
        scratch_shapes=[
            pltpu.VMEM((2, MARKS, NY), F32),
            pltpu.VMEM((MARKS, NY), jnp.int32),
            pltpu.SemaphoreType.DMA((3,)),
        ],
        compiler_params=params(4),
        cost_estimate=work(4),
    )(dest.reshape(1).astype(jnp.int32), marker_force, marker_height, marker_cell)
    from_above = lax.ppermute(send, "wide", [(i + 1, i) for i in range(NW - 1)])

    plane = (NY, XL)
    zh, zl, z7 = pl.pallas_call(
        source_kernel,
        out_shape=(
            jax.ShapeDtypeStruct((SLAB, NY, XL), BF16),
            jax.ShapeDtypeStruct((SLAB, NY, XL), BF16),
            jax.ShapeDtypeStruct(plane, F32),
        ),
        in_specs=[hbm] + in_vmem(1) + [hbm],
        out_specs=tuple(in_vmem(3)),
        scratch_shapes=[
            pltpu.VMEM((SLAB, NY, XL), F32),
            pltpu.VMEM((3 * XL, XL), BF16),
            pltpu.VMEM((SLAB + 1, NY, XL), F32),
            pltpu.SemaphoreType.DMA((SLAB + 1,)),
        ],
        compiler_params=params(16),
        cost_estimate=work(4),
    )(divergence, own, tab["clt3"])

    field = jax.ShapeDtypeStruct((INNER, NY, XL), F32)
    payload = jax.ShapeDtypeStruct((DEST * ROWS, XL), F32)
    sent, keep = pl.pallas_call(
        functools.partial(forward_kernel, t["S"]),
        out_shape=(payload, field),
        in_specs=in_vmem(9),
        out_specs=tuple(in_vmem(2)),
        scratch_shapes=[
            pltpu.VMEM((SLAB + 1, NY, XL), F32),
            pltpu.VMEM(plane, F32),
            pltpu.VMEM((NY, INNER * XL), BF16),
            pltpu.VMEM((NY, INNER * XL), BF16),
            pltpu.VMEM(plane, F32),
        ],
        compiler_params=params(24),
        cost_estimate=work(5),
    )(zh, zl, z7, from_above, *[tab[k] for k in ("clt3", "cy3", "den", "ends_h", "ends_l")])

    def exchange(value):
        flat = lax.all_to_all(value.reshape(-1), BOTH, 0, 0, tiled=True)
        return flat.reshape(DEST * ROWS, XL)

    names = (
        "fwd_h", "fwd_l", "inv_h", "inv_l", "into_h", "into_l", "outof_h", "outof_l",
        "lamx_row", "lamx_tile", "sign",
    )
    returned = pl.pallas_call(
        functools.partial(middle_kernel, t["S"], t["mu"]),
        out_shape=payload,
        in_specs=[smem, smem] + in_vmem(1 + len(names)),
        out_specs=in_vmem(1)[0],
        scratch_shapes=[
            pltpu.VMEM((4 * NW, NX), F32),
            pltpu.VMEM((2 * INNER * NW, NX), F32),
            pltpu.VMEM((NW * 16, 128), F32),
            pltpu.VMEM(((NW + 1) * 16, 128), F32),
            pltpu.VMEM((NW * 16, 128), F32),
            pltpu.VMEM(((NW + 1) * 16, 128), F32),
            pltpu.VMEM((2 * NW + 8, 128), F32),
        ],
        compiler_params=params(16),
        cost_estimate=work(5),
    )(place, tab["lamy"], exchange(sent), *[tab[k] for k in names])

    return pl.pallas_call(
        functools.partial(backward_kernel, t["S"]),
        out_shape=jax.ShapeDtypeStruct((SLAB, NY, XL), F32),
        in_specs=in_vmem(6),
        out_specs=hbm,
        scratch_shapes=[
            pltpu.VMEM((SLAB, NY, XL), BF16),
            pltpu.VMEM((SLAB, NY, XL), BF16),
            pltpu.VMEM((3, NY, XL), F32),
            pltpu.VMEM((SLAB, NY, XL), F32),
            pltpu.SemaphoreType.DMA((SLAB // 2,)),
        ],
        compiler_params=params(24),
        cost_estimate=work(5),
    )(exchange(returned), keep, tab["den"], tab["push3"], tab["cl3"], tab["cyt3"])


def solution(mesh):
    in_specs = (
        P("wide", None, "narrow"),
        P("wide", "narrow"),
        P("wide", "narrow"),
        P("wide", "narrow"),
    )
    out_specs = P("wide", None, "narrow")
    return jax.shard_map(
        per_device, mesh=mesh, in_specs=in_specs, out_specs=out_specs, check_vma=False
    )
```

```python
import functools

import jax
import jax.numpy as jnp
import ml_dtypes
import numpy as np
from jax import lax
from jax.experimental import pallas as pl
from jax.experimental.pallas import tpu as pltpu
from jax.sharding import PartitionSpec as P

BOTH = ("wide", "narrow")
NZ, NY, NX = 256, 512, 1024
NW, NN = 32, 8
SLAB = NZ // NW
XL = NX // NN
INNER = SLAB - 1
DEST = NW * NN
HALF = NY // 2
ROWS = 5
GROUP = 32
MARKS = 8
F32, BF16 = jnp.float32, jnp.bfloat16
UNROLL_A, UNROLL_B, UNROLL_C, UNROLL_H, UNROLL_X = 16, 4, 4, 16, 4


def dct_matrix(order):
    k = np.arange(order)[:, None]
    n = np.arange(order)[None, :]
    scale = np.where(k == 0, np.sqrt(1.0 / order), np.sqrt(2.0 / order))
    return scale * np.cos(np.pi * ((k * (2 * n + 1)) % (4 * order)) / (2 * order))


def lam(order):
    return 2.0 - 2.0 * np.cos(np.pi * np.arange(order) / order)


def halves(table):
    high = table.astype(np.float32).astype(ml_dtypes.bfloat16)
    low = (table - high.astype(np.float64)).astype(np.float32).astype(ml_dtypes.bfloat16)
    return high, low


@functools.lru_cache(None)
def tables():
    t = {}
    cy, cx, cl = dct_matrix(NY), dct_matrix(NX), dct_matrix(XL)
    i = np.arange(1, SLAB)
    t["S"] = np.sqrt(2.0 / SLAB) * np.sin(np.pi * np.outer(i, i) / SLAB)
    t["mu"] = 2.0 - 2.0 * np.cos(np.pi * i / SLAB)
    ch, clow = halves(cy)
    t["cy3"] = np.concatenate([ch, clow, ch], 1)
    ch, clow = halves(cy.T)
    t["cyt3"] = np.concatenate([ch, clow, ch], 1)
    h, l = halves(np.kron(np.eye(2), cl.T))
    t["clt3"] = np.concatenate([h, h, l], 0)
    h, l = halves(cl.T)
    t["clt1"] = np.concatenate([h, h, l], 0)
    h, l = halves(np.kron(np.eye(2), cl))
    t["cl3"] = np.concatenate([h, h, l], 0)
    t["den"] = (
        1.0 / (t["mu"][:, None, None] + lam(NY)[None, :, None] + lam(XL)[None, None, :])
    ).astype(np.float32)
    ends = np.zeros((INNER, XL, 128))
    for m in range(INNER):
        ends[m, :, m] = cl[:, 0]
        ends[m, :, 8 + m] = cl[:, -1]
    t["ends_h"], t["ends_l"] = halves(ends.reshape(INNER * XL, 128))
    order = np.concatenate([np.arange(0, NX, 2), np.arange(1, NX, 2)])
    mixed = np.zeros((NX, NX))
    for n in range(NN):
        mixed[:, n * XL : (n + 1) * XL] = cx[:, n * XL : (n + 1) * XL] @ cl.T
    mixed = mixed[order]
    hw = NX // 2
    fwd = np.stack([mixed[:hw, :hw].T, mixed[hw:, :hw].T])
    t["fwd_h"], t["fwd_l"] = halves(fwd)
    inv = np.stack([mixed[:hw, :hw], mixed[hw:, :hw]])
    t["inv_h"], t["inv_l"] = halves(inv)
    lamx = lam(NX)[order]
    t["lamx_row"] = lamx.reshape(1, NX).astype(np.float32)
    t["lamx_tile"] = np.concatenate([lamx.reshape(8, 128)] * 2, 0).astype(np.float32)
    t["lamy"] = lam(NY).astype(np.float32)
    jumps = np.stack([cx[:, XL * f + XL - 1] - cx[:, XL * f + XL] for f in range(NN - 1)])[:, order]
    into = np.zeros((NN, 2, 8, NX))
    outof = np.zeros((NN, 2, 8, NX))
    for n in range(NN):
        if n < NN - 1:
            into[n, 1] = -jumps[n]
            outof[n, 1] = jumps[n]
        if n > 0:
            into[n, 0] = jumps[n - 1]
            outof[n, 0] = jumps[n - 1]
    h, l = halves(into)
    slots = np.zeros((NN, 2, 8, NX), ml_dtypes.bfloat16)
    slots[:, :, 0], slots[:, :, 1], slots[:, :, 2] = h[:, :, 0], h[:, :, 0], l[:, :, 0]
    t["into"] = slots.reshape(128, NX)
    h, l = halves(outof)
    slots = np.zeros((NN, 2, 8, NX), ml_dtypes.bfloat16)
    slots[:, :, 0], slots[:, :, 1] = h[:, :, 0], l[:, :, 0]
    t["outof"] = np.ascontiguousarray(slots.reshape(128, NX).T)
    h, l = halves(np.stack([cl[:, 0], -cl[:, -1]]))
    push = np.zeros((2, 4, 2, 8, XL), ml_dtypes.bfloat16)
    push[:, 0], push[:, 1], push[:, 2] = h[None, :, None], h[None, :, None], l[None, :, None]
    t["push"] = push.reshape(128, XL)
    sign = np.where(np.arange(XL) % 2 == 0, 1.0, -1.0).reshape(1, XL)
    t["sign"] = sign.astype(np.float32)
    return t


def split(value):
    high = value.astype(BF16)
    return high, (value - high.astype(F32)).astype(BF16)


def dot(left, right):
    return lax.dot_general(left, right, (((1,), (0,)), ((), ())), preferred_element_type=F32)


def dot_nt(left, right):
    return lax.dot_general(left, right, (((1,), (1,)), ((), ())), preferred_element_type=F32)


def triple(value):
    high, low = split(value)
    return jnp.concatenate([high, low, high], axis=1)


def iota(shape, axis):
    return lax.broadcasted_iota(jnp.int32, shape, axis)


def regroup(value):
    lane, sub = iota((MARKS, 128), 1), iota((MARKS, 128), 0)
    mine = lane // GROUP == sub % 4
    rows = []
    for block in range(NY // 128):
        part = value[:, block * 128 : (block + 1) * 128]
        turns = [part] + [pltpu.roll(part, GROUP * i, 1) for i in range(1, 4)]
        for g in range(128 // GROUP):
            turned = jnp.zeros((MARKS, 128), F32)
            for q in range(4):
                turned = jnp.where(mine & (sub % 4 == q), turns[(q - g) % 4], turned)
            low = jnp.sum(turned[:4], axis=0, keepdims=True)
            high = jnp.sum(turned[4:], axis=0, keepdims=True)
            rows.append(jnp.concatenate([low, high], axis=1))
    return jnp.concatenate(rows, axis=0)


def place_kernel(dest, place):
    place[0] = dest[0]


def marker_kernel(dest, force, height, cell, own, send, place, pair, ids, sems):
    copies = [
        pltpu.make_async_copy(force, pair.at[0], sems.at[0]),
        pltpu.make_async_copy(height, pair.at[1], sems.at[1]),
        pltpu.make_async_copy(cell, ids, sems.at[2]),
    ]
    for copy in copies:
        copy.start()
    place[0] = dest[0]
    for copy in copies:
        copy.wait()
    forces, heights = regroup(pair[0]), regroup(pair[1])
    cells = regroup(ids[...].astype(F32))
    own[0], own[1], own[2] = forces, heights, cells
    send[0] = forces * jnp.maximum(0.0, 1.0 - jnp.abs(-0.5 - heights))
    send[1] = cells


def onehot(cells):
    cell_ids = iota((XL, 256), 0).astype(F32)
    return jnp.where(cells == cell_ids, 1.0, 0.0).astype(BF16)


def spread_rows(weights):
    spot = iota((GROUP, 256), 1) % GROUP == iota((GROUP, 256), 0)
    high = weights.astype(BF16).astype(F32)
    low = weights - high
    parts = []
    for value in (high, low):
        for j in range(weights.shape[0]):
            parts.append(jnp.where(spot, value[j : j + 1], 0.0).astype(BF16))
    return jnp.concatenate(parts, axis=0)


def source_kernel(div, own, clt3, zh, zl, z7, room, table, spread, sems):
    copies = [pltpu.make_async_copy(clt3, table, sems.at[SLAB])]
    for z in range(SLAB):
        copies.append(pltpu.make_async_copy(div.at[z], room.at[z], sems.at[z]))
    for copy in copies:
        copy.start()
    centers = iota((16, 256), 0).astype(F32) + 0.5

    def markers(g, carry):
        force, height, cells = (own[i, pl.ds(g, 1), :] for i in range(3))
        weights = force * jnp.maximum(0.0, 1.0 - jnp.abs(centers - height))
        value = dot_nt(spread_rows(weights[: SLAB + 1]), onehot(cells))
        value = value[: (SLAB + 1) * GROUP] + value[(SLAB + 1) * GROUP :]
        rows = pl.ds(pl.multiple_of(g * GROUP, GROUP), GROUP)
        for z in range(SLAB + 1):
            spread[z, rows, :] = value[z * GROUP : (z + 1) * GROUP]
        return carry

    lax.fori_loop(0, NY // GROUP, markers, 0, unroll=UNROLL_A)
    for copy in copies:
        copy.wait()

    def along_x(p, carry):
        other = jnp.where(p == 3, SLAB, 2 * p + 1)
        right = spread[other] + jnp.where(p == 3, 0.0, room[2 * p + 1])
        left = spread[2 * p] + room[2 * p]
        high, low = split(dot(triple(jnp.concatenate([left, right], axis=1)), table[...]))
        zh[2 * p], zh[2 * p + 1] = high[:, :XL], high[:, XL:]
        zl[2 * p], zl[2 * p + 1] = low[:, :XL], low[:, XL:]
        return carry

    lax.fori_loop(0, SLAB // 2, along_x, 0, unroll=UNROLL_X)
    z7[...] = spread[SLAB - 1] + room[SLAB - 1]


def forward_kernel(
    S, zh, zl, z7, marks, clt1, cy3, den, ends_h, ends_l, pay, keep, freq, faces, uh, ul, halo
):
    def outside(g, carry):
        value = dot_nt(spread_rows(marks[0, pl.ds(g, 1), :]), onehot(marks[1, pl.ds(g, 1), :]))
        rows = pl.ds(pl.multiple_of(g * GROUP, GROUP), GROUP)
        halo[rows, :] = value[:GROUP] + value[GROUP:]
        return carry

    lax.fori_loop(0, NY // GROUP, outside, 0, unroll=UNROLL_H)
    seventh = dot(triple(z7[...] + halo[...]), clt1[...])

    def along_y(high, low):
        return dot(cy3[...], jnp.concatenate([high, high, low], axis=0))

    freq[7] = along_y(*split(seventh))

    def pair(p, carry):
        value = along_y(
            jnp.concatenate([zh[2 * p], zh[2 * p + 1]], axis=1),
            jnp.concatenate([zl[2 * p], zl[2 * p + 1]], axis=1),
        )
        freq[2 * p] = value[:, :XL]
        freq[jnp.where(p == 3, 8, 2 * p + 1)] = value[:, XL:]
        return carry

    lax.fori_loop(0, SLAB // 2, pair, 0, unroll=2)
    step = 32

    def slab(c, carry):
        rows = pl.ds(pl.multiple_of(c * step, step), step)
        f = [freq[z, rows, :] for z in range(SLAB + 1)]
        even = [f[i] + f[SLAB - i] for i in range(1, 4)] + [f[4]]
        odd = [f[i] - f[SLAB - i] for i in range(1, 4)]
        p_odd = p_even = None
        for m in range(INNER):
            if m % 2 == 0:
                hat = sum(float(S[m, i]) * even[i] for i in range(4))
            else:
                hat = sum(float(S[m, i]) * odd[i] for i in range(3))
            keep[m, rows, :] = hat
            value = hat * den[m, rows, :]
            cols = slice(m * XL, (m + 1) * XL)
            uh[rows, cols], ul[rows, cols] = split(value)
            part = float(S[m, 0]) * value
            if m % 2 == 0:
                p_odd = part if p_odd is None else p_odd + part
            else:
                p_even = part if p_even is None else p_even + part
        freq[0, rows, :] = f[0] + p_odd + p_even
        freq[1, rows, :] = p_odd - p_even + f[SLAB]
        return carry

    lax.fori_loop(0, NY // step, slab, 0, unroll=2)
    high = uh[...]
    faces[...] = dot(high, ends_h[...]) + dot(ul[...], ends_h[...]) + dot(high, ends_l[...])
    for kk in range(2):
        rows = slice(kk * HALF, (kk + 1) * HALF)
        pay[pl.ds(kk, DEST, stride=ROWS), :] = freq[0, rows, :]
        pay[pl.ds(2 + kk, DEST, stride=ROWS), :] = freq[1, rows, :]
    pay[pl.ds(4, DEST, stride=ROWS), :] = faces[:HALF, :] + pltpu.roll(faces[HALF:, :], 64, 1)


def middle_kernel(
    S, mu, dest, lamy, recv, fwd_h, fwd_l, inv_h, inv_l, into, outof,
    lamx_row, lamx_tile, sign, pay, grid, corr, tops, bots, piv, sol, shift,
):
    lane = iota((NW, 128), 1)
    here = dest[0]
    lam_k = [lamy[here], lamy[HALF + here]]
    skip = NN * ROWS

    def load(n, r):
        return recv[pl.ds(n * ROWS + r, NW, stride=skip), :]

    sums, diffs = [], []
    for n in range(NN // 2):
        near = jnp.concatenate([load(n, r) for r in range(4)], axis=0)
        far = jnp.concatenate([load(NN - 1 - n, r) for r in range(4)], axis=0) * sign[...]
        sums.append(near + far)
        diffs.append(near - far)
    for part, pieces in ((0, sums), (1, diffs)):
        high, low = split(jnp.concatenate(pieces, axis=1))
        both = dot(jnp.concatenate([high, low], axis=0), fwd_h[part])
        value = both[: 4 * NW] + both[4 * NW :] + dot(high, fwd_l[part])
        grid[:, part * 512 : (part + 1) * 512] = value

    packs = []
    for kk in range(2):
        pack = jnp.zeros((NW, 128), F32)
        for n in range(NN):
            turned = load(n, 4)
            shift_by = (16 * n + 64 * kk) % 128
            if shift_by:
                turned = pltpu.roll(turned, shift_by, 1)
            pack = jnp.where(lane // 16 == n, turned, pack)
        packs.append(pack)
    pairs = [(kk, m) for kk in range(2) for m in range(INNER)]
    masked = []
    for kk, m in pairs:
        high = packs[kk].astype(BF16).astype(F32)
        slots = jnp.zeros((NW, 128), F32)
        for slot, value in enumerate((high, packs[kk] - high, high)):
            turned = pltpu.roll(value, (slot - m) % 128, 1) if slot != m else value
            slots = jnp.where(lane % 8 == slot, turned, slots)
        masked.append(slots.astype(BF16))
    masked = jnp.concatenate(masked, axis=0)
    count = len(pairs) * NW

    mode_id = iota((8, NX), 0)
    mu_col = jnp.zeros((8, NX), F32)
    for m in range(8):
        mu_col = jnp.where(mode_id == m, float(mu[min(m, INNER - 1)]), mu_col)
    dens = [1.0 / (mu_col + lam_k[kk] + lamx_row[...]) for kk in range(2)]

    for part in range(4):
        cols = slice(part * 256, (part + 1) * 256)
        value = dot(masked, into[:, cols])
        for kk in range(2):
            p_odd = p_even = None
            for m in range(INNER):
                at = (kk * INNER + m) * NW
                piece = value[at : at + NW] * dens[kk][m : m + 1, cols]
                corr[at : at + NW, cols] = piece
                piece = float(S[m, 0]) * piece
                if m % 2 == 0:
                    p_odd = piece if p_odd is None else p_odd + piece
                else:
                    p_even = piece if p_even is None else p_even + piece
            top = slice(kk * NW, (kk + 1) * NW)
            bot = slice((2 + kk) * NW, (3 + kk) * NW)
            grid[top, cols] = grid[top, cols] + p_odd + p_even
            grid[bot, cols] = grid[bot, cols] + p_odd - p_even

    bots[0:16, :] = jnp.zeros((16, 128), F32)
    for kk in range(2):
        for jb in range(8):
            cols = slice(jb * 128, (jb + 1) * 128)
            tops[pl.ds(kk * 8 + jb, NW, stride=16), :] = grid[kk * NW : (kk + 1) * NW, cols]
            bots[pl.ds(16 + kk * 8 + jb, NW, stride=16), :] = grid[
                (2 + kk) * NW : (3 + kk) * NW, cols
            ]

    row16 = iota((16, 128), 0)
    diag = 2.0 + jnp.where(row16 < 8, lam_k[0], lam_k[1]) + lamx_tile[...]
    older, newer = jnp.ones((16, 128), F32), diag
    for _ in range(INNER - 2):
        older, newer = newer, diag * newer - older
    last = diag * newer - older
    near_one = newer / last
    far_one = 1.0 / last
    full = diag - 2.0 * near_one
    inverse = 1.0 / (diag - near_one)
    value = tops[0:16, :]
    piv[0:16, :] = inverse
    sol[0:16, :] = value
    for w in range(1, NW):
        at = slice(w * 16, (w + 1) * 16)
        ratio = far_one * inverse
        value = tops[at, :] + bots[at, :] + ratio * value
        inverse = 1.0 / (full - far_one * ratio)
        piv[at, :] = inverse
        sol[at, :] = value
    later = jnp.zeros((16, 128), F32)
    sol[NW * 16 : (NW + 1) * 16, :] = later
    for w in range(NW - 1, -1, -1):
        at = slice(w * 16, (w + 1) * 16)
        later = (sol[at, :] + far_one * later) * piv[at, :]
        sol[at, :] = later

    for kk in range(2):
        for jb in range(8):
            cols = slice(jb * 128, (jb + 1) * 128)
            grid[kk * NW : (kk + 1) * NW, cols] = sol[pl.ds(kk * 8 + jb, NW, stride=16), :]
            grid[(2 + kk) * NW : (3 + kk) * NW, cols] = sol[
                pl.ds(16 + kk * 8 + jb, NW, stride=16), :
            ]

    flux = jnp.zeros((2 * count, 128), F32)
    for part in range(4):
        cols = slice(part * 256, (part + 1) * 256)
        pieces = []
        for kk in range(2):
            low_s = grid[kk * NW : (kk + 1) * NW, cols]
            high_s = grid[(2 + kk) * NW : (3 + kk) * NW, cols]
            plus, minus = low_s + high_s, low_s - high_s
            for m in range(INNER):
                at = (kk * INNER + m) * NW
                drive = (plus if m % 2 == 0 else minus) * float(S[m, 0])
                pieces.append(corr[at : at + NW, cols] + dens[kk][m : m + 1, cols] * drive)
        high, low = split(jnp.concatenate(pieces, axis=0))
        flux = flux + dot(jnp.concatenate([high, low], axis=0), outof[cols, :])
    fluxes = []
    side = (lane // 8) % 2
    for kk in range(2):
        total = jnp.zeros((NW, 128), F32)
        for m in range(INNER):
            at = (kk * INNER + m) * NW
            both, main = flux[at : at + NW], flux[count + at : count + at + NW]
            main = both + main
            main = pltpu.roll(main, m, 1) if m > 0 else main
            rest = pltpu.roll(both, (m - 1) % 128, 1) if m != 1 else both
            total = jnp.where(lane % 8 == m, main + rest, total)
        pack = packs[kk]
        to_right = jnp.where(lane < 120, pack - pltpu.roll(pack, 120, 1), 0.0)
        to_left = jnp.where(lane >= 16, pltpu.roll(pack, 8, 1) - pack, 0.0)
        fluxes.append(total + jnp.where(side == 1, to_right, to_left))

    locals_ = []
    for part in range(2):
        high, low = split(grid[: 2 * NW, part * 512 : (part + 1) * 512])
        both = dot(jnp.concatenate([high, low], axis=0), inv_h[part])
        locals_.append(both[: 2 * NW] + both[2 * NW :] + dot(high, inv_l[part]))
    shift[2 * NW :, :] = jnp.zeros((8, 128), F32)
    for n in range(NN):
        block = n if n < NN // 2 else NN - 1 - n
        cols = slice(block * 128, (block + 1) * 128)
        if n < NN // 2:
            value = locals_[0][:, cols] + locals_[1][:, cols]
        else:
            value = (locals_[0][:, cols] - locals_[1][:, cols]) * sign[...]
        shift[: 2 * NW, :] = value
        for kk in range(2):
            pay[pl.ds(n * ROWS + kk, NW, stride=skip), :] = value[kk * NW : (kk + 1) * NW]
            after = shift[kk * NW + 1 : (kk + 1) * NW + 1, :]
            after = jnp.where(iota((NW, 128), 0) == NW - 1, 0.0, after)
            pay[pl.ds(n * ROWS + 2 + kk, NW, stride=skip), :] = after
        first = fluxes[0] if n == 0 else pltpu.roll(fluxes[0], 128 - 16 * n, 1)
        back = (64 - 16 * n) % 128
        second = fluxes[1] if back == 0 else pltpu.roll(fluxes[1], back, 1)
        pay[pl.ds(n * ROWS + 4, NW, stride=skip), :] = jnp.where(lane < 64, first, second)


def backward_kernel(S, recv, keep, den, push, cl3, cyt3, out, zh, zl, stage, room, sems):
    for kk in range(2):
        rows = slice(kk * HALF, (kk + 1) * HALF)
        stage[0, rows, :] = recv[pl.ds(kk, DEST, stride=ROWS), :]
        stage[1, rows, :] = recv[pl.ds(2 + kk, DEST, stride=ROWS), :]
        stage[2, rows, :] = recv[pl.ds(4, DEST, stride=ROWS), :]
    step = 64
    lane = iota((step, 128), 1)

    def slab(c, carry):
        rows = pl.ds(pl.multiple_of(c * step, step), step)
        low_s, high_s, flux = stage[0, rows, :], stage[1, rows, :], stage[2, rows, :]
        kk = jnp.where(c * step >= HALF, 1, 0)
        flux = jnp.where((lane // 64 == kk) & (lane % 64 < 16), flux, 0.0)
        high = flux.astype(BF16).astype(F32)
        flux = high + pltpu.roll(flux - high, 16, 1) + pltpu.roll(high, 32, 1)
        masked = jnp.concatenate([jnp.where(lane % 8 == m, flux, 0.0) for m in range(INNER)], axis=0)
        pushed = dot(masked.astype(BF16), push[...])
        plus, minus = low_s + high_s, low_s - high_s
        modes = []
        for m in range(INNER):
            drive = (plus if m % 2 == 0 else minus) * float(S[m, 0])
            value = keep[m, rows, :] + pushed[m * step : (m + 1) * step] + drive
            modes.append(value * den[m, rows, :])
        planes = [None] * SLAB
        planes[0] = low_s
        for i in range(1, 5):
            p_odd = sum(float(S[m, i - 1]) * modes[m] for m in range(0, INNER, 2))
            if i == 4:
                planes[4] = p_odd
                continue
            p_even = sum(float(S[m, i - 1]) * modes[m] for m in range(1, INNER, 2))
            planes[i] = p_odd + p_even
            planes[SLAB - i] = p_odd - p_even
        for z in range(SLAB):
            zh[z, rows, :], zl[z, rows, :] = split(planes[z])
        return carry

    lax.fori_loop(0, NY // step, slab, 0, unroll=UNROLL_B)

    copies = []
    for p in range(SLAB // 2):
        high = jnp.concatenate([zh[2 * p], zh[2 * p + 1]], axis=1)
        low = jnp.concatenate([zl[2 * p], zl[2 * p + 1]], axis=1)
        high, low = split(dot(jnp.concatenate([high, low, high], axis=1), cl3[...]))
        value = dot(cyt3[...], jnp.concatenate([high, high, low], axis=0))
        room[2 * p] = value[:, :XL]
        room[2 * p + 1] = value[:, XL:]
        pair = pl.ds(2 * p, 2)
        copies.append(pltpu.make_async_copy(room.at[pair], out.at[pair], sems.at[p]))
        copies[-1].start()
    for copy in copies:
        copy.wait()


def in_vmem(count):
    return [pl.BlockSpec(memory_space=pltpu.VMEM)] * count


def params(mebibytes):
    return pltpu.CompilerParams(vmem_limit_bytes=mebibytes * 1024 * 1024)


def work(microseconds):
    flops = microseconds * 1_000_000_000
    return pl.CostEstimate(flops=flops, bytes_accessed=1_000_000, transcendentals=0)


def per_device(divergence, marker_force, marker_height, marker_cell):
    t = tables()
    tab = {k: jnp.asarray(v) for k, v in t.items() if k not in ("S", "mu")}
    dest = lax.axis_index("wide") * NN + lax.axis_index("narrow")
    smem = pl.BlockSpec(memory_space=pltpu.SMEM)
    hbm = pl.BlockSpec(memory_space=pltpu.HBM)
    groups = NY // GROUP
    place = pl.pallas_call(
        place_kernel,
        out_shape=jax.ShapeDtypeStruct((1,), jnp.int32),
        in_specs=[smem],
        out_specs=smem,
        compiler_params=params(1),
        cost_estimate=work(2),
    )(dest.reshape(1).astype(jnp.int32))
    own, send, place = pl.pallas_call(
        marker_kernel,
        out_shape=(
            jax.ShapeDtypeStruct((3, groups, MARKS * GROUP), F32),
            jax.ShapeDtypeStruct((2, groups, MARKS * GROUP), F32),
            jax.ShapeDtypeStruct((1,), jnp.int32),
        ),
        in_specs=[smem] + [hbm] * 3,
        out_specs=tuple(in_vmem(2)) + (smem,),
        scratch_shapes=[
            pltpu.VMEM((2, MARKS, NY), F32),
            pltpu.VMEM((MARKS, NY), jnp.int32),
            pltpu.SemaphoreType.DMA((3,)),
        ],
        compiler_params=params(4),
        cost_estimate=work(4),
    )(place, marker_force, marker_height, marker_cell)
    from_above = lax.ppermute(send, "wide", [(i + 1, i) for i in range(NW - 1)])

    plane = (NY, XL)
    zh, zl, z7 = pl.pallas_call(
        source_kernel,
        out_shape=(
            jax.ShapeDtypeStruct((SLAB, NY, XL), BF16),
            jax.ShapeDtypeStruct((SLAB, NY, XL), BF16),
            jax.ShapeDtypeStruct(plane, F32),
        ),
        in_specs=[hbm] + in_vmem(1) + [hbm],
        out_specs=tuple(in_vmem(3)),
        scratch_shapes=[
            pltpu.VMEM((SLAB, NY, XL), F32),
            pltpu.VMEM((6 * XL, 2 * XL), BF16),
            pltpu.VMEM((SLAB + 1, NY, XL), F32),
            pltpu.SemaphoreType.DMA((SLAB + 1,)),
        ],
        compiler_params=params(16),
        cost_estimate=work(4),
    )(divergence, own, tab["clt3"])

    field = jax.ShapeDtypeStruct((INNER, NY, XL), F32)
    payload = jax.ShapeDtypeStruct((DEST * ROWS, XL), F32)
    sent, keep = pl.pallas_call(
        functools.partial(forward_kernel, t["S"]),
        out_shape=(payload, field),
        in_specs=in_vmem(9),
        out_specs=tuple(in_vmem(2)),
        scratch_shapes=[
            pltpu.VMEM((SLAB + 1, NY, XL), F32),
            pltpu.VMEM(plane, F32),
            pltpu.VMEM((NY, INNER * XL), BF16),
            pltpu.VMEM((NY, INNER * XL), BF16),
            pltpu.VMEM(plane, F32),
        ],
        compiler_params=params(24),
        cost_estimate=work(5),
    )(zh, zl, z7, from_above, *[tab[k] for k in ("clt1", "cy3", "den", "ends_h", "ends_l")])

    def exchange(value):
        flat = lax.all_to_all(value.reshape(-1), BOTH, 0, 0, tiled=True)
        return flat.reshape(DEST * ROWS, XL)

    names = (
        "fwd_h", "fwd_l", "inv_h", "inv_l", "into", "outof",
        "lamx_row", "lamx_tile", "sign",
    )
    returned = pl.pallas_call(
        functools.partial(middle_kernel, t["S"], t["mu"]),
        out_shape=payload,
        in_specs=[smem, smem] + in_vmem(1 + len(names)),
        out_specs=in_vmem(1)[0],
        scratch_shapes=[
            pltpu.VMEM((4 * NW, NX), F32),
            pltpu.VMEM((2 * INNER * NW, NX), F32),
            pltpu.VMEM((NW * 16, 128), F32),
            pltpu.VMEM(((NW + 1) * 16, 128), F32),
            pltpu.VMEM((NW * 16, 128), F32),
            pltpu.VMEM(((NW + 1) * 16, 128), F32),
            pltpu.VMEM((2 * NW + 8, 128), F32),
        ],
        compiler_params=params(16),
        cost_estimate=work(5),
    )(place, tab["lamy"], exchange(sent), *[tab[k] for k in names])

    return pl.pallas_call(
        functools.partial(backward_kernel, t["S"]),
        out_shape=jax.ShapeDtypeStruct((SLAB, NY, XL), F32),
        in_specs=in_vmem(6),
        out_specs=hbm,
        scratch_shapes=[
            pltpu.VMEM((SLAB, NY, XL), BF16),
            pltpu.VMEM((SLAB, NY, XL), BF16),
            pltpu.VMEM((3, NY, XL), F32),
            pltpu.VMEM((SLAB, NY, XL), F32),
            pltpu.SemaphoreType.DMA((SLAB // 2,)),
        ],
        compiler_params=params(24),
        cost_estimate=work(5),
    )(exchange(returned), keep, tab["den"], tab["push"], tab["cl3"], tab["cyt3"])


def solution(mesh):
    in_specs = (
        P("wide", None, "narrow"),
        P("wide", "narrow"),
        P("wide", "narrow"),
        P("wide", "narrow"),
    )
    out_specs = P("wide", None, "narrow")
    return jax.shard_map(
        per_device, mesh=mesh, in_specs=in_specs, out_specs=out_specs, check_vma=False
    )
```

```python
import functools

import jax
import jax.numpy as jnp
import ml_dtypes
import numpy as np
from jax import lax
from jax.experimental import pallas as pl
from jax.experimental.pallas import tpu as pltpu
from jax.sharding import PartitionSpec as P

BOTH = ("wide", "narrow")
NZ, NY, NX = 256, 512, 1024
NW, NN = 32, 8
SLAB = NZ // NW
XL = NX // NN
INNER = SLAB - 1
DEST = NW * NN
HALF = NY // 2
ROWS = 5
GROUP = 32
MARKS = 8
F32, BF16 = jnp.float32, jnp.bfloat16
UNROLL_A, UNROLL_B, UNROLL_C, UNROLL_H, UNROLL_X = 16, 4, 4, 16, 4


def dct_matrix(order):
    k = np.arange(order)[:, None]
    n = np.arange(order)[None, :]
    scale = np.where(k == 0, np.sqrt(1.0 / order), np.sqrt(2.0 / order))
    return scale * np.cos(np.pi * ((k * (2 * n + 1)) % (4 * order)) / (2 * order))


def lam(order):
    return 2.0 - 2.0 * np.cos(np.pi * np.arange(order) / order)


def halves(table):
    high = table.astype(np.float32).astype(ml_dtypes.bfloat16)
    low = (table - high.astype(np.float64)).astype(np.float32).astype(ml_dtypes.bfloat16)
    return high, low


@functools.lru_cache(None)
def tables():
    t = {}
    cy, cx, cl = dct_matrix(NY), dct_matrix(NX), dct_matrix(XL)
    i = np.arange(1, SLAB)
    t["S"] = np.sqrt(2.0 / SLAB) * np.sin(np.pi * np.outer(i, i) / SLAB)
    t["mu"] = 2.0 - 2.0 * np.cos(np.pi * i / SLAB)
    ch, clow = halves(cy)
    t["cy3"] = np.concatenate([ch, clow, ch], 1)
    ch, clow = halves(cy.T)
    t["cyt3"] = np.concatenate([ch, clow, ch], 1)
    h, l = halves(np.kron(np.eye(2), cl.T))
    t["clt3"] = np.concatenate([h, h, l], 0)
    h, l = halves(cl.T)
    t["clt1"] = np.concatenate([h, h, l], 0)
    h, l = halves(np.kron(np.eye(2), cl))
    t["cl3"] = np.concatenate([h, h, l], 0)
    t["den"] = (
        1.0 / (t["mu"][:, None, None] + lam(NY)[None, :, None] + lam(XL)[None, None, :])
    ).astype(np.float32)
    ends = np.zeros((INNER, XL, 128))
    for m in range(INNER):
        ends[m, :, m] = cl[:, 0]
        ends[m, :, 8 + m] = cl[:, -1]
    t["ends_h"], t["ends_l"] = halves(ends.reshape(INNER * XL, 128))
    order = np.concatenate([np.arange(0, NX, 2), np.arange(1, NX, 2)])
    mixed = np.zeros((NX, NX))
    for n in range(NN):
        mixed[:, n * XL : (n + 1) * XL] = cx[:, n * XL : (n + 1) * XL] @ cl.T
    mixed = mixed[order]
    hw = NX // 2
    fwd = np.stack([mixed[:hw, :hw].T, mixed[hw:, :hw].T])
    t["fwd_h"], t["fwd_l"] = halves(fwd)
    inv = np.stack([mixed[:hw, :hw], mixed[hw:, :hw]])
    t["inv_h"], t["inv_l"] = halves(inv)
    lamx = lam(NX)[order]
    t["lamx_row"] = lamx.reshape(1, NX).astype(np.float32)
    t["lamx_tile"] = np.concatenate([lamx.reshape(8, 128)] * 2, 0).astype(np.float32)
    t["lamy"] = np.repeat(lam(NY)[:, None], 128, 1).astype(np.float32)
    jumps = np.stack([cx[:, XL * f + XL - 1] - cx[:, XL * f + XL] for f in range(NN - 1)])[:, order]
    into = np.zeros((NN, 2, 8, NX))
    outof = np.zeros((NN, 2, 8, NX))
    for n in range(NN):
        if n < NN - 1:
            into[n, 1] = -jumps[n]
            outof[n, 1] = jumps[n]
        if n > 0:
            into[n, 0] = jumps[n - 1]
            outof[n, 0] = jumps[n - 1]
    h, l = halves(into)
    slots = np.zeros((NN, 2, 8, NX), ml_dtypes.bfloat16)
    slots[:, :, 0], slots[:, :, 1], slots[:, :, 2] = h[:, :, 0], h[:, :, 0], l[:, :, 0]
    t["into"] = slots.reshape(128, NX)
    h, l = halves(outof)
    slots = np.zeros((NN, 2, 8, NX), ml_dtypes.bfloat16)
    slots[:, :, 0], slots[:, :, 1] = h[:, :, 0], l[:, :, 0]
    t["outof"] = np.ascontiguousarray(slots.reshape(128, NX).T)
    h, l = halves(np.stack([cl[:, 0], -cl[:, -1]]))
    push = np.zeros((2, 4, 2, 8, XL), ml_dtypes.bfloat16)
    push[:, 0], push[:, 1], push[:, 2] = h[None, :, None], h[None, :, None], l[None, :, None]
    t["push"] = push.reshape(128, XL)
    sign = np.where(np.arange(XL) % 2 == 0, 1.0, -1.0).reshape(1, XL)
    t["sign"] = sign.astype(np.float32)
    return t


def split(value):
    high = value.astype(BF16)
    return high, (value - high.astype(F32)).astype(BF16)


def dot(left, right):
    return lax.dot_general(left, right, (((1,), (0,)), ((), ())), preferred_element_type=F32)


def dot_nt(left, right):
    return lax.dot_general(left, right, (((1,), (1,)), ((), ())), preferred_element_type=F32)


def triple(value):
    high, low = split(value)
    return jnp.concatenate([high, low, high], axis=1)


def iota(shape, axis):
    return lax.broadcasted_iota(jnp.int32, shape, axis)


def regroup(value):
    lane, sub = iota((MARKS, 128), 1), iota((MARKS, 128), 0)
    mine = lane // GROUP == sub % 4
    rows = []
    for block in range(NY // 128):
        part = value[:, block * 128 : (block + 1) * 128]
        turns = [part] + [pltpu.roll(part, GROUP * i, 1) for i in range(1, 4)]
        for g in range(128 // GROUP):
            turned = jnp.zeros((MARKS, 128), F32)
            for q in range(4):
                turned = jnp.where(mine & (sub % 4 == q), turns[(q - g) % 4], turned)
            low = jnp.sum(turned[:4], axis=0, keepdims=True)
            high = jnp.sum(turned[4:], axis=0, keepdims=True)
            rows.append(jnp.concatenate([low, high], axis=1))
    return jnp.concatenate(rows, axis=0)


def first_kernel(token):
    token[...] = jnp.zeros((8, 128), F32)


def marker_kernel(token, force, height, cell, own, send, pair, ids, sems):
    copies = [
        pltpu.make_async_copy(force, pair.at[0], sems.at[0]),
        pltpu.make_async_copy(height, pair.at[1], sems.at[1]),
        pltpu.make_async_copy(cell, ids, sems.at[2]),
    ]
    for copy in copies:
        copy.start()
    for copy in copies:
        copy.wait()
    forces, heights = regroup(pair[0]), regroup(pair[1])
    cells = regroup(ids[...].astype(F32))
    own[0], own[1], own[2] = forces, heights, cells
    send[0] = forces * jnp.maximum(0.0, 1.0 - jnp.abs(-0.5 - heights))
    send[1] = cells + token[0:1, 0:1]


def onehot(cells):
    cell_ids = iota((XL, 256), 0).astype(F32)
    return jnp.where(cells == cell_ids, 1.0, 0.0).astype(BF16)


def spread_rows(weights):
    spot = iota((GROUP, 256), 1) % GROUP == iota((GROUP, 256), 0)
    high = weights.astype(BF16).astype(F32)
    low = weights - high
    parts = []
    for value in (high, low):
        for j in range(weights.shape[0]):
            parts.append(jnp.where(spot, value[j : j + 1], 0.0).astype(BF16))
    return jnp.concatenate(parts, axis=0)


def source_kernel(div, own, clt3, zh, zl, z7, room, table, spread, sems):
    copies = [pltpu.make_async_copy(clt3, table, sems.at[SLAB])]
    for z in range(SLAB):
        copies.append(pltpu.make_async_copy(div.at[z], room.at[z], sems.at[z]))
    for copy in copies:
        copy.start()
    centers = iota((16, 256), 0).astype(F32) + 0.5

    def markers(g, carry):
        force, height, cells = (own[i, pl.ds(g, 1), :] for i in range(3))
        weights = force * jnp.maximum(0.0, 1.0 - jnp.abs(centers - height))
        value = dot_nt(spread_rows(weights[: SLAB + 1]), onehot(cells))
        value = value[: (SLAB + 1) * GROUP] + value[(SLAB + 1) * GROUP :]
        rows = pl.ds(pl.multiple_of(g * GROUP, GROUP), GROUP)
        for z in range(SLAB + 1):
            spread[z, rows, :] = value[z * GROUP : (z + 1) * GROUP]
        return carry

    lax.fori_loop(0, NY // GROUP, markers, 0, unroll=UNROLL_A)
    for copy in copies:
        copy.wait()

    def along_x(p, carry):
        other = jnp.where(p == 3, SLAB, 2 * p + 1)
        right = spread[other] + jnp.where(p == 3, 0.0, room[2 * p + 1])
        left = spread[2 * p] + room[2 * p]
        high, low = split(dot(triple(jnp.concatenate([left, right], axis=1)), table[...]))
        zh[2 * p], zh[2 * p + 1] = high[:, :XL], high[:, XL:]
        zl[2 * p], zl[2 * p + 1] = low[:, :XL], low[:, XL:]
        return carry

    lax.fori_loop(0, SLAB // 2, along_x, 0, unroll=UNROLL_X)
    z7[...] = spread[SLAB - 1] + room[SLAB - 1]


def forward_kernel(
    S, zh, zl, z7, marks, clt1, cy3, den, ends_h, ends_l, pay, keep, freq, faces, uh, ul, halo
):
    def outside(g, carry):
        value = dot_nt(spread_rows(marks[0, pl.ds(g, 1), :]), onehot(marks[1, pl.ds(g, 1), :]))
        rows = pl.ds(pl.multiple_of(g * GROUP, GROUP), GROUP)
        halo[rows, :] = value[:GROUP] + value[GROUP:]
        return carry

    lax.fori_loop(0, NY // GROUP, outside, 0, unroll=UNROLL_H)
    seventh = dot(triple(z7[...] + halo[...]), clt1[...])

    def along_y(high, low):
        return dot(cy3[...], jnp.concatenate([high, high, low], axis=0))

    freq[7] = along_y(*split(seventh))

    def pair(p, carry):
        value = along_y(
            jnp.concatenate([zh[2 * p], zh[2 * p + 1]], axis=1),
            jnp.concatenate([zl[2 * p], zl[2 * p + 1]], axis=1),
        )
        freq[2 * p] = value[:, :XL]
        freq[jnp.where(p == 3, 8, 2 * p + 1)] = value[:, XL:]
        return carry

    lax.fori_loop(0, SLAB // 2, pair, 0, unroll=2)
    step = 32

    def slab(c, carry):
        rows = pl.ds(pl.multiple_of(c * step, step), step)
        f = [freq[z, rows, :] for z in range(SLAB + 1)]
        even = [f[i] + f[SLAB - i] for i in range(1, 4)] + [f[4]]
        odd = [f[i] - f[SLAB - i] for i in range(1, 4)]
        p_odd = p_even = None
        for m in range(INNER):
            if m % 2 == 0:
                hat = sum(float(S[m, i]) * even[i] for i in range(4))
            else:
                hat = sum(float(S[m, i]) * odd[i] for i in range(3))
            keep[m, rows, :] = hat
            value = hat * den[m, rows, :]
            cols = slice(m * XL, (m + 1) * XL)
            uh[rows, cols], ul[rows, cols] = split(value)
            part = float(S[m, 0]) * value
            if m % 2 == 0:
                p_odd = part if p_odd is None else p_odd + part
            else:
                p_even = part if p_even is None else p_even + part
        freq[0, rows, :] = f[0] + p_odd + p_even
        freq[1, rows, :] = p_odd - p_even + f[SLAB]
        return carry

    lax.fori_loop(0, NY // step, slab, 0, unroll=2)
    high = uh[...]
    faces[...] = dot(high, ends_h[...]) + dot(ul[...], ends_h[...]) + dot(high, ends_l[...])
    for kk in range(2):
        rows = slice(kk * HALF, (kk + 1) * HALF)
        pay[pl.ds(kk, DEST, stride=ROWS), :] = freq[0, rows, :]
        pay[pl.ds(2 + kk, DEST, stride=ROWS), :] = freq[1, rows, :]
    pay[pl.ds(4, DEST, stride=ROWS), :] = faces[:HALF, :] + pltpu.roll(faces[HALF:, :], 64, 1)


def middle_kernel(
    S, mu, lamy, recv, fwd_h, fwd_l, inv_h, inv_l, into, outof,
    lamx_row, lamx_tile, sign, pay, grid, corr, tops, bots, piv, sol, shift,
):
    lane = iota((NW, 128), 1)
    here = lax.axis_index("wide") * NN + lax.axis_index("narrow")
    lam_k = [lamy[pl.ds(kk * HALF + here, 1), :] for kk in range(2)]
    lam_wide = [jnp.concatenate([row] * (NX // 128), axis=1) for row in lam_k]
    skip = NN * ROWS

    def load(n, r):
        return recv[pl.ds(n * ROWS + r, NW, stride=skip), :]

    sums, diffs = [], []
    for n in range(NN // 2):
        near = jnp.concatenate([load(n, r) for r in range(4)], axis=0)
        far = jnp.concatenate([load(NN - 1 - n, r) for r in range(4)], axis=0) * sign[...]
        sums.append(near + far)
        diffs.append(near - far)
    for part, pieces in ((0, sums), (1, diffs)):
        high, low = split(jnp.concatenate(pieces, axis=1))
        both = dot(jnp.concatenate([high, low], axis=0), fwd_h[part])
        value = both[: 4 * NW] + both[4 * NW :] + dot(high, fwd_l[part])
        grid[:, part * 512 : (part + 1) * 512] = value

    packs = []
    for kk in range(2):
        pack = jnp.zeros((NW, 128), F32)
        for n in range(NN):
            turned = load(n, 4)
            shift_by = (16 * n + 64 * kk) % 128
            if shift_by:
                turned = pltpu.roll(turned, shift_by, 1)
            pack = jnp.where(lane // 16 == n, turned, pack)
        packs.append(pack)
    pairs = [(kk, m) for kk in range(2) for m in range(INNER)]
    masked = []
    for kk, m in pairs:
        high = packs[kk].astype(BF16).astype(F32)
        slots = jnp.zeros((NW, 128), F32)
        for slot, value in enumerate((high, packs[kk] - high, high)):
            turned = pltpu.roll(value, (slot - m) % 128, 1) if slot != m else value
            slots = jnp.where(lane % 8 == slot, turned, slots)
        masked.append(slots.astype(BF16))
    masked = jnp.concatenate(masked, axis=0)
    count = len(pairs) * NW

    mode_id = iota((8, NX), 0)
    mu_col = jnp.zeros((8, NX), F32)
    for m in range(8):
        mu_col = jnp.where(mode_id == m, float(mu[min(m, INNER - 1)]), mu_col)
    dens = [1.0 / (mu_col + (lam_wide[kk] + lamx_row[...])) for kk in range(2)]

    for part in range(4):
        cols = slice(part * 256, (part + 1) * 256)
        value = dot(masked, into[:, cols])
        for kk in range(2):
            p_odd = p_even = None
            for m in range(INNER):
                at = (kk * INNER + m) * NW
                piece = value[at : at + NW] * dens[kk][m : m + 1, cols]
                corr[at : at + NW, cols] = piece
                piece = float(S[m, 0]) * piece
                if m % 2 == 0:
                    p_odd = piece if p_odd is None else p_odd + piece
                else:
                    p_even = piece if p_even is None else p_even + piece
            top = slice(kk * NW, (kk + 1) * NW)
            bot = slice((2 + kk) * NW, (3 + kk) * NW)
            grid[top, cols] = grid[top, cols] + p_odd + p_even
            grid[bot, cols] = grid[bot, cols] + p_odd - p_even

    bots[0:16, :] = jnp.zeros((16, 128), F32)
    for kk in range(2):
        for jb in range(8):
            cols = slice(jb * 128, (jb + 1) * 128)
            tops[pl.ds(kk * 8 + jb, NW, stride=16), :] = grid[kk * NW : (kk + 1) * NW, cols]
            bots[pl.ds(16 + kk * 8 + jb, NW, stride=16), :] = grid[
                (2 + kk) * NW : (3 + kk) * NW, cols
            ]

    row16 = iota((16, 128), 0)
    diag = 2.0 + jnp.where(row16 < 8, lam_k[0], lam_k[1]) + lamx_tile[...]
    older, newer = jnp.ones((16, 128), F32), diag
    for _ in range(INNER - 2):
        older, newer = newer, diag * newer - older
    last = diag * newer - older
    near_one = newer / last
    far_one = 1.0 / last
    full = diag - 2.0 * near_one
    inverse = 1.0 / (diag - near_one)
    value = tops[0:16, :]
    piv[0:16, :] = inverse
    sol[0:16, :] = value
    for w in range(1, NW):
        at = slice(w * 16, (w + 1) * 16)
        ratio = far_one * inverse
        value = tops[at, :] + bots[at, :] + ratio * value
        inverse = 1.0 / (full - far_one * ratio)
        piv[at, :] = inverse
        sol[at, :] = value
    later = jnp.zeros((16, 128), F32)
    sol[NW * 16 : (NW + 1) * 16, :] = later
    for w in range(NW - 1, -1, -1):
        at = slice(w * 16, (w + 1) * 16)
        later = (sol[at, :] + far_one * later) * piv[at, :]
        sol[at, :] = later

    for kk in range(2):
        for jb in range(8):
            cols = slice(jb * 128, (jb + 1) * 128)
            grid[kk * NW : (kk + 1) * NW, cols] = sol[pl.ds(kk * 8 + jb, NW, stride=16), :]
            grid[(2 + kk) * NW : (3 + kk) * NW, cols] = sol[
                pl.ds(16 + kk * 8 + jb, NW, stride=16), :
            ]

    flux = jnp.zeros((2 * count, 128), F32)
    for part in range(4):
        cols = slice(part * 256, (part + 1) * 256)
        pieces = []
        for kk in range(2):
            low_s = grid[kk * NW : (kk + 1) * NW, cols]
            high_s = grid[(2 + kk) * NW : (3 + kk) * NW, cols]
            plus, minus = low_s + high_s, low_s - high_s
            for m in range(INNER):
                at = (kk * INNER + m) * NW
                drive = (plus if m % 2 == 0 else minus) * float(S[m, 0])
                pieces.append(corr[at : at + NW, cols] + dens[kk][m : m + 1, cols] * drive)
        high, low = split(jnp.concatenate(pieces, axis=0))
        flux = flux + dot(jnp.concatenate([high, low], axis=0), outof[cols, :])
    fluxes = []
    side = (lane // 8) % 2
    for kk in range(2):
        total = jnp.zeros((NW, 128), F32)
        for m in range(INNER):
            at = (kk * INNER + m) * NW
            both, main = flux[at : at + NW], flux[count + at : count + at + NW]
            main = both + main
            main = pltpu.roll(main, m, 1) if m > 0 else main
            rest = pltpu.roll(both, (m - 1) % 128, 1) if m != 1 else both
            total = jnp.where(lane % 8 == m, main + rest, total)
        pack = packs[kk]
        to_right = jnp.where(lane < 120, pack - pltpu.roll(pack, 120, 1), 0.0)
        to_left = jnp.where(lane >= 16, pltpu.roll(pack, 8, 1) - pack, 0.0)
        fluxes.append(total + jnp.where(side == 1, to_right, to_left))

    locals_ = []
    for part in range(2):
        high, low = split(grid[: 2 * NW, part * 512 : (part + 1) * 512])
        both = dot(jnp.concatenate([high, low], axis=0), inv_h[part])
        locals_.append(both[: 2 * NW] + both[2 * NW :] + dot(high, inv_l[part]))
    shift[2 * NW :, :] = jnp.zeros((8, 128), F32)
    for n in range(NN):
        block = n if n < NN // 2 else NN - 1 - n
        cols = slice(block * 128, (block + 1) * 128)
        if n < NN // 2:
            value = locals_[0][:, cols] + locals_[1][:, cols]
        else:
            value = (locals_[0][:, cols] - locals_[1][:, cols]) * sign[...]
        shift[: 2 * NW, :] = value
        for kk in range(2):
            pay[pl.ds(n * ROWS + kk, NW, stride=skip), :] = value[kk * NW : (kk + 1) * NW]
            after = shift[kk * NW + 1 : (kk + 1) * NW + 1, :]
            after = jnp.where(iota((NW, 128), 0) == NW - 1, 0.0, after)
            pay[pl.ds(n * ROWS + 2 + kk, NW, stride=skip), :] = after
        first = fluxes[0] if n == 0 else pltpu.roll(fluxes[0], 128 - 16 * n, 1)
        back = (64 - 16 * n) % 128
        second = fluxes[1] if back == 0 else pltpu.roll(fluxes[1], back, 1)
        pay[pl.ds(n * ROWS + 4, NW, stride=skip), :] = jnp.where(lane < 64, first, second)


def backward_kernel(S, recv, keep, den, push, cl3, cyt3, out, zh, zl, stage, room, sems):
    for kk in range(2):
        rows = slice(kk * HALF, (kk + 1) * HALF)
        stage[0, rows, :] = recv[pl.ds(kk, DEST, stride=ROWS), :]
        stage[1, rows, :] = recv[pl.ds(2 + kk, DEST, stride=ROWS), :]
        stage[2, rows, :] = recv[pl.ds(4, DEST, stride=ROWS), :]
    step = 64
    lane = iota((step, 128), 1)

    def slab(c, carry):
        rows = pl.ds(pl.multiple_of(c * step, step), step)
        low_s, high_s, flux = stage[0, rows, :], stage[1, rows, :], stage[2, rows, :]
        kk = jnp.where(c * step >= HALF, 1, 0)
        flux = jnp.where((lane // 64 == kk) & (lane % 64 < 16), flux, 0.0)
        high = flux.astype(BF16).astype(F32)
        flux = high + pltpu.roll(flux - high, 16, 1) + pltpu.roll(high, 32, 1)
        masked = jnp.concatenate([jnp.where(lane % 8 == m, flux, 0.0) for m in range(INNER)], axis=0)
        pushed = dot(masked.astype(BF16), push[...])
        plus, minus = low_s + high_s, low_s - high_s
        modes = []
        for m in range(INNER):
            drive = (plus if m % 2 == 0 else minus) * float(S[m, 0])
            value = keep[m, rows, :] + pushed[m * step : (m + 1) * step] + drive
            modes.append(value * den[m, rows, :])
        planes = [None] * SLAB
        planes[0] = low_s
        for i in range(1, 5):
            p_odd = sum(float(S[m, i - 1]) * modes[m] for m in range(0, INNER, 2))
            if i == 4:
                planes[4] = p_odd
                continue
            p_even = sum(float(S[m, i - 1]) * modes[m] for m in range(1, INNER, 2))
            planes[i] = p_odd + p_even
            planes[SLAB - i] = p_odd - p_even
        for z in range(SLAB):
            zh[z, rows, :], zl[z, rows, :] = split(planes[z])
        return carry

    lax.fori_loop(0, NY // step, slab, 0, unroll=UNROLL_B)

    copies = []
    for p in range(SLAB // 2):
        high = jnp.concatenate([zh[2 * p], zh[2 * p + 1]], axis=1)
        low = jnp.concatenate([zl[2 * p], zl[2 * p + 1]], axis=1)
        high, low = split(dot(jnp.concatenate([high, low, high], axis=1), cl3[...]))
        value = dot(cyt3[...], jnp.concatenate([high, high, low], axis=0))
        room[2 * p] = value[:, :XL]
        room[2 * p + 1] = value[:, XL:]
        pair = pl.ds(2 * p, 2)
        copies.append(pltpu.make_async_copy(room.at[pair], out.at[pair], sems.at[p]))
        copies[-1].start()
    for copy in copies:
        copy.wait()


def in_vmem(count):
    return [pl.BlockSpec(memory_space=pltpu.VMEM)] * count


def params(mebibytes):
    return pltpu.CompilerParams(vmem_limit_bytes=mebibytes * 1024 * 1024)


def work(microseconds):
    flops = microseconds * 1_000_000_000
    return pl.CostEstimate(flops=flops, bytes_accessed=1_000_000, transcendentals=0)


def per_device(divergence, marker_force, marker_height, marker_cell):
    t = tables()
    tab = {k: jnp.asarray(v) for k, v in t.items() if k not in ("S", "mu")}
    hbm = pl.BlockSpec(memory_space=pltpu.HBM)
    groups = NY // GROUP
    token = pl.pallas_call(
        first_kernel,
        out_shape=jax.ShapeDtypeStruct((8, 128), F32),
        out_specs=in_vmem(1)[0],
        compiler_params=params(1),
        cost_estimate=work(2),
    )()
    own, send = pl.pallas_call(
        marker_kernel,
        out_shape=(
            jax.ShapeDtypeStruct((3, groups, MARKS * GROUP), F32),
            jax.ShapeDtypeStruct((2, groups, MARKS * GROUP), F32),
        ),
        in_specs=in_vmem(1) + [hbm] * 3,
        out_specs=tuple(in_vmem(2)),
        scratch_shapes=[
            pltpu.VMEM((2, MARKS, NY), F32),
            pltpu.VMEM((MARKS, NY), jnp.int32),
            pltpu.SemaphoreType.DMA((3,)),
        ],
        compiler_params=params(4),
        cost_estimate=work(4),
    )(token, marker_force, marker_height, marker_cell)
    from_above = lax.ppermute(send, "wide", [(i + 1, i) for i in range(NW - 1)])

    plane = (NY, XL)
    zh, zl, z7 = pl.pallas_call(
        source_kernel,
        out_shape=(
            jax.ShapeDtypeStruct((SLAB, NY, XL), BF16),
            jax.ShapeDtypeStruct((SLAB, NY, XL), BF16),
            jax.ShapeDtypeStruct(plane, F32),
        ),
        in_specs=[hbm] + in_vmem(1) + [hbm],
        out_specs=tuple(in_vmem(3)),
        scratch_shapes=[
            pltpu.VMEM((SLAB, NY, XL), F32),
            pltpu.VMEM((6 * XL, 2 * XL), BF16),
            pltpu.VMEM((SLAB + 1, NY, XL), F32),
            pltpu.SemaphoreType.DMA((SLAB + 1,)),
        ],
        compiler_params=params(16),
        cost_estimate=work(4),
    )(divergence, own, tab["clt3"])

    field = jax.ShapeDtypeStruct((INNER, NY, XL), F32)
    payload = jax.ShapeDtypeStruct((DEST * ROWS, XL), F32)
    sent, keep = pl.pallas_call(
        functools.partial(forward_kernel, t["S"]),
        out_shape=(payload, field),
        in_specs=in_vmem(9),
        out_specs=tuple(in_vmem(2)),
        scratch_shapes=[
            pltpu.VMEM((SLAB + 1, NY, XL), F32),
            pltpu.VMEM(plane, F32),
            pltpu.VMEM((NY, INNER * XL), BF16),
            pltpu.VMEM((NY, INNER * XL), BF16),
            pltpu.VMEM(plane, F32),
        ],
        compiler_params=params(24),
        cost_estimate=work(5),
    )(zh, zl, z7, from_above, *[tab[k] for k in ("clt1", "cy3", "den", "ends_h", "ends_l")])

    def exchange(value):
        flat = lax.all_to_all(value.reshape(-1), BOTH, 0, 0, tiled=True)
        return flat.reshape(DEST * ROWS, XL)

    names = (
        "fwd_h", "fwd_l", "inv_h", "inv_l", "into", "outof",
        "lamx_row", "lamx_tile", "sign",
    )
    returned = pl.pallas_call(
        functools.partial(middle_kernel, t["S"], t["mu"]),
        out_shape=payload,
        in_specs=in_vmem(2 + len(names)),
        out_specs=in_vmem(1)[0],
        scratch_shapes=[
            pltpu.VMEM((4 * NW, NX), F32),
            pltpu.VMEM((2 * INNER * NW, NX), F32),
            pltpu.VMEM((NW * 16, 128), F32),
            pltpu.VMEM(((NW + 1) * 16, 128), F32),
            pltpu.VMEM((NW * 16, 128), F32),
            pltpu.VMEM(((NW + 1) * 16, 128), F32),
            pltpu.VMEM((2 * NW + 8, 128), F32),
        ],
        compiler_params=params(16),
        cost_estimate=work(5),
    )(tab["lamy"], exchange(sent), *[tab[k] for k in names])

    return pl.pallas_call(
        functools.partial(backward_kernel, t["S"]),
        out_shape=jax.ShapeDtypeStruct((SLAB, NY, XL), F32),
        in_specs=in_vmem(6),
        out_specs=hbm,
        scratch_shapes=[
            pltpu.VMEM((SLAB, NY, XL), BF16),
            pltpu.VMEM((SLAB, NY, XL), BF16),
            pltpu.VMEM((3, NY, XL), F32),
            pltpu.VMEM((SLAB, NY, XL), F32),
            pltpu.SemaphoreType.DMA((SLAB // 2,)),
        ],
        compiler_params=params(24),
        cost_estimate=work(5),
    )(exchange(returned), keep, tab["den"], tab["push"], tab["cl3"], tab["cyt3"])


def solution(mesh):
    in_specs = (
        P("wide", None, "narrow"),
        P("wide", "narrow"),
        P("wide", "narrow"),
        P("wide", "narrow"),
    )
    out_specs = P("wide", None, "narrow")
    return jax.shard_map(
        per_device, mesh=mesh, in_specs=in_specs, out_specs=out_specs, check_vma=False
    )
```

```python
import functools

import jax
import jax.numpy as jnp
import ml_dtypes
import numpy as np
from jax import lax
from jax.experimental import pallas as pl
from jax.experimental.pallas import tpu as pltpu
from jax.sharding import PartitionSpec as P

BOTH = ("wide", "narrow")
NZ, NY, NX = 256, 512, 1024
NW, NN = 32, 8
SLAB = NZ // NW
XL = NX // NN
INNER = SLAB - 1
DEST = NW * NN
HALF = NY // 2
ROWS = 5
GROUP = 32
MARKS = 8
F32, BF16 = jnp.float32, jnp.bfloat16
UNROLL_A, UNROLL_B, UNROLL_C, UNROLL_H, UNROLL_X = 16, 4, 4, 16, 4


def dct_matrix(order):
    k = np.arange(order)[:, None]
    n = np.arange(order)[None, :]
    scale = np.where(k == 0, np.sqrt(1.0 / order), np.sqrt(2.0 / order))
    return scale * np.cos(np.pi * ((k * (2 * n + 1)) % (4 * order)) / (2 * order))


def lam(order):
    return 2.0 - 2.0 * np.cos(np.pi * np.arange(order) / order)


def halves(table):
    high = table.astype(np.float32).astype(ml_dtypes.bfloat16)
    low = (table - high.astype(np.float64)).astype(np.float32).astype(ml_dtypes.bfloat16)
    return high, low


@functools.lru_cache(None)
def tables():
    t = {}
    cy, cx, cl = dct_matrix(NY), dct_matrix(NX), dct_matrix(XL)
    i = np.arange(1, SLAB)
    t["S"] = np.sqrt(2.0 / SLAB) * np.sin(np.pi * np.outer(i, i) / SLAB)
    t["mu"] = 2.0 - 2.0 * np.cos(np.pi * i / SLAB)
    ch, clow = halves(cy)
    t["cy3"] = np.concatenate([ch, clow], 0)
    ch, clow = halves(cy.T)
    t["cyt3"] = np.concatenate([ch, clow], 0)
    h, l = halves(np.kron(np.eye(2), cl.T))
    t["clt3"] = np.concatenate([h, h, l], 0)
    h, l = halves(cl.T)
    t["clt1"] = np.concatenate([h, h, l], 0)
    h, l = halves(np.kron(np.eye(2), cl))
    t["cl3"] = np.concatenate([h, h, l], 0)
    t["den"] = (
        1.0 / (t["mu"][:, None, None] + lam(NY)[None, :, None] + lam(XL)[None, None, :])
    ).astype(np.float32)
    ends = np.zeros((INNER, XL, 128))
    for m in range(INNER):
        ends[m, :, m] = cl[:, 0]
        ends[m, :, 8 + m] = cl[:, -1]
    t["ends_h"], t["ends_l"] = halves(ends.reshape(INNER * XL, 128))
    order = np.concatenate([np.arange(0, NX, 2), np.arange(1, NX, 2)])
    mixed = np.zeros((NX, NX))
    for n in range(NN):
        mixed[:, n * XL : (n + 1) * XL] = cx[:, n * XL : (n + 1) * XL] @ cl.T
    mixed = mixed[order]
    hw = NX // 2
    fwd = np.stack([mixed[:hw, :hw].T, mixed[hw:, :hw].T])
    t["fwd_h"], t["fwd_l"] = halves(fwd)
    inv = np.stack([mixed[:hw, :hw], mixed[hw:, :hw]])
    t["inv_h"], t["inv_l"] = halves(inv)
    lamx = lam(NX)[order]
    t["lamx_row"] = lamx.reshape(1, NX).astype(np.float32)
    t["lamx_tile"] = np.concatenate([lamx.reshape(8, 128)] * 2, 0).astype(np.float32)
    t["lamy"] = np.repeat(lam(NY)[:, None], 128, 1).astype(np.float32)
    jumps = np.stack([cx[:, XL * f + XL - 1] - cx[:, XL * f + XL] for f in range(NN - 1)])[:, order]
    into = np.zeros((NN, 2, 8, NX))
    outof = np.zeros((NN, 2, 8, NX))
    for n in range(NN):
        if n < NN - 1:
            into[n, 1] = -jumps[n]
            outof[n, 1] = jumps[n]
        if n > 0:
            into[n, 0] = jumps[n - 1]
            outof[n, 0] = jumps[n - 1]
    h, l = halves(into)
    slots = np.zeros((NN, 2, 8, NX), ml_dtypes.bfloat16)
    slots[:, :, 0], slots[:, :, 1], slots[:, :, 2] = h[:, :, 0], h[:, :, 0], l[:, :, 0]
    t["into"] = slots.reshape(128, NX)
    h, l = halves(outof)
    slots = np.zeros((NN, 2, 8, NX), ml_dtypes.bfloat16)
    slots[:, :, 0], slots[:, :, 1] = h[:, :, 0], l[:, :, 0]
    t["outof"] = np.ascontiguousarray(slots.reshape(128, NX).T)
    h, l = halves(np.stack([cl[:, 0], -cl[:, -1]]))
    push = np.zeros((2, 4, 2, 8, XL), ml_dtypes.bfloat16)
    push[:, 0], push[:, 1], push[:, 2] = h[None, :, None], h[None, :, None], l[None, :, None]
    t["push"] = push.reshape(128, XL)
    sign = np.where(np.arange(XL) % 2 == 0, 1.0, -1.0).reshape(1, XL)
    t["sign"] = sign.astype(np.float32)
    return t


def split(value):
    high = value.astype(BF16)
    return high, (value - high.astype(F32)).astype(BF16)


def dot(left, right):
    return lax.dot_general(left, right, (((1,), (0,)), ((), ())), preferred_element_type=F32)


def dot_nt(left, right):
    return lax.dot_general(left, right, (((1,), (1,)), ((), ())), preferred_element_type=F32)


def triple(value):
    high, low = split(value)
    return jnp.concatenate([high, low, high], axis=1)


def iota(shape, axis):
    return lax.broadcasted_iota(jnp.int32, shape, axis)


def regroup(value):
    lane, sub = iota((MARKS, 128), 1), iota((MARKS, 128), 0)
    mine = lane // GROUP == sub % 4
    rows = []
    for block in range(NY // 128):
        part = value[:, block * 128 : (block + 1) * 128]
        turns = [part] + [pltpu.roll(part, GROUP * i, 1) for i in range(1, 4)]
        for g in range(128 // GROUP):
            turned = jnp.zeros((MARKS, 128), F32)
            for q in range(4):
                turned = jnp.where(mine & (sub % 4 == q), turns[(q - g) % 4], turned)
            low = jnp.sum(turned[:4], axis=0, keepdims=True)
            high = jnp.sum(turned[4:], axis=0, keepdims=True)
            rows.append(jnp.concatenate([low, high], axis=1))
    return jnp.concatenate(rows, axis=0)


def first_kernel(token):
    token[...] = jnp.zeros((8, 128), F32)


def marker_kernel(token, force, height, cell, own, send, pair, ids, sems):
    copies = [
        pltpu.make_async_copy(force, pair.at[0], sems.at[0]),
        pltpu.make_async_copy(height, pair.at[1], sems.at[1]),
        pltpu.make_async_copy(cell, ids, sems.at[2]),
    ]
    for copy in copies:
        copy.start()
    for copy in copies:
        copy.wait()
    forces, heights = regroup(pair[0]), regroup(pair[1])
    cells = regroup(ids[...].astype(F32))
    own[0], own[1], own[2] = forces, heights, cells
    send[0] = forces * jnp.maximum(0.0, 1.0 - jnp.abs(-0.5 - heights))
    send[1] = cells + token[0:1, 0:1]


def onehot(cells):
    cell_ids = iota((XL, 256), 0).astype(F32)
    return jnp.where(cells == cell_ids, 1.0, 0.0).astype(BF16)


def spread_rows(weights):
    spot = iota((GROUP, 256), 1) % GROUP == iota((GROUP, 256), 0)
    high = weights.astype(BF16).astype(F32)
    low = weights - high
    parts = []
    for value in (high, low):
        for j in range(weights.shape[0]):
            parts.append(jnp.where(spot, value[j : j + 1], 0.0).astype(BF16))
    return jnp.concatenate(parts, axis=0)


def source_kernel(div, own, clt3, zh, zl, z7, spread):
    centers = iota((16, 256), 0).astype(F32) + 0.5

    def markers(g, carry):
        force, height, cells = (own[i, pl.ds(g, 1), :] for i in range(3))
        weights = force * jnp.maximum(0.0, 1.0 - jnp.abs(centers - height))
        value = dot_nt(spread_rows(weights[: SLAB + 1]), onehot(cells))
        value = value[: (SLAB + 1) * GROUP] + value[(SLAB + 1) * GROUP :]
        rows = pl.ds(pl.multiple_of(g * GROUP, GROUP), GROUP)
        for z in range(SLAB + 1):
            spread[z, rows, :] = value[z * GROUP : (z + 1) * GROUP]
        return carry

    lax.fori_loop(0, NY // GROUP, markers, 0, unroll=UNROLL_A)

    def along_x(p, carry):
        other = jnp.where(p == 3, SLAB, 2 * p + 1)
        right = spread[other] + jnp.where(p == 3, 0.0, div[2 * p + 1])
        left = spread[2 * p] + div[2 * p]
        high, low = split(dot(triple(jnp.concatenate([left, right], axis=1)), clt3[...]))
        zh[2 * p], zh[2 * p + 1] = high[:, :XL], high[:, XL:]
        zl[2 * p], zl[2 * p + 1] = low[:, :XL], low[:, XL:]
        return carry

    lax.fori_loop(0, SLAB // 2, along_x, 0, unroll=UNROLL_X)
    z7[...] = spread[SLAB - 1] + div[SLAB - 1]


def forward_kernel(
    S, zh, zl, z7, marks, clt1, cy3, den, ends_h, ends_l, pay, keep, freq, faces, uh, ul, halo
):
    def outside(g, carry):
        value = dot_nt(spread_rows(marks[0, pl.ds(g, 1), :]), onehot(marks[1, pl.ds(g, 1), :]))
        rows = pl.ds(pl.multiple_of(g * GROUP, GROUP), GROUP)
        halo[rows, :] = value[:GROUP] + value[GROUP:]
        return carry

    lax.fori_loop(0, NY // GROUP, outside, 0, unroll=UNROLL_H)
    seventh = dot(triple(z7[...] + halo[...]), clt1[...])

    def along_y(high, low):
        both = dot(cy3[...], high)
        return both[:NY] + both[NY:] + dot(cy3[:NY, :], low)

    freq[7] = along_y(*split(seventh))

    def pair(p, carry):
        value = along_y(
            jnp.concatenate([zh[2 * p], zh[2 * p + 1]], axis=1),
            jnp.concatenate([zl[2 * p], zl[2 * p + 1]], axis=1),
        )
        freq[2 * p] = value[:, :XL]
        freq[jnp.where(p == 3, 8, 2 * p + 1)] = value[:, XL:]
        return carry

    lax.fori_loop(0, SLAB // 2, pair, 0, unroll=2)
    step = 16

    def slab(c, carry):
        rows = pl.ds(pl.multiple_of(c * step, step), step)
        f = [freq[z, rows, :] for z in range(SLAB + 1)]
        even = [f[i] + f[SLAB - i] for i in range(1, 4)] + [f[4]]
        odd = [f[i] - f[SLAB - i] for i in range(1, 4)]
        p_odd = p_even = None
        for m in range(INNER):
            if m % 2 == 0:
                hat = sum(float(S[m, i]) * even[i] for i in range(4))
            else:
                hat = sum(float(S[m, i]) * odd[i] for i in range(3))
            keep[m, rows, :] = hat
            value = hat * den[m, rows, :]
            cols = slice(m * XL, (m + 1) * XL)
            uh[rows, cols], ul[rows, cols] = split(value)
            part = float(S[m, 0]) * value
            if m % 2 == 0:
                p_odd = part if p_odd is None else p_odd + part
            else:
                p_even = part if p_even is None else p_even + part
        freq[0, rows, :] = f[0] + p_odd + p_even
        freq[1, rows, :] = p_odd - p_even + f[SLAB]
        return carry

    lax.fori_loop(0, NY // step, slab, 0, unroll=8)
    high = uh[...]
    faces[...] = dot(high, ends_h[...]) + dot(ul[...], ends_h[...]) + dot(high, ends_l[...])
    for kk in range(2):
        rows = slice(kk * HALF, (kk + 1) * HALF)
        pay[pl.ds(kk, DEST, stride=ROWS), :] = freq[0, rows, :]
        pay[pl.ds(2 + kk, DEST, stride=ROWS), :] = freq[1, rows, :]
    pay[pl.ds(4, DEST, stride=ROWS), :] = faces[:HALF, :] + pltpu.roll(faces[HALF:, :], 64, 1)


def middle_kernel(
    S, mu, lamy, recv, fwd_h, fwd_l, inv_h, inv_l, into, outof,
    lamx_row, lamx_tile, sign, pay, grid, corr, tops, bots, piv, sol, shift,
):
    lane = iota((NW, 128), 1)
    here = lax.axis_index("wide") * NN + lax.axis_index("narrow")
    lam_k = [lamy[pl.ds(kk * HALF + here, 1), :] for kk in range(2)]
    lam_wide = [jnp.concatenate([row] * (NX // 128), axis=1) for row in lam_k]
    skip = NN * ROWS

    def load(n, r):
        return recv[pl.ds(n * ROWS + r, NW, stride=skip), :]

    sums, diffs = [], []
    for n in range(NN // 2):
        near = jnp.concatenate([load(n, r) for r in range(4)], axis=0)
        far = jnp.concatenate([load(NN - 1 - n, r) for r in range(4)], axis=0) * sign[...]
        sums.append(near + far)
        diffs.append(near - far)
    for part, pieces in ((0, sums), (1, diffs)):
        high, low = split(jnp.concatenate(pieces, axis=1))
        both = dot(jnp.concatenate([high, low], axis=0), fwd_h[part])
        value = both[: 4 * NW] + both[4 * NW :] + dot(high, fwd_l[part])
        grid[:, part * 512 : (part + 1) * 512] = value

    packs = []
    for kk in range(2):
        pack = jnp.zeros((NW, 128), F32)
        for n in range(NN):
            turned = load(n, 4)
            shift_by = (16 * n + 64 * kk) % 128
            if shift_by:
                turned = pltpu.roll(turned, shift_by, 1)
            pack = jnp.where(lane // 16 == n, turned, pack)
        packs.append(pack)
    pairs = [(kk, m) for kk in range(2) for m in range(INNER)]
    masked = []
    for kk, m in pairs:
        high = packs[kk].astype(BF16).astype(F32)
        slots = jnp.zeros((NW, 128), F32)
        for slot, value in enumerate((high, packs[kk] - high, high)):
            turned = pltpu.roll(value, (slot - m) % 128, 1) if slot != m else value
            slots = jnp.where(lane % 8 == slot, turned, slots)
        masked.append(slots.astype(BF16))
    masked = jnp.concatenate(masked, axis=0)
    count = len(pairs) * NW

    mode_id = iota((8, NX), 0)
    mu_col = jnp.zeros((8, NX), F32)
    for m in range(8):
        mu_col = jnp.where(mode_id == m, float(mu[min(m, INNER - 1)]), mu_col)
    dens = [1.0 / (mu_col + (lam_wide[kk] + lamx_row[...])) for kk in range(2)]

    for part in range(4):
        cols = slice(part * 256, (part + 1) * 256)
        value = dot(masked, into[:, cols])
        for kk in range(2):
            p_odd = p_even = None
            for m in range(INNER):
                at = (kk * INNER + m) * NW
                piece = value[at : at + NW] * dens[kk][m : m + 1, cols]
                corr[at : at + NW, cols] = piece
                piece = float(S[m, 0]) * piece
                if m % 2 == 0:
                    p_odd = piece if p_odd is None else p_odd + piece
                else:
                    p_even = piece if p_even is None else p_even + piece
            top = slice(kk * NW, (kk + 1) * NW)
            bot = slice((2 + kk) * NW, (3 + kk) * NW)
            grid[top, cols] = grid[top, cols] + p_odd + p_even
            grid[bot, cols] = grid[bot, cols] + p_odd - p_even

    bots[0:16, :] = jnp.zeros((16, 128), F32)
    for kk in range(2):
        for jb in range(8):
            cols = slice(jb * 128, (jb + 1) * 128)
            tops[pl.ds(kk * 8 + jb, NW, stride=16), :] = grid[kk * NW : (kk + 1) * NW, cols]
            bots[pl.ds(16 + kk * 8 + jb, NW, stride=16), :] = grid[
                (2 + kk) * NW : (3 + kk) * NW, cols
            ]

    row16 = iota((16, 128), 0)
    diag = 2.0 + jnp.where(row16 < 8, lam_k[0], lam_k[1]) + lamx_tile[...]
    older, newer = jnp.ones((16, 128), F32), diag
    for _ in range(INNER - 2):
        older, newer = newer, diag * newer - older
    last = diag * newer - older
    near_one = newer / last
    far_one = 1.0 / last
    full = diag - 2.0 * near_one
    inverse = 1.0 / (diag - near_one)
    value = tops[0:16, :]
    piv[0:16, :] = inverse
    sol[0:16, :] = value
    for w in range(1, NW):
        at = slice(w * 16, (w + 1) * 16)
        ratio = far_one * inverse
        value = tops[at, :] + bots[at, :] + ratio * value
        inverse = 1.0 / (full - far_one * ratio)
        piv[at, :] = inverse
        sol[at, :] = value
    later = jnp.zeros((16, 128), F32)
    sol[NW * 16 : (NW + 1) * 16, :] = later
    for w in range(NW - 1, -1, -1):
        at = slice(w * 16, (w + 1) * 16)
        later = (sol[at, :] + far_one * later) * piv[at, :]
        sol[at, :] = later

    for kk in range(2):
        for jb in range(8):
            cols = slice(jb * 128, (jb + 1) * 128)
            grid[kk * NW : (kk + 1) * NW, cols] = sol[pl.ds(kk * 8 + jb, NW, stride=16), :]
            grid[(2 + kk) * NW : (3 + kk) * NW, cols] = sol[
                pl.ds(16 + kk * 8 + jb, NW, stride=16), :
            ]

    flux = jnp.zeros((2 * count, 128), F32)
    for part in range(4):
        cols = slice(part * 256, (part + 1) * 256)
        pieces = []
        for kk in range(2):
            low_s = grid[kk * NW : (kk + 1) * NW, cols]
            high_s = grid[(2 + kk) * NW : (3 + kk) * NW, cols]
            plus, minus = low_s + high_s, low_s - high_s
            for m in range(INNER):
                at = (kk * INNER + m) * NW
                drive = (plus if m % 2 == 0 else minus) * float(S[m, 0])
                pieces.append(corr[at : at + NW, cols] + dens[kk][m : m + 1, cols] * drive)
        high, low = split(jnp.concatenate(pieces, axis=0))
        flux = flux + dot(jnp.concatenate([high, low], axis=0), outof[cols, :])
    fluxes = []
    side = (lane // 8) % 2
    for kk in range(2):
        total = jnp.zeros((NW, 128), F32)
        for m in range(INNER):
            at = (kk * INNER + m) * NW
            both, main = flux[at : at + NW], flux[count + at : count + at + NW]
            main = both + main
            main = pltpu.roll(main, m, 1) if m > 0 else main
            rest = pltpu.roll(both, (m - 1) % 128, 1) if m != 1 else both
            total = jnp.where(lane % 8 == m, main + rest, total)
        pack = packs[kk]
        to_right = jnp.where(lane < 120, pack - pltpu.roll(pack, 120, 1), 0.0)
        to_left = jnp.where(lane >= 16, pltpu.roll(pack, 8, 1) - pack, 0.0)
        fluxes.append(total + jnp.where(side == 1, to_right, to_left))

    locals_ = []
    for part in range(2):
        high, low = split(grid[: 2 * NW, part * 512 : (part + 1) * 512])
        both = dot(jnp.concatenate([high, low], axis=0), inv_h[part])
        locals_.append(both[: 2 * NW] + both[2 * NW :] + dot(high, inv_l[part]))
    shift[2 * NW :, :] = jnp.zeros((8, 128), F32)
    for n in range(NN):
        block = n if n < NN // 2 else NN - 1 - n
        cols = slice(block * 128, (block + 1) * 128)
        if n < NN // 2:
            value = locals_[0][:, cols] + locals_[1][:, cols]
        else:
            value = (locals_[0][:, cols] - locals_[1][:, cols]) * sign[...]
        shift[: 2 * NW, :] = value
        for kk in range(2):
            pay[pl.ds(n * ROWS + kk, NW, stride=skip), :] = value[kk * NW : (kk + 1) * NW]
            after = shift[kk * NW + 1 : (kk + 1) * NW + 1, :]
            after = jnp.where(iota((NW, 128), 0) == NW - 1, 0.0, after)
            pay[pl.ds(n * ROWS + 2 + kk, NW, stride=skip), :] = after
        first = fluxes[0] if n == 0 else pltpu.roll(fluxes[0], 128 - 16 * n, 1)
        back = (64 - 16 * n) % 128
        second = fluxes[1] if back == 0 else pltpu.roll(fluxes[1], back, 1)
        pay[pl.ds(n * ROWS + 4, NW, stride=skip), :] = jnp.where(lane < 64, first, second)


def backward_kernel(S, recv, keep, den, push, cl3, cyt3, out, zh, zl, stage, room, sems):
    for kk in range(2):
        rows = slice(kk * HALF, (kk + 1) * HALF)
        stage[0, rows, :] = recv[pl.ds(kk, DEST, stride=ROWS), :]
        stage[1, rows, :] = recv[pl.ds(2 + kk, DEST, stride=ROWS), :]
        stage[2, rows, :] = recv[pl.ds(4, DEST, stride=ROWS), :]
    step = 128
    lane = iota((step, 128), 1)

    def slab(c, carry):
        rows = pl.ds(pl.multiple_of(c * step, step), step)
        low_s, high_s, flux = stage[0, rows, :], stage[1, rows, :], stage[2, rows, :]
        kk = jnp.where(c * step >= HALF, 1, 0)
        flux = jnp.where((lane // 64 == kk) & (lane % 64 < 16), flux, 0.0)
        high = flux.astype(BF16).astype(F32)
        flux = high + pltpu.roll(flux - high, 16, 1) + pltpu.roll(high, 32, 1)
        masked = jnp.concatenate([jnp.where(lane % 8 == m, flux, 0.0) for m in range(INNER)], axis=0)
        pushed = dot(masked.astype(BF16), push[...])
        plus, minus = low_s + high_s, low_s - high_s
        modes = []
        for m in range(INNER):
            drive = (plus if m % 2 == 0 else minus) * float(S[m, 0])
            value = keep[m, rows, :] + pushed[m * step : (m + 1) * step] + drive
            modes.append(value * den[m, rows, :])
        planes = [None] * SLAB
        planes[0] = low_s
        for i in range(1, 5):
            p_odd = sum(float(S[m, i - 1]) * modes[m] for m in range(0, INNER, 2))
            if i == 4:
                planes[4] = p_odd
                continue
            p_even = sum(float(S[m, i - 1]) * modes[m] for m in range(1, INNER, 2))
            planes[i] = p_odd + p_even
            planes[SLAB - i] = p_odd - p_even
        for z in range(SLAB):
            zh[z, rows, :], zl[z, rows, :] = split(planes[z])
        return carry

    lax.fori_loop(0, NY // step, slab, 0, unroll=UNROLL_B)

    copies = []
    for p in range(SLAB // 2):
        high = jnp.concatenate([zh[2 * p], zh[2 * p + 1]], axis=1)
        low = jnp.concatenate([zl[2 * p], zl[2 * p + 1]], axis=1)
        high, low = split(dot(jnp.concatenate([high, low, high], axis=1), cl3[...]))
        both = dot(cyt3[...], high)
        value = both[:NY] + both[NY:] + dot(cyt3[:NY, :], low)
        room[2 * p] = value[:, :XL]
        room[2 * p + 1] = value[:, XL:]
        pair = pl.ds(2 * p, 2)
        copies.append(pltpu.make_async_copy(room.at[pair], out.at[pair], sems.at[p]))
        copies[-1].start()
    for copy in copies:
        copy.wait()


def in_vmem(count):
    return [pl.BlockSpec(memory_space=pltpu.VMEM)] * count


def params(mebibytes):
    return pltpu.CompilerParams(vmem_limit_bytes=mebibytes * 1024 * 1024)


def work(microseconds):
    flops = microseconds * 1_000_000_000
    return pl.CostEstimate(flops=flops, bytes_accessed=1_000_000, transcendentals=0)


def per_device(divergence, marker_force, marker_height, marker_cell):
    t = tables()
    tab = {k: jnp.asarray(v) for k, v in t.items() if k not in ("S", "mu")}
    hbm = pl.BlockSpec(memory_space=pltpu.HBM)
    groups = NY // GROUP
    token = pl.pallas_call(
        first_kernel,
        out_shape=jax.ShapeDtypeStruct((8, 128), F32),
        out_specs=in_vmem(1)[0],
        compiler_params=params(1),
        cost_estimate=work(2),
    )()
    own, send = pl.pallas_call(
        marker_kernel,
        out_shape=(
            jax.ShapeDtypeStruct((3, groups, MARKS * GROUP), F32),
            jax.ShapeDtypeStruct((2, groups, MARKS * GROUP), F32),
        ),
        in_specs=in_vmem(1) + [hbm] * 3,
        out_specs=tuple(in_vmem(2)),
        scratch_shapes=[
            pltpu.VMEM((2, MARKS, NY), F32),
            pltpu.VMEM((MARKS, NY), jnp.int32),
            pltpu.SemaphoreType.DMA((3,)),
        ],
        compiler_params=params(4),
        cost_estimate=work(4),
    )(token, marker_force, marker_height, marker_cell)
    from_above = lax.ppermute(send, "wide", [(i + 1, i) for i in range(NW - 1)])

    plane = (NY, XL)
    zh, zl, z7 = pl.pallas_call(
        source_kernel,
        out_shape=(
            jax.ShapeDtypeStruct((SLAB, NY, XL), BF16),
            jax.ShapeDtypeStruct((SLAB, NY, XL), BF16),
            jax.ShapeDtypeStruct(plane, F32),
        ),
        in_specs=in_vmem(3),
        out_specs=tuple(in_vmem(3)),
        scratch_shapes=[pltpu.VMEM((SLAB + 1, NY, XL), F32)],
        compiler_params=params(16),
        cost_estimate=work(4),
    )(divergence, own, tab["clt3"])

    field = jax.ShapeDtypeStruct((INNER, NY, XL), F32)
    payload = jax.ShapeDtypeStruct((DEST * ROWS, XL), F32)
    sent, keep = pl.pallas_call(
        functools.partial(forward_kernel, t["S"]),
        out_shape=(payload, field),
        in_specs=in_vmem(9),
        out_specs=tuple(in_vmem(2)),
        scratch_shapes=[
            pltpu.VMEM((SLAB + 1, NY, XL), F32),
            pltpu.VMEM(plane, F32),
            pltpu.VMEM((NY, INNER * XL), BF16),
            pltpu.VMEM((NY, INNER * XL), BF16),
            pltpu.VMEM(plane, F32),
        ],
        compiler_params=params(24),
        cost_estimate=work(5),
    )(zh, zl, z7, from_above, *[tab[k] for k in ("clt1", "cy3", "den", "ends_h", "ends_l")])

    def exchange(value):
        flat = lax.all_to_all(value.reshape(-1), BOTH, 0, 0, tiled=True)
        return flat.reshape(DEST * ROWS, XL)

    names = (
        "fwd_h", "fwd_l", "inv_h", "inv_l", "into", "outof",
        "lamx_row", "lamx_tile", "sign",
    )
    returned = pl.pallas_call(
        functools.partial(middle_kernel, t["S"], t["mu"]),
        out_shape=payload,
        in_specs=in_vmem(2 + len(names)),
        out_specs=in_vmem(1)[0],
        scratch_shapes=[
            pltpu.VMEM((4 * NW, NX), F32),
            pltpu.VMEM((2 * INNER * NW, NX), F32),
            pltpu.VMEM((NW * 16, 128), F32),
            pltpu.VMEM(((NW + 1) * 16, 128), F32),
            pltpu.VMEM((NW * 16, 128), F32),
            pltpu.VMEM(((NW + 1) * 16, 128), F32),
            pltpu.VMEM((2 * NW + 8, 128), F32),
        ],
        compiler_params=params(16),
        cost_estimate=work(5),
    )(tab["lamy"], exchange(sent), *[tab[k] for k in names])

    return pl.pallas_call(
        functools.partial(backward_kernel, t["S"]),
        out_shape=jax.ShapeDtypeStruct((SLAB, NY, XL), F32),
        in_specs=in_vmem(6),
        out_specs=hbm,
        scratch_shapes=[
            pltpu.VMEM((SLAB, NY, XL), BF16),
            pltpu.VMEM((SLAB, NY, XL), BF16),
            pltpu.VMEM((3, NY, XL), F32),
            pltpu.VMEM((SLAB, NY, XL), F32),
            pltpu.SemaphoreType.DMA((SLAB // 2,)),
        ],
        compiler_params=params(24),
        cost_estimate=work(5),
    )(exchange(returned), keep, tab["den"], tab["push"], tab["cl3"], tab["cyt3"])


def solution(mesh):
    in_specs = (
        P("wide", None, "narrow"),
        P("wide", "narrow"),
        P("wide", "narrow"),
        P("wide", "narrow"),
    )
    out_specs = P("wide", None, "narrow")
    return jax.shard_map(
        per_device, mesh=mesh, in_specs=in_specs, out_specs=out_specs, check_vma=False
    )
```

```python
import functools

import jax
import jax.numpy as jnp
import ml_dtypes
import numpy as np
from jax import lax
from jax.experimental import pallas as pl
from jax.experimental.pallas import tpu as pltpu
from jax.sharding import PartitionSpec as P

BOTH = ("wide", "narrow")
NZ, NY, NX = 256, 512, 1024
NW, NN = 32, 8
SLAB = NZ // NW
XL = NX // NN
INNER = SLAB - 1
DEST = NW * NN
HALF = NY // 2
ROWS = 5
GROUP = 32
MARKS = 8
F32, BF16 = jnp.float32, jnp.bfloat16
UNROLL_A, UNROLL_B, UNROLL_C, UNROLL_H, UNROLL_X = 16, 4, 4, 16, 4


def dct_matrix(order):
    k = np.arange(order)[:, None]
    n = np.arange(order)[None, :]
    scale = np.where(k == 0, np.sqrt(1.0 / order), np.sqrt(2.0 / order))
    return scale * np.cos(np.pi * ((k * (2 * n + 1)) % (4 * order)) / (2 * order))


def lam(order):
    return 2.0 - 2.0 * np.cos(np.pi * np.arange(order) / order)


def halves(table):
    high = table.astype(np.float32).astype(ml_dtypes.bfloat16)
    low = (table - high.astype(np.float64)).astype(np.float32).astype(ml_dtypes.bfloat16)
    return high, low


@functools.lru_cache(None)
def tables():
    t = {}
    cy, cx, cl = dct_matrix(NY), dct_matrix(NX), dct_matrix(XL)
    i = np.arange(1, SLAB)
    t["S"] = np.sqrt(2.0 / SLAB) * np.sin(np.pi * np.outer(i, i) / SLAB)
    t["mu"] = 2.0 - 2.0 * np.cos(np.pi * i / SLAB)
    ch, clow = halves(cy)
    t["cy3"] = np.concatenate([ch, clow], 0)
    ch, clow = halves(cy.T)
    t["cyt3"] = np.concatenate([ch, clow], 0)
    h, l = halves(np.kron(np.eye(2), cl.T))
    t["clt3"] = np.concatenate([h, h, l], 0)
    h, l = halves(cl.T)
    t["clt1"] = np.concatenate([h, h, l], 0)
    h, l = halves(np.kron(np.eye(2), cl))
    t["cl3"] = np.concatenate([h, h, l], 0)
    t["den"] = (
        1.0 / (t["mu"][:, None, None] + lam(NY)[None, :, None] + lam(XL)[None, None, :])
    ).astype(np.float32)
    ends = np.zeros((INNER, XL, 128))
    for m in range(INNER):
        ends[m, :, m] = cl[:, 0]
        ends[m, :, 8 + m] = cl[:, -1]
    h, l = halves(ends.reshape(INNER * XL, 128))
    t["ends"] = h + np.roll(l, 16, 1)
    order = np.concatenate([np.arange(0, NX, 2), np.arange(1, NX, 2)])
    mixed = np.zeros((NX, NX))
    for n in range(NN):
        mixed[:, n * XL : (n + 1) * XL] = cx[:, n * XL : (n + 1) * XL] @ cl.T
    mixed = mixed[order]
    hw = NX // 2
    fwd = np.stack([mixed[:hw, :hw].T, mixed[hw:, :hw].T])
    t["fwd_h"], t["fwd_l"] = halves(fwd)
    inv = np.stack([mixed[:hw, :hw], mixed[hw:, :hw]])
    t["inv_h"], t["inv_l"] = halves(inv)
    lamx = lam(NX)[order]
    t["lamx_row"] = lamx.reshape(1, NX).astype(np.float32)
    t["lamx_tile"] = np.concatenate([lamx.reshape(8, 128)] * 2, 0).astype(np.float32)
    t["lamy"] = np.repeat(lam(NY)[:, None], 128, 1).astype(np.float32)
    jumps = np.stack([cx[:, XL * f + XL - 1] - cx[:, XL * f + XL] for f in range(NN - 1)])[:, order]
    into = np.zeros((NN, 2, 8, NX))
    outof = np.zeros((NN, 2, 8, NX))
    for n in range(NN):
        if n < NN - 1:
            into[n, 1] = -jumps[n]
            outof[n, 1] = jumps[n]
        if n > 0:
            into[n, 0] = jumps[n - 1]
            outof[n, 0] = jumps[n - 1]
    h, l = halves(into)
    slots = np.zeros((NN, 2, 8, NX), ml_dtypes.bfloat16)
    slots[:, :, 0], slots[:, :, 1], slots[:, :, 2] = h[:, :, 0], h[:, :, 0], l[:, :, 0]
    t["into"] = slots.reshape(128, NX)
    h, l = halves(outof)
    slots = np.zeros((NN, 2, 8, NX), ml_dtypes.bfloat16)
    slots[:, :, 0], slots[:, :, 1] = h[:, :, 0], l[:, :, 0]
    t["outof"] = np.ascontiguousarray(slots.reshape(128, NX).T)
    h, l = halves(np.stack([cl[:, 0], -cl[:, -1]]))
    push = np.zeros((2, 4, 2, 8, XL), ml_dtypes.bfloat16)
    push[:, 0], push[:, 1], push[:, 2] = h[None, :, None], h[None, :, None], l[None, :, None]
    t["push"] = push.reshape(128, XL)
    sign = np.where(np.arange(XL) % 2 == 0, 1.0, -1.0).reshape(1, XL)
    t["sign"] = sign.astype(np.float32)
    return t


def split(value):
    high = value.astype(BF16)
    return high, (value - high.astype(F32)).astype(BF16)


def dot(left, right):
    return lax.dot_general(left, right, (((1,), (0,)), ((), ())), preferred_element_type=F32)


def dot_nt(left, right):
    return lax.dot_general(left, right, (((1,), (1,)), ((), ())), preferred_element_type=F32)


def triple(value):
    high, low = split(value)
    return jnp.concatenate([high, low, high], axis=1)


def iota(shape, axis):
    return lax.broadcasted_iota(jnp.int32, shape, axis)


def regroup(value):
    lane, sub = iota((MARKS, 128), 1), iota((MARKS, 128), 0)
    mine = lane // GROUP == sub % 4
    rows = []
    for block in range(NY // 128):
        part = value[:, block * 128 : (block + 1) * 128]
        turns = [part] + [pltpu.roll(part, GROUP * i, 1) for i in range(1, 4)]
        for g in range(128 // GROUP):
            turned = jnp.zeros((MARKS, 128), F32)
            for q in range(4):
                turned = jnp.where(mine & (sub % 4 == q), turns[(q - g) % 4], turned)
            low = jnp.sum(turned[:4], axis=0, keepdims=True)
            high = jnp.sum(turned[4:], axis=0, keepdims=True)
            rows.append(jnp.concatenate([low, high], axis=1))
    return jnp.concatenate(rows, axis=0)


def first_kernel(token):
    token[...] = jnp.zeros((8, 128), F32)


def marker_kernel(token, force, height, cell, own, send, pair, ids, sems):
    copies = [
        pltpu.make_async_copy(force, pair.at[0], sems.at[0]),
        pltpu.make_async_copy(height, pair.at[1], sems.at[1]),
        pltpu.make_async_copy(cell, ids, sems.at[2]),
    ]
    for copy in copies:
        copy.start()
    for copy in copies:
        copy.wait()
    forces, heights = regroup(pair[0]), regroup(pair[1])
    cells = regroup(ids[...].astype(F32))
    own[0], own[1], own[2] = forces, heights, cells
    send[0] = forces * jnp.maximum(0.0, 1.0 - jnp.abs(-0.5 - heights))
    send[1] = cells + token[0:1, 0:1]


def onehot(cells):
    cell_ids = iota((XL, 256), 0).astype(F32)
    return jnp.where(cells == cell_ids, 1.0, 0.0).astype(BF16)


def spread_rows(weights):
    spot = iota((GROUP, 256), 1) % GROUP == iota((GROUP, 256), 0)
    high = weights.astype(BF16).astype(F32)
    low = weights - high
    parts = []
    for value in (high, low):
        for j in range(weights.shape[0]):
            parts.append(jnp.where(spot, value[j : j + 1], 0.0).astype(BF16))
    return jnp.concatenate(parts, axis=0)


def source_kernel(div, own, clt3, zh, zl, z7, spread):
    centers = iota((16, 256), 0).astype(F32) + 0.5

    def markers(g, carry):
        force, height, cells = (own[i, pl.ds(g, 1), :] for i in range(3))
        weights = force * jnp.maximum(0.0, 1.0 - jnp.abs(centers - height))
        value = dot_nt(spread_rows(weights[: SLAB + 1]), onehot(cells))
        value = value[: (SLAB + 1) * GROUP] + value[(SLAB + 1) * GROUP :]
        rows = pl.ds(pl.multiple_of(g * GROUP, GROUP), GROUP)
        for z in range(SLAB + 1):
            spread[z, rows, :] = value[z * GROUP : (z + 1) * GROUP]
        return carry

    lax.fori_loop(0, NY // GROUP, markers, 0, unroll=UNROLL_A)

    def along_x(p, carry):
        other = jnp.where(p == 3, SLAB, 2 * p + 1)
        right = spread[other] + jnp.where(p == 3, 0.0, div[2 * p + 1])
        left = spread[2 * p] + div[2 * p]
        high, low = split(dot(triple(jnp.concatenate([left, right], axis=1)), clt3[...]))
        zh[2 * p], zh[2 * p + 1] = high[:, :XL], high[:, XL:]
        zl[2 * p], zl[2 * p + 1] = low[:, :XL], low[:, XL:]
        return carry

    lax.fori_loop(0, SLAB // 2, along_x, 0, unroll=UNROLL_X)
    z7[...] = spread[SLAB - 1] + div[SLAB - 1]


def forward_kernel(
    S, zh, zl, z7, marks, clt1, cy3, den, ends, pay, keep, freq, faces, uh, ul, halo
):
    def outside(g, carry):
        value = dot_nt(spread_rows(marks[0, pl.ds(g, 1), :]), onehot(marks[1, pl.ds(g, 1), :]))
        rows = pl.ds(pl.multiple_of(g * GROUP, GROUP), GROUP)
        halo[rows, :] = value[:GROUP] + value[GROUP:]
        return carry

    lax.fori_loop(0, NY // GROUP, outside, 0, unroll=UNROLL_H)
    seventh = dot(triple(z7[...] + halo[...]), clt1[...])

    def along_y(high, low):
        both = dot(cy3[...], high)
        return both[:NY] + both[NY:] + dot(cy3[:NY, :], low)

    freq[7] = along_y(*split(seventh))

    def pair(p, carry):
        value = along_y(
            jnp.concatenate([zh[2 * p], zh[2 * p + 1]], axis=1),
            jnp.concatenate([zl[2 * p], zl[2 * p + 1]], axis=1),
        )
        freq[2 * p] = value[:, :XL]
        freq[jnp.where(p == 3, 8, 2 * p + 1)] = value[:, XL:]
        return carry

    lax.fori_loop(0, SLAB // 2, pair, 0, unroll=2)
    step = 16

    def slab(c, carry):
        rows = pl.ds(pl.multiple_of(c * step, step), step)
        f = [freq[z, rows, :] for z in range(SLAB + 1)]
        even = [f[i] + f[SLAB - i] for i in range(1, 4)] + [f[4]]
        odd = [f[i] - f[SLAB - i] for i in range(1, 4)]
        p_odd = p_even = None
        for m in range(INNER):
            if m % 2 == 0:
                hat = sum(float(S[m, i]) * even[i] for i in range(4))
            else:
                hat = sum(float(S[m, i]) * odd[i] for i in range(3))
            keep[m, rows, :] = hat
            value = hat * den[m, rows, :]
            cols = slice(m * XL, (m + 1) * XL)
            uh[rows, cols], ul[rows, cols] = split(value)
            part = float(S[m, 0]) * value
            if m % 2 == 0:
                p_odd = part if p_odd is None else p_odd + part
            else:
                p_even = part if p_even is None else p_even + part
        freq[0, rows, :] = f[0] + p_odd + p_even
        freq[1, rows, :] = p_odd - p_even + f[SLAB]
        return carry

    lax.fori_loop(0, NY // step, slab, 0, unroll=8)
    high = dot(uh[...], ends[...])
    faces[...] = high + dot(ul[...], ends[...]) + pltpu.roll(high, 112, 1)
    for kk in range(2):
        rows = slice(kk * HALF, (kk + 1) * HALF)
        pay[pl.ds(kk, DEST, stride=ROWS), :] = freq[0, rows, :]
        pay[pl.ds(2 + kk, DEST, stride=ROWS), :] = freq[1, rows, :]
    pay[pl.ds(4, DEST, stride=ROWS), :] = faces[:HALF, :] + pltpu.roll(faces[HALF:, :], 64, 1)


def middle_kernel(
    S, mu, lamy, recv, fwd_h, fwd_l, inv_h, inv_l, into, outof,
    lamx_row, lamx_tile, sign, pay, grid, corr, tops, bots, piv, sol, shift,
):
    lane = iota((NW, 128), 1)
    here = lax.axis_index("wide") * NN + lax.axis_index("narrow")
    lam_k = [lamy[pl.ds(kk * HALF + here, 1), :] for kk in range(2)]
    lam_wide = [jnp.concatenate([row] * (NX // 128), axis=1) for row in lam_k]
    skip = NN * ROWS

    def load(n, r):
        return recv[pl.ds(n * ROWS + r, NW, stride=skip), :]

    sums, diffs = [], []
    for n in range(NN // 2):
        near = jnp.concatenate([load(n, r) for r in range(4)], axis=0)
        far = jnp.concatenate([load(NN - 1 - n, r) for r in range(4)], axis=0) * sign[...]
        sums.append(near + far)
        diffs.append(near - far)
    for part, pieces in ((0, sums), (1, diffs)):
        high, low = split(jnp.concatenate(pieces, axis=1))
        both = dot(jnp.concatenate([high, low], axis=0), fwd_h[part])
        value = both[: 4 * NW] + both[4 * NW :] + dot(high, fwd_l[part])
        grid[:, part * 512 : (part + 1) * 512] = value

    packs = []
    for kk in range(2):
        pack = jnp.zeros((NW, 128), F32)
        for n in range(NN):
            turned = load(n, 4)
            shift_by = (16 * n + 64 * kk) % 128
            if shift_by:
                turned = pltpu.roll(turned, shift_by, 1)
            pack = jnp.where(lane // 16 == n, turned, pack)
        packs.append(pack)
    pairs = [(kk, m) for kk in range(2) for m in range(INNER)]
    masked = []
    for kk, m in pairs:
        high = packs[kk].astype(BF16).astype(F32)
        slots = jnp.zeros((NW, 128), F32)
        for slot, value in enumerate((high, packs[kk] - high, high)):
            turned = pltpu.roll(value, (slot - m) % 128, 1) if slot != m else value
            slots = jnp.where(lane % 8 == slot, turned, slots)
        masked.append(slots.astype(BF16))
    masked = jnp.concatenate(masked, axis=0)
    count = len(pairs) * NW

    mode_id = iota((8, NX), 0)
    mu_col = jnp.zeros((8, NX), F32)
    for m in range(8):
        mu_col = jnp.where(mode_id == m, float(mu[min(m, INNER - 1)]), mu_col)
    dens = [1.0 / (mu_col + (lam_wide[kk] + lamx_row[...])) for kk in range(2)]

    for part in range(4):
        cols = slice(part * 256, (part + 1) * 256)
        value = dot(masked, into[:, cols])
        for kk in range(2):
            p_odd = p_even = None
            for m in range(INNER):
                at = (kk * INNER + m) * NW
                piece = value[at : at + NW] * dens[kk][m : m + 1, cols]
                corr[at : at + NW, cols] = piece
                piece = float(S[m, 0]) * piece
                if m % 2 == 0:
                    p_odd = piece if p_odd is None else p_odd + piece
                else:
                    p_even = piece if p_even is None else p_even + piece
            top = slice(kk * NW, (kk + 1) * NW)
            bot = slice((2 + kk) * NW, (3 + kk) * NW)
            grid[top, cols] = grid[top, cols] + p_odd + p_even
            grid[bot, cols] = grid[bot, cols] + p_odd - p_even

    bots[0:16, :] = jnp.zeros((16, 128), F32)
    for kk in range(2):
        for jb in range(8):
            cols = slice(jb * 128, (jb + 1) * 128)
            tops[pl.ds(kk * 8 + jb, NW, stride=16), :] = grid[kk * NW : (kk + 1) * NW, cols]
            bots[pl.ds(16 + kk * 8 + jb, NW, stride=16), :] = grid[
                (2 + kk) * NW : (3 + kk) * NW, cols
            ]

    row16 = iota((16, 128), 0)
    diag = 2.0 + jnp.where(row16 < 8, lam_k[0], lam_k[1]) + lamx_tile[...]
    older, newer = jnp.ones((16, 128), F32), diag
    for _ in range(INNER - 2):
        older, newer = newer, diag * newer - older
    last = diag * newer - older
    near_one = newer / last
    far_one = 1.0 / last
    full = diag - 2.0 * near_one
    inverse = 1.0 / (diag - near_one)
    value = tops[0:16, :]
    piv[0:16, :] = inverse
    sol[0:16, :] = value
    for w in range(1, NW):
        at = slice(w * 16, (w + 1) * 16)
        ratio = far_one * inverse
        value = tops[at, :] + bots[at, :] + ratio * value
        inverse = 1.0 / (full - far_one * ratio)
        piv[at, :] = inverse
        sol[at, :] = value
    later = jnp.zeros((16, 128), F32)
    sol[NW * 16 : (NW + 1) * 16, :] = later
    for w in range(NW - 1, -1, -1):
        at = slice(w * 16, (w + 1) * 16)
        later = (sol[at, :] + far_one * later) * piv[at, :]
        sol[at, :] = later

    for kk in range(2):
        for jb in range(8):
            cols = slice(jb * 128, (jb + 1) * 128)
            grid[kk * NW : (kk + 1) * NW, cols] = sol[pl.ds(kk * 8 + jb, NW, stride=16), :]
            grid[(2 + kk) * NW : (3 + kk) * NW, cols] = sol[
                pl.ds(16 + kk * 8 + jb, NW, stride=16), :
            ]

    flux = jnp.zeros((2 * count, 128), F32)
    for part in range(4):
        cols = slice(part * 256, (part + 1) * 256)
        pieces = []
        for kk in range(2):
            low_s = grid[kk * NW : (kk + 1) * NW, cols]
            high_s = grid[(2 + kk) * NW : (3 + kk) * NW, cols]
            plus, minus = low_s + high_s, low_s - high_s
            for m in range(INNER):
                at = (kk * INNER + m) * NW
                drive = (plus if m % 2 == 0 else minus) * float(S[m, 0])
                pieces.append(corr[at : at + NW, cols] + dens[kk][m : m + 1, cols] * drive)
        high, low = split(jnp.concatenate(pieces, axis=0))
        flux = flux + dot(jnp.concatenate([high, low], axis=0), outof[cols, :])
    fluxes = []
    side = (lane // 8) % 2
    for kk in range(2):
        total = jnp.zeros((NW, 128), F32)
        for m in range(INNER):
            at = (kk * INNER + m) * NW
            both, main = flux[at : at + NW], flux[count + at : count + at + NW]
            main = both + main
            main = pltpu.roll(main, m, 1) if m > 0 else main
            rest = pltpu.roll(both, (m - 1) % 128, 1) if m != 1 else both
            total = jnp.where(lane % 8 == m, main + rest, total)
        pack = packs[kk]
        to_right = jnp.where(lane < 120, pack - pltpu.roll(pack, 120, 1), 0.0)
        to_left = jnp.where(lane >= 16, pltpu.roll(pack, 8, 1) - pack, 0.0)
        fluxes.append(total + jnp.where(side == 1, to_right, to_left))

    locals_ = []
    for part in range(2):
        high, low = split(grid[: 2 * NW, part * 512 : (part + 1) * 512])
        both = dot(jnp.concatenate([high, low], axis=0), inv_h[part])
        locals_.append(both[: 2 * NW] + both[2 * NW :] + dot(high, inv_l[part]))
    shift[2 * NW :, :] = jnp.zeros((8, 128), F32)
    for n in range(NN):
        block = n if n < NN // 2 else NN - 1 - n
        cols = slice(block * 128, (block + 1) * 128)
        if n < NN // 2:
            value = locals_[0][:, cols] + locals_[1][:, cols]
        else:
            value = (locals_[0][:, cols] - locals_[1][:, cols]) * sign[...]
        shift[: 2 * NW, :] = value
        for kk in range(2):
            pay[pl.ds(n * ROWS + kk, NW, stride=skip), :] = value[kk * NW : (kk + 1) * NW]
            after = shift[kk * NW + 1 : (kk + 1) * NW + 1, :]
            after = jnp.where(iota((NW, 128), 0) == NW - 1, 0.0, after)
            pay[pl.ds(n * ROWS + 2 + kk, NW, stride=skip), :] = after
        first = fluxes[0] if n == 0 else pltpu.roll(fluxes[0], 128 - 16 * n, 1)
        back = (64 - 16 * n) % 128
        second = fluxes[1] if back == 0 else pltpu.roll(fluxes[1], back, 1)
        pay[pl.ds(n * ROWS + 4, NW, stride=skip), :] = jnp.where(lane < 64, first, second)


def backward_kernel(S, recv, keep, den, push, cl3, cyt3, out, zh, zl, stage, room, sems):
    for kk in range(2):
        rows = slice(kk * HALF, (kk + 1) * HALF)
        stage[0, rows, :] = recv[pl.ds(kk, DEST, stride=ROWS), :]
        stage[1, rows, :] = recv[pl.ds(2 + kk, DEST, stride=ROWS), :]
        stage[2, rows, :] = recv[pl.ds(4, DEST, stride=ROWS), :]
    step = 128
    lane = iota((step, 128), 1)

    def slab(c, carry):
        rows = pl.ds(pl.multiple_of(c * step, step), step)
        low_s, high_s, flux = stage[0, rows, :], stage[1, rows, :], stage[2, rows, :]
        kk = jnp.where(c * step >= HALF, 1, 0)
        flux = jnp.where((lane // 64 == kk) & (lane % 64 < 16), flux, 0.0)
        high = flux.astype(BF16).astype(F32)
        flux = high + pltpu.roll(flux - high, 16, 1) + pltpu.roll(high, 32, 1)
        masked = jnp.concatenate([jnp.where(lane % 8 == m, flux, 0.0) for m in range(INNER)], axis=0)
        pushed = dot(masked.astype(BF16), push[...])
        plus, minus = low_s + high_s, low_s - high_s
        modes = []
        for m in range(INNER):
            drive = (plus if m % 2 == 0 else minus) * float(S[m, 0])
            value = keep[m, rows, :] + pushed[m * step : (m + 1) * step] + drive
            modes.append(value * den[m, rows, :])
        planes = [None] * SLAB
        planes[0] = low_s
        for i in range(1, 5):
            p_odd = sum(float(S[m, i - 1]) * modes[m] for m in range(0, INNER, 2))
            if i == 4:
                planes[4] = p_odd
                continue
            p_even = sum(float(S[m, i - 1]) * modes[m] for m in range(1, INNER, 2))
            planes[i] = p_odd + p_even
            planes[SLAB - i] = p_odd - p_even
        for z in range(SLAB):
            zh[z, rows, :], zl[z, rows, :] = split(planes[z])
        return carry

    lax.fori_loop(0, NY // step, slab, 0, unroll=UNROLL_B)

    copies = []
    for p in range(SLAB // 2):
        high = jnp.concatenate([zh[2 * p], zh[2 * p + 1]], axis=1)
        low = jnp.concatenate([zl[2 * p], zl[2 * p + 1]], axis=1)
        high, low = split(dot(jnp.concatenate([high, low, high], axis=1), cl3[...]))
        both = dot(cyt3[...], high)
        value = both[:NY] + both[NY:] + dot(cyt3[:NY, :], low)
        room[2 * p] = value[:, :XL]
        room[2 * p + 1] = value[:, XL:]
        pair = pl.ds(2 * p, 2)
        copies.append(pltpu.make_async_copy(room.at[pair], out.at[pair], sems.at[p]))
        copies[-1].start()
    for copy in copies:
        copy.wait()


def in_vmem(count):
    return [pl.BlockSpec(memory_space=pltpu.VMEM)] * count


def params(mebibytes):
    return pltpu.CompilerParams(vmem_limit_bytes=mebibytes * 1024 * 1024)


def work(microseconds):
    flops = microseconds * 1_000_000_000
    return pl.CostEstimate(flops=flops, bytes_accessed=1_000_000, transcendentals=0)


def per_device(divergence, marker_force, marker_height, marker_cell):
    t = tables()
    tab = {k: jnp.asarray(v) for k, v in t.items() if k not in ("S", "mu")}
    hbm = pl.BlockSpec(memory_space=pltpu.HBM)
    groups = NY // GROUP
    token = pl.pallas_call(
        first_kernel,
        out_shape=jax.ShapeDtypeStruct((8, 128), F32),
        out_specs=in_vmem(1)[0],
        compiler_params=params(1),
        cost_estimate=work(2),
    )()
    own, send = pl.pallas_call(
        marker_kernel,
        out_shape=(
            jax.ShapeDtypeStruct((3, groups, MARKS * GROUP), F32),
            jax.ShapeDtypeStruct((2, groups, MARKS * GROUP), F32),
        ),
        in_specs=in_vmem(1) + [hbm] * 3,
        out_specs=tuple(in_vmem(2)),
        scratch_shapes=[
            pltpu.VMEM((2, MARKS, NY), F32),
            pltpu.VMEM((MARKS, NY), jnp.int32),
            pltpu.SemaphoreType.DMA((3,)),
        ],
        compiler_params=params(4),
        cost_estimate=work(4),
    )(token, marker_force, marker_height, marker_cell)
    from_above = lax.ppermute(send, "wide", [(i + 1, i) for i in range(NW - 1)])

    plane = (NY, XL)
    zh, zl, z7 = pl.pallas_call(
        source_kernel,
        out_shape=(
            jax.ShapeDtypeStruct((SLAB, NY, XL), BF16),
            jax.ShapeDtypeStruct((SLAB, NY, XL), BF16),
            jax.ShapeDtypeStruct(plane, F32),
        ),
        in_specs=in_vmem(3),
        out_specs=tuple(in_vmem(3)),
        scratch_shapes=[pltpu.VMEM((SLAB + 1, NY, XL), F32)],
        compiler_params=params(16),
        cost_estimate=work(4),
    )(divergence, own, tab["clt3"])

    field = jax.ShapeDtypeStruct((INNER, NY, XL), F32)
    payload = jax.ShapeDtypeStruct((DEST * ROWS, XL), F32)
    sent, keep = pl.pallas_call(
        functools.partial(forward_kernel, t["S"]),
        out_shape=(payload, field),
        in_specs=in_vmem(8),
        out_specs=tuple(in_vmem(2)),
        scratch_shapes=[
            pltpu.VMEM((SLAB + 1, NY, XL), F32),
            pltpu.VMEM(plane, F32),
            pltpu.VMEM((NY, INNER * XL), BF16),
            pltpu.VMEM((NY, INNER * XL), BF16),
            pltpu.VMEM(plane, F32),
        ],
        compiler_params=params(24),
        cost_estimate=work(5),
    )(zh, zl, z7, from_above, *[tab[k] for k in ("clt1", "cy3", "den", "ends")])

    def exchange(value):
        flat = lax.all_to_all(value.reshape(-1), BOTH, 0, 0, tiled=True)
        return flat.reshape(DEST * ROWS, XL)

    names = (
        "fwd_h", "fwd_l", "inv_h", "inv_l", "into", "outof",
        "lamx_row", "lamx_tile", "sign",
    )
    returned = pl.pallas_call(
        functools.partial(middle_kernel, t["S"], t["mu"]),
        out_shape=payload,
        in_specs=in_vmem(2 + len(names)),
        out_specs=in_vmem(1)[0],
        scratch_shapes=[
            pltpu.VMEM((4 * NW, NX), F32),
            pltpu.VMEM((2 * INNER * NW, NX), F32),
            pltpu.VMEM((NW * 16, 128), F32),
            pltpu.VMEM(((NW + 1) * 16, 128), F32),
            pltpu.VMEM((NW * 16, 128), F32),
            pltpu.VMEM(((NW + 1) * 16, 128), F32),
            pltpu.VMEM((2 * NW + 8, 128), F32),
        ],
        compiler_params=params(16),
        cost_estimate=work(5),
    )(tab["lamy"], exchange(sent), *[tab[k] for k in names])

    return pl.pallas_call(
        functools.partial(backward_kernel, t["S"]),
        out_shape=jax.ShapeDtypeStruct((SLAB, NY, XL), F32),
        in_specs=in_vmem(6),
        out_specs=hbm,
        scratch_shapes=[
            pltpu.VMEM((SLAB, NY, XL), BF16),
            pltpu.VMEM((SLAB, NY, XL), BF16),
            pltpu.VMEM((3, NY, XL), F32),
            pltpu.VMEM((SLAB, NY, XL), F32),
            pltpu.SemaphoreType.DMA((SLAB // 2,)),
        ],
        compiler_params=params(24),
        cost_estimate=work(5),
    )(exchange(returned), keep, tab["den"], tab["push"], tab["cl3"], tab["cyt3"])


def solution(mesh):
    in_specs = (
        P("wide", None, "narrow"),
        P("wide", "narrow"),
        P("wide", "narrow"),
        P("wide", "narrow"),
    )
    out_specs = P("wide", None, "narrow")
    return jax.shard_map(
        per_device, mesh=mesh, in_specs=in_specs, out_specs=out_specs, check_vma=False
    )
```

```python
import functools

import jax
import jax.numpy as jnp
import ml_dtypes
import numpy as np
from jax import lax
from jax.experimental import pallas as pl
from jax.experimental.pallas import tpu as pltpu
from jax.sharding import PartitionSpec as P

BOTH = ("wide", "narrow")
NZ, NY, NX = 256, 512, 1024
NW, NN = 32, 8
SLAB = NZ // NW
XL = NX // NN
INNER = SLAB - 1
DEST = NW * NN
HALF = NY // 2
ROWS = 5
GROUP = 32
MARKS = 8
F32, BF16 = jnp.float32, jnp.bfloat16
UNROLL_A, UNROLL_B, UNROLL_C, UNROLL_H, UNROLL_X = 16, 4, 4, 16, 4


def dct_matrix(order):
    k = np.arange(order)[:, None]
    n = np.arange(order)[None, :]
    scale = np.where(k == 0, np.sqrt(1.0 / order), np.sqrt(2.0 / order))
    return scale * np.cos(np.pi * ((k * (2 * n + 1)) % (4 * order)) / (2 * order))


def lam(order):
    return 2.0 - 2.0 * np.cos(np.pi * np.arange(order) / order)


def halves(table):
    high = table.astype(np.float32).astype(ml_dtypes.bfloat16)
    low = (table - high.astype(np.float64)).astype(np.float32).astype(ml_dtypes.bfloat16)
    return high, low


@functools.lru_cache(None)
def tables():
    t = {}
    cy, cx, cl = dct_matrix(NY), dct_matrix(NX), dct_matrix(XL)
    i = np.arange(1, SLAB)
    t["S"] = np.sqrt(2.0 / SLAB) * np.sin(np.pi * np.outer(i, i) / SLAB)
    t["mu"] = 2.0 - 2.0 * np.cos(np.pi * i / SLAB)
    ch, clow = halves(cy)
    t["cy3"] = np.concatenate([ch, clow], 0)
    ch, clow = halves(cy.T)
    t["cyt3"] = np.concatenate([ch, clow], 0)
    h, l = halves(np.kron(np.eye(2), cl.T))
    t["clt3"] = np.concatenate([h, h, l], 0)
    h, l = halves(cl.T)
    t["clt1"] = np.concatenate([h, h, l], 0)
    h, l = halves(np.kron(np.eye(2), cl))
    t["cl3"] = np.concatenate([h, h, l], 0)
    t["den"] = (
        1.0 / (t["mu"][:, None, None] + lam(NY)[None, :, None] + lam(XL)[None, None, :])
    ).astype(np.float32)
    ends = np.zeros((INNER, XL, 128))
    for m in range(INNER):
        ends[m, :, m] = cl[:, 0]
        ends[m, :, 8 + m] = cl[:, -1]
    h, l = halves(ends.reshape(INNER * XL, 128))
    t["ends"] = h + np.roll(l, 16, 1)
    order = np.concatenate([np.arange(0, NX, 2), np.arange(1, NX, 2)])
    mixed = np.zeros((NX, NX))
    for n in range(NN):
        mixed[:, n * XL : (n + 1) * XL] = cx[:, n * XL : (n + 1) * XL] @ cl.T
    mixed = mixed[order]
    hw = NX // 2
    fwd = np.stack([mixed[:hw, :hw].T, mixed[hw:, :hw].T])
    t["fwd_h"], t["fwd_l"] = halves(fwd)
    inv = np.stack([mixed[:hw, :hw], mixed[hw:, :hw]])
    t["inv_h"], t["inv_l"] = halves(inv)
    lamx = lam(NX)[order]
    t["lamx_row"] = lamx.reshape(1, NX).astype(np.float32)
    t["lamx_tile"] = np.concatenate([lamx.reshape(8, 128)] * 2, 0).astype(np.float32)
    t["lamy"] = np.repeat(lam(NY)[:, None], 128, 1).astype(np.float32)
    jumps = np.stack([cx[:, XL * f + XL - 1] - cx[:, XL * f + XL] for f in range(NN - 1)])[:, order]
    into = np.zeros((NN, 2, 8, NX))
    outof = np.zeros((NN, 2, 8, NX))
    for n in range(NN):
        if n < NN - 1:
            into[n, 1] = -jumps[n]
            outof[n, 1] = jumps[n]
        if n > 0:
            into[n, 0] = jumps[n - 1]
            outof[n, 0] = jumps[n - 1]
    h, l = halves(into)
    slots = np.zeros((NN, 2, 8, NX), ml_dtypes.bfloat16)
    slots[:, :, 0], slots[:, :, 1], slots[:, :, 2] = h[:, :, 0], h[:, :, 0], l[:, :, 0]
    t["into"] = slots.reshape(128, NX)
    h, l = halves(outof)
    slots = np.zeros((NN, 2, 8, NX), ml_dtypes.bfloat16)
    slots[:, :, 0], slots[:, :, 1] = h[:, :, 0], l[:, :, 0]
    t["outof"] = np.ascontiguousarray(slots.reshape(128, NX).T)
    h, l = halves(np.stack([cl[:, 0], -cl[:, -1]]))
    push = np.zeros((2, 4, 2, 8, XL), ml_dtypes.bfloat16)
    push[:, 0], push[:, 1], push[:, 2] = h[None, :, None], h[None, :, None], l[None, :, None]
    t["push"] = push.reshape(128, XL)
    sign = np.where(np.arange(XL) % 2 == 0, 1.0, -1.0).reshape(1, XL)
    t["sign"] = sign.astype(np.float32)
    return t


def split(value):
    high = value.astype(BF16)
    return high, (value - high.astype(F32)).astype(BF16)


def dot(left, right):
    return lax.dot_general(left, right, (((1,), (0,)), ((), ())), preferred_element_type=F32)


def dot_nt(left, right):
    return lax.dot_general(left, right, (((1,), (1,)), ((), ())), preferred_element_type=F32)


def triple(value):
    high, low = split(value)
    return jnp.concatenate([high, low, high], axis=1)


def iota(shape, axis):
    return lax.broadcasted_iota(jnp.int32, shape, axis)


def regroup(value):
    lane, sub = iota((MARKS, 128), 1), iota((MARKS, 128), 0)
    mine = lane // GROUP == sub % 4
    rows = []
    for block in range(NY // 128):
        part = value[:, block * 128 : (block + 1) * 128]
        turns = [part] + [pltpu.roll(part, GROUP * i, 1) for i in range(1, 4)]
        for g in range(128 // GROUP):
            turned = jnp.zeros((MARKS, 128), F32)
            for q in range(4):
                turned = jnp.where(mine & (sub % 4 == q), turns[(q - g) % 4], turned)
            low = jnp.sum(turned[:4], axis=0, keepdims=True)
            high = jnp.sum(turned[4:], axis=0, keepdims=True)
            rows.append(jnp.concatenate([low, high], axis=1))
    return jnp.concatenate(rows, axis=0)


def first_kernel(token):
    token[...] = jnp.zeros((8, 128), F32)


def marker_kernel(token, force, height, cell, own, send):
    forces, heights = regroup(force[...]), regroup(height[...])
    cells = regroup(cell[...].astype(F32))
    own[0], own[1], own[2] = forces, heights, cells
    send[0] = forces * jnp.maximum(0.0, 1.0 - jnp.abs(-0.5 - heights))
    send[1] = cells + token[0:1, 0:1]


def onehot(cells):
    cell_ids = iota((XL, 256), 0).astype(F32)
    return jnp.where(cells == cell_ids, 1.0, 0.0).astype(BF16)


def spread_rows(weights):
    spot = iota((GROUP, 256), 1) % GROUP == iota((GROUP, 256), 0)
    high = weights.astype(BF16).astype(F32)
    low = weights - high
    parts = []
    for value in (high, low):
        for j in range(weights.shape[0]):
            parts.append(jnp.where(spot, value[j : j + 1], 0.0).astype(BF16))
    return jnp.concatenate(parts, axis=0)


def source_kernel(div, own, clt3, zh, zl, z7, spread):
    centers = iota((16, 256), 0).astype(F32) + 0.5

    def markers(g, carry):
        force, height, cells = (own[i, pl.ds(g, 1), :] for i in range(3))
        weights = force * jnp.maximum(0.0, 1.0 - jnp.abs(centers - height))
        value = dot_nt(spread_rows(weights[: SLAB + 1]), onehot(cells))
        value = value[: (SLAB + 1) * GROUP] + value[(SLAB + 1) * GROUP :]
        rows = pl.ds(pl.multiple_of(g * GROUP, GROUP), GROUP)
        for z in range(SLAB + 1):
            spread[z, rows, :] = value[z * GROUP : (z + 1) * GROUP]
        return carry

    lax.fori_loop(0, NY // GROUP, markers, 0, unroll=UNROLL_A)

    def along_x(p, carry):
        other = jnp.where(p == 3, SLAB, 2 * p + 1)
        right = spread[other] + jnp.where(p == 3, 0.0, div[2 * p + 1])
        left = spread[2 * p] + div[2 * p]
        high, low = split(dot(triple(jnp.concatenate([left, right], axis=1)), clt3[...]))
        zh[2 * p], zh[2 * p + 1] = high[:, :XL], high[:, XL:]
        zl[2 * p], zl[2 * p + 1] = low[:, :XL], low[:, XL:]
        return carry

    lax.fori_loop(0, SLAB // 2, along_x, 0, unroll=UNROLL_X)
    z7[...] = spread[SLAB - 1] + div[SLAB - 1]


def forward_kernel(
    S, zh, zl, z7, marks, clt1, cy3, den, ends, pay, keep, freq, faces, uh, ul, halo
):
    def outside(g, carry):
        value = dot_nt(spread_rows(marks[0, pl.ds(g, 1), :]), onehot(marks[1, pl.ds(g, 1), :]))
        rows = pl.ds(pl.multiple_of(g * GROUP, GROUP), GROUP)
        halo[rows, :] = value[:GROUP] + value[GROUP:]
        return carry

    lax.fori_loop(0, NY // GROUP, outside, 0, unroll=UNROLL_H)
    seventh = dot(triple(z7[...] + halo[...]), clt1[...])

    def along_y(high, low):
        both = dot(cy3[...], high)
        return both[:NY] + both[NY:] + dot(cy3[:NY, :], low)

    freq[7] = along_y(*split(seventh))

    def pair(p, carry):
        value = along_y(
            jnp.concatenate([zh[2 * p], zh[2 * p + 1]], axis=1),
            jnp.concatenate([zl[2 * p], zl[2 * p + 1]], axis=1),
        )
        freq[2 * p] = value[:, :XL]
        freq[jnp.where(p == 3, 8, 2 * p + 1)] = value[:, XL:]
        return carry

    lax.fori_loop(0, SLAB // 2, pair, 0, unroll=2)
    step = 16

    def slab(c, carry):
        rows = pl.ds(pl.multiple_of(c * step, step), step)
        f = [freq[z, rows, :] for z in range(SLAB + 1)]
        even = [f[i] + f[SLAB - i] for i in range(1, 4)] + [f[4]]
        odd = [f[i] - f[SLAB - i] for i in range(1, 4)]
        p_odd = p_even = None
        for m in range(INNER):
            if m % 2 == 0:
                hat = sum(float(S[m, i]) * even[i] for i in range(4))
            else:
                hat = sum(float(S[m, i]) * odd[i] for i in range(3))
            keep[m, rows, :] = hat
            value = hat * den[m, rows, :]
            cols = slice(m * XL, (m + 1) * XL)
            uh[rows, cols], ul[rows, cols] = split(value)
            part = float(S[m, 0]) * value
            if m % 2 == 0:
                p_odd = part if p_odd is None else p_odd + part
            else:
                p_even = part if p_even is None else p_even + part
        freq[0, rows, :] = f[0] + p_odd + p_even
        freq[1, rows, :] = p_odd - p_even + f[SLAB]
        return carry

    lax.fori_loop(0, NY // step, slab, 0, unroll=8)
    high = dot(uh[...], ends[...])
    faces[...] = high + dot(ul[...], ends[...]) + pltpu.roll(high, 112, 1)
    for kk in range(2):
        rows = slice(kk * HALF, (kk + 1) * HALF)
        pay[pl.ds(kk, DEST, stride=ROWS), :] = freq[0, rows, :]
        pay[pl.ds(2 + kk, DEST, stride=ROWS), :] = freq[1, rows, :]
    pay[pl.ds(4, DEST, stride=ROWS), :] = faces[:HALF, :] + pltpu.roll(faces[HALF:, :], 64, 1)


def middle_kernel(
    S, mu, lamy, recv, fwd_h, fwd_l, inv_h, inv_l, into, outof,
    lamx_row, lamx_tile, sign, pay, grid, corr, tops, bots, piv, sol, shift,
):
    lane = iota((NW, 128), 1)
    here = lax.axis_index("wide") * NN + lax.axis_index("narrow")
    lam_k = [lamy[pl.ds(kk * HALF + here, 1), :] for kk in range(2)]
    lam_wide = [jnp.concatenate([row] * (NX // 128), axis=1) for row in lam_k]
    skip = NN * ROWS

    def load(n, r):
        return recv[pl.ds(n * ROWS + r, NW, stride=skip), :]

    sums, diffs = [], []
    for n in range(NN // 2):
        near = jnp.concatenate([load(n, r) for r in range(4)], axis=0)
        far = jnp.concatenate([load(NN - 1 - n, r) for r in range(4)], axis=0) * sign[...]
        sums.append(near + far)
        diffs.append(near - far)
    for part, pieces in ((0, sums), (1, diffs)):
        high, low = split(jnp.concatenate(pieces, axis=1))
        both = dot(jnp.concatenate([high, low], axis=0), fwd_h[part])
        value = both[: 4 * NW] + both[4 * NW :] + dot(high, fwd_l[part])
        grid[:, part * 512 : (part + 1) * 512] = value

    packs = []
    for kk in range(2):
        pack = jnp.zeros((NW, 128), F32)
        for n in range(NN):
            turned = load(n, 4)
            shift_by = (16 * n + 64 * kk) % 128
            if shift_by:
                turned = pltpu.roll(turned, shift_by, 1)
            pack = jnp.where(lane // 16 == n, turned, pack)
        packs.append(pack)
    pairs = [(kk, m) for kk in range(2) for m in range(INNER)]
    masked = []
    for kk, m in pairs:
        high = packs[kk].astype(BF16).astype(F32)
        slots = jnp.zeros((NW, 128), F32)
        for slot, value in enumerate((high, packs[kk] - high, high)):
            turned = pltpu.roll(value, (slot - m) % 128, 1) if slot != m else value
            slots = jnp.where(lane % 8 == slot, turned, slots)
        masked.append(slots.astype(BF16))
    masked = jnp.concatenate(masked, axis=0)
    count = len(pairs) * NW

    mode_id = iota((8, NX), 0)
    mu_col = jnp.zeros((8, NX), F32)
    for m in range(8):
        mu_col = jnp.where(mode_id == m, float(mu[min(m, INNER - 1)]), mu_col)
    dens = [1.0 / (mu_col + (lam_wide[kk] + lamx_row[...])) for kk in range(2)]

    for part in range(4):
        cols = slice(part * 256, (part + 1) * 256)
        value = dot(masked, into[:, cols])
        for kk in range(2):
            p_odd = p_even = None
            for m in range(INNER):
                at = (kk * INNER + m) * NW
                piece = value[at : at + NW] * dens[kk][m : m + 1, cols]
                corr[at : at + NW, cols] = piece
                piece = float(S[m, 0]) * piece
                if m % 2 == 0:
                    p_odd = piece if p_odd is None else p_odd + piece
                else:
                    p_even = piece if p_even is None else p_even + piece
            top = slice(kk * NW, (kk + 1) * NW)
            bot = slice((2 + kk) * NW, (3 + kk) * NW)
            grid[top, cols] = grid[top, cols] + p_odd + p_even
            grid[bot, cols] = grid[bot, cols] + p_odd - p_even

    bots[0:16, :] = jnp.zeros((16, 128), F32)
    for kk in range(2):
        for jb in range(8):
            cols = slice(jb * 128, (jb + 1) * 128)
            tops[pl.ds(kk * 8 + jb, NW, stride=16), :] = grid[kk * NW : (kk + 1) * NW, cols]
            bots[pl.ds(16 + kk * 8 + jb, NW, stride=16), :] = grid[
                (2 + kk) * NW : (3 + kk) * NW, cols
            ]

    row16 = iota((16, 128), 0)
    diag = 2.0 + jnp.where(row16 < 8, lam_k[0], lam_k[1]) + lamx_tile[...]
    older, newer = jnp.ones((16, 128), F32), diag
    for _ in range(INNER - 2):
        older, newer = newer, diag * newer - older
    last = diag * newer - older
    near_one = newer / last
    far_one = 1.0 / last
    full = diag - 2.0 * near_one
    inverse = 1.0 / (diag - near_one)
    value = tops[0:16, :]
    piv[0:16, :] = inverse
    sol[0:16, :] = value
    for w in range(1, NW):
        at = slice(w * 16, (w + 1) * 16)
        ratio = far_one * inverse
        value = tops[at, :] + bots[at, :] + ratio * value
        inverse = 1.0 / (full - far_one * ratio)
        piv[at, :] = inverse
        sol[at, :] = value
    later = jnp.zeros((16, 128), F32)
    sol[NW * 16 : (NW + 1) * 16, :] = later
    for w in range(NW - 1, -1, -1):
        at = slice(w * 16, (w + 1) * 16)
        later = (sol[at, :] + far_one * later) * piv[at, :]
        sol[at, :] = later

    for kk in range(2):
        for jb in range(8):
            cols = slice(jb * 128, (jb + 1) * 128)
            grid[kk * NW : (kk + 1) * NW, cols] = sol[pl.ds(kk * 8 + jb, NW, stride=16), :]
            grid[(2 + kk) * NW : (3 + kk) * NW, cols] = sol[
                pl.ds(16 + kk * 8 + jb, NW, stride=16), :
            ]

    flux = jnp.zeros((2 * count, 128), F32)
    for part in range(4):
        cols = slice(part * 256, (part + 1) * 256)
        pieces = []
        for kk in range(2):
            low_s = grid[kk * NW : (kk + 1) * NW, cols]
            high_s = grid[(2 + kk) * NW : (3 + kk) * NW, cols]
            plus, minus = low_s + high_s, low_s - high_s
            for m in range(INNER):
                at = (kk * INNER + m) * NW
                drive = (plus if m % 2 == 0 else minus) * float(S[m, 0])
                pieces.append(corr[at : at + NW, cols] + dens[kk][m : m + 1, cols] * drive)
        high, low = split(jnp.concatenate(pieces, axis=0))
        flux = flux + dot(jnp.concatenate([high, low], axis=0), outof[cols, :])
    fluxes = []
    side = (lane // 8) % 2
    for kk in range(2):
        total = jnp.zeros((NW, 128), F32)
        for m in range(INNER):
            at = (kk * INNER + m) * NW
            both, main = flux[at : at + NW], flux[count + at : count + at + NW]
            main = both + main
            main = pltpu.roll(main, m, 1) if m > 0 else main
            rest = pltpu.roll(both, (m - 1) % 128, 1) if m != 1 else both
            total = jnp.where(lane % 8 == m, main + rest, total)
        pack = packs[kk]
        to_right = jnp.where(lane < 120, pack - pltpu.roll(pack, 120, 1), 0.0)
        to_left = jnp.where(lane >= 16, pltpu.roll(pack, 8, 1) - pack, 0.0)
        fluxes.append(total + jnp.where(side == 1, to_right, to_left))

    locals_ = []
    for part in range(2):
        high, low = split(grid[: 2 * NW, part * 512 : (part + 1) * 512])
        both = dot(jnp.concatenate([high, low], axis=0), inv_h[part])
        locals_.append(both[: 2 * NW] + both[2 * NW :] + dot(high, inv_l[part]))
    shift[2 * NW :, :] = jnp.zeros((8, 128), F32)
    for n in range(NN):
        block = n if n < NN // 2 else NN - 1 - n
        cols = slice(block * 128, (block + 1) * 128)
        if n < NN // 2:
            value = locals_[0][:, cols] + locals_[1][:, cols]
        else:
            value = (locals_[0][:, cols] - locals_[1][:, cols]) * sign[...]
        shift[: 2 * NW, :] = value
        for kk in range(2):
            pay[pl.ds(n * ROWS + kk, NW, stride=skip), :] = value[kk * NW : (kk + 1) * NW]
            after = shift[kk * NW + 1 : (kk + 1) * NW + 1, :]
            after = jnp.where(iota((NW, 128), 0) == NW - 1, 0.0, after)
            pay[pl.ds(n * ROWS + 2 + kk, NW, stride=skip), :] = after
        first = fluxes[0] if n == 0 else pltpu.roll(fluxes[0], 128 - 16 * n, 1)
        back = (64 - 16 * n) % 128
        second = fluxes[1] if back == 0 else pltpu.roll(fluxes[1], back, 1)
        pay[pl.ds(n * ROWS + 4, NW, stride=skip), :] = jnp.where(lane < 64, first, second)


def backward_kernel(S, recv, keep, den, push, cl3, cyt3, out, zh, zl, stage, room, sems):
    for kk in range(2):
        rows = slice(kk * HALF, (kk + 1) * HALF)
        stage[0, rows, :] = recv[pl.ds(kk, DEST, stride=ROWS), :]
        stage[1, rows, :] = recv[pl.ds(2 + kk, DEST, stride=ROWS), :]
        stage[2, rows, :] = recv[pl.ds(4, DEST, stride=ROWS), :]
    step = 128
    lane = iota((step, 128), 1)

    def slab(c, carry):
        rows = pl.ds(pl.multiple_of(c * step, step), step)
        low_s, high_s, flux = stage[0, rows, :], stage[1, rows, :], stage[2, rows, :]
        kk = jnp.where(c * step >= HALF, 1, 0)
        flux = jnp.where((lane // 64 == kk) & (lane % 64 < 16), flux, 0.0)
        high = flux.astype(BF16).astype(F32)
        flux = high + pltpu.roll(flux - high, 16, 1) + pltpu.roll(high, 32, 1)
        masked = jnp.concatenate([jnp.where(lane % 8 == m, flux, 0.0) for m in range(INNER)], axis=0)
        pushed = dot(masked.astype(BF16), push[...])
        plus, minus = low_s + high_s, low_s - high_s
        modes = []
        for m in range(INNER):
            drive = (plus if m % 2 == 0 else minus) * float(S[m, 0])
            value = keep[m, rows, :] + pushed[m * step : (m + 1) * step] + drive
            modes.append(value * den[m, rows, :])
        planes = [None] * SLAB
        planes[0] = low_s
        for i in range(1, 5):
            p_odd = sum(float(S[m, i - 1]) * modes[m] for m in range(0, INNER, 2))
            if i == 4:
                planes[4] = p_odd
                continue
            p_even = sum(float(S[m, i - 1]) * modes[m] for m in range(1, INNER, 2))
            planes[i] = p_odd + p_even
            planes[SLAB - i] = p_odd - p_even
        for z in range(SLAB):
            zh[z, rows, :], zl[z, rows, :] = split(planes[z])
        return carry

    lax.fori_loop(0, NY // step, slab, 0, unroll=UNROLL_B)

    copies = []
    for p in range(SLAB // 2):
        high = jnp.concatenate([zh[2 * p], zh[2 * p + 1]], axis=1)
        low = jnp.concatenate([zl[2 * p], zl[2 * p + 1]], axis=1)
        high, low = split(dot(jnp.concatenate([high, low, high], axis=1), cl3[...]))
        both = dot(cyt3[...], high)
        value = both[:NY] + both[NY:] + dot(cyt3[:NY, :], low)
        room[2 * p] = value[:, :XL]
        room[2 * p + 1] = value[:, XL:]
        pair = pl.ds(2 * p, 2)
        copies.append(pltpu.make_async_copy(room.at[pair], out.at[pair], sems.at[p]))
        copies[-1].start()
    for copy in copies:
        copy.wait()


def in_vmem(count):
    return [pl.BlockSpec(memory_space=pltpu.VMEM)] * count


def params(mebibytes):
    return pltpu.CompilerParams(vmem_limit_bytes=mebibytes * 1024 * 1024)


def work(microseconds):
    flops = microseconds * 1_000_000_000
    return pl.CostEstimate(flops=flops, bytes_accessed=1_000_000, transcendentals=0)


def per_device(divergence, marker_force, marker_height, marker_cell):
    t = tables()
    tab = {k: jnp.asarray(v) for k, v in t.items() if k not in ("S", "mu")}
    hbm = pl.BlockSpec(memory_space=pltpu.HBM)
    groups = NY // GROUP
    token = pl.pallas_call(
        first_kernel,
        out_shape=jax.ShapeDtypeStruct((8, 128), F32),
        out_specs=in_vmem(1)[0],
        compiler_params=params(1),
        cost_estimate=work(2),
    )()
    own, send = pl.pallas_call(
        marker_kernel,
        out_shape=(
            jax.ShapeDtypeStruct((3, groups, MARKS * GROUP), F32),
            jax.ShapeDtypeStruct((2, groups, MARKS * GROUP), F32),
        ),
        in_specs=in_vmem(4),
        out_specs=tuple(in_vmem(2)),
        compiler_params=params(4),
        cost_estimate=work(4),
    )(token, marker_force, marker_height, marker_cell)
    from_above = lax.ppermute(send, "wide", [(i + 1, i) for i in range(NW - 1)])

    plane = (NY, XL)
    zh, zl, z7 = pl.pallas_call(
        source_kernel,
        out_shape=(
            jax.ShapeDtypeStruct((SLAB, NY, XL), BF16),
            jax.ShapeDtypeStruct((SLAB, NY, XL), BF16),
            jax.ShapeDtypeStruct(plane, F32),
        ),
        in_specs=in_vmem(3),
        out_specs=tuple(in_vmem(3)),
        scratch_shapes=[pltpu.VMEM((SLAB + 1, NY, XL), F32)],
        compiler_params=params(16),
        cost_estimate=work(4),
    )(divergence, own, tab["clt3"])

    field = jax.ShapeDtypeStruct((INNER, NY, XL), F32)
    payload = jax.ShapeDtypeStruct((DEST * ROWS, XL), F32)
    sent, keep = pl.pallas_call(
        functools.partial(forward_kernel, t["S"]),
        out_shape=(payload, field),
        in_specs=in_vmem(8),
        out_specs=tuple(in_vmem(2)),
        scratch_shapes=[
            pltpu.VMEM((SLAB + 1, NY, XL), F32),
            pltpu.VMEM(plane, F32),
            pltpu.VMEM((NY, INNER * XL), BF16),
            pltpu.VMEM((NY, INNER * XL), BF16),
            pltpu.VMEM(plane, F32),
        ],
        compiler_params=params(24),
        cost_estimate=work(5),
    )(zh, zl, z7, from_above, *[tab[k] for k in ("clt1", "cy3", "den", "ends")])

    def exchange(value):
        flat = lax.all_to_all(value.reshape(-1), BOTH, 0, 0, tiled=True)
        return flat.reshape(DEST * ROWS, XL)

    names = (
        "fwd_h", "fwd_l", "inv_h", "inv_l", "into", "outof",
        "lamx_row", "lamx_tile", "sign",
    )
    returned = pl.pallas_call(
        functools.partial(middle_kernel, t["S"], t["mu"]),
        out_shape=payload,
        in_specs=in_vmem(2 + len(names)),
        out_specs=in_vmem(1)[0],
        scratch_shapes=[
            pltpu.VMEM((4 * NW, NX), F32),
            pltpu.VMEM((2 * INNER * NW, NX), F32),
            pltpu.VMEM((NW * 16, 128), F32),
            pltpu.VMEM(((NW + 1) * 16, 128), F32),
            pltpu.VMEM((NW * 16, 128), F32),
            pltpu.VMEM(((NW + 1) * 16, 128), F32),
            pltpu.VMEM((2 * NW + 8, 128), F32),
        ],
        compiler_params=params(16),
        cost_estimate=work(5),
    )(tab["lamy"], exchange(sent), *[tab[k] for k in names])

    return pl.pallas_call(
        functools.partial(backward_kernel, t["S"]),
        out_shape=jax.ShapeDtypeStruct((SLAB, NY, XL), F32),
        in_specs=in_vmem(6),
        out_specs=hbm,
        scratch_shapes=[
            pltpu.VMEM((SLAB, NY, XL), BF16),
            pltpu.VMEM((SLAB, NY, XL), BF16),
            pltpu.VMEM((3, NY, XL), F32),
            pltpu.VMEM((SLAB, NY, XL), F32),
            pltpu.SemaphoreType.DMA((SLAB // 2,)),
        ],
        compiler_params=params(24),
        cost_estimate=work(5),
    )(exchange(returned), keep, tab["den"], tab["push"], tab["cl3"], tab["cyt3"])


def solution(mesh):
    in_specs = (
        P("wide", None, "narrow"),
        P("wide", "narrow"),
        P("wide", "narrow"),
        P("wide", "narrow"),
    )
    out_specs = P("wide", None, "narrow")
    return jax.shard_map(
        per_device, mesh=mesh, in_specs=in_specs, out_specs=out_specs, check_vma=False
    )
```
